32 devices in a mesh: frag: 2 (over y), vir: 4 (over z), occ: 2 (over x), rep: 2 (over core).
Axes of the slice: x: 2, y: 2, z: 4, core: 2. Of those that a mesh axis runs over, the one named last changes fastest.
Arguments:
- amplitudes: bfloat16 [16, 4, 1024, 1024], P('frag', 'rep', 'vir'), parts along dimension 0, may hold values from -6 to 6
- integrals: bfloat16 [8, 4, 1024, 1024], P(('frag', 'rep'), 'occ', 'vir'), parts along dimension 0, may hold values from -0.09375 to 0.09375
- amp_mask: int32 [8, 16, 16], P('frag'), parts along dimension 0, may hold values 0 or 1
- int_mask: int32 [8, 4, 16, 16], P('frag'), parts along dimension 0, may hold values 0 or 1
- eps_slab: float32 [16], P('frag'), parts along dimension 0, may hold values from -1.6 to -0.4
- eps_pair: float32 [8], P(('frag', 'occ', 'rep')), parts along dimension 0, may hold values from -1.6 to -0.4
- eps_vir: float32 [2048], P('frag'), parts along dimension 0, may hold values from 0.3 to 3
Outputs:
- update: float32 [16, 1024, 4, 1024], P('frag', 'vir', ('occ', 'rep')), parts along dimension 0
The draws below stay inside these ranges and needn't reach their ends.
There are 2 independent parts, one for each index of `frag`. The reference program is written for one: setup_inputs(seed, part) draws one part's arguments, and reference() takes and returns one part's arrays. A program takes and returns all parts, laid end to end along the dimension named above; each array names one. Nothing has to cross between parts.
All inputs are finite; a program needn't handle non-finite values.
Results may differ from the reference program's by a relative error of at most 0.0022.
Values may be sent and summed in bfloat16 or wider, within the bound.
No kernel may reach another device: no remote copies, remote signals or barrier semaphores. Data moves between devices by JAX's collectives and lax.ppermute only.
A program may use at most 192 MiB of HBM per device.

```python
import math
import jax
import jax.numpy as jnp
from jax import lax

TILE = 64
V = 1024
SLAB = 8
K = 4
J = 4
NVT = 16


def place_ends(array, rng, smallest, largest):
    longest = array.shape.index(max(array.shape))
    spots = []
    for shift in (0, 1):
        where = [jax.random.randint(jax.random.fold_in(rng, axis), (), 0, length) for axis, length in enumerate(array.shape)]
        where[longest] = (where[longest] + shift) % array.shape[longest]
        spots.append(tuple(where))
    return array.at[spots[0]].set(smallest).at[spots[1]].set(largest)


def block_levels(own_key, dims, shards, smallest, high):
    def one(axis_at, parts):
        draws = jax.random.uniform(jax.random.fold_in(jax.random.fold_in(own_key, 6), axis_at), (parts,), jnp.float32, smallest / len(shards), high / len(shards))
        return jnp.repeat(jnp.exp(draws), dims[axis_at] // parts).reshape((-1,) + (1,) * (len(dims) - axis_at - 1))

    factor_of = one(*shards[0])
    for cut in shards[1:]:
        factor_of = factor_of * one(*cut)
    return factor_of


def bell_draw(stream_key, extent, deviation, most, shards=(), kind=jnp.bfloat16):
    entries = deviation * jax.random.normal(stream_key, extent, jnp.float32)
    if shards:
        entries = entries * block_levels(stream_key, extent, shards, -0.22, 0.18)
    return jnp.clip(entries, -most, most).astype(kind)


def setup_inputs(seed: int = 0, part: int = 0) -> dict:
    key_of = jax.random.split(jax.random.key(seed), 8)
    part_splits = jax.random.split(jax.random.fold_in(key_of[7], part), 8)
    return {
        "amplitudes": bell_draw(part_splits[0], (SLAB, K, V, V), 1.0, 6.0, ((1, 2), (2, 4))),
        "integrals": bell_draw(part_splits[1], (K, J, V, V), (K * V) ** -0.5, 0.09375, ((0, 2), (1, 2), (2, 4))),
        "amp_mask": place_ends((jax.random.randint(part_splits[2], (K, NVT, NVT), 0, 2) < 1).astype(jnp.int32), jax.random.fold_in(part_splits[2], 1), 0, 1),
        "int_mask": place_ends((jax.random.randint(part_splits[3], (K, J, NVT, NVT), 0, 2) < 1).astype(jnp.int32), jax.random.fold_in(part_splits[3], 1), 0, 1),
        "eps_slab": jnp.clip(jax.random.uniform(part_splits[4], (SLAB,), jnp.float32, -1.6, -0.4), -1.6, -0.4),
        "eps_pair": jnp.clip(-1.6 + 1.2 * jax.random.uniform(part_splits[5], (J,), jnp.float32) ** block_levels(part_splits[5], (J,), ((0, 4),), -0.2, 0.2), -1.6, -0.4),
        "eps_vir": jnp.clip(jnp.exp(jax.random.uniform(part_splits[6], (V,), jnp.float32, math.log(0.3), math.log(3.0))), 0.3, 3.0),
    }


def spread(mask_tiles):
    return jnp.repeat(jnp.repeat(mask_tiles, TILE, axis=-2), TILE, axis=-1).astype(jnp.float32)


def reference(amplitudes, integrals, amp_mask, int_mask, eps_slab, eps_pair, eps_vir):
    screened = (amplitudes.astype(jnp.float32) * spread(amp_mask)[None]).astype(jnp.bfloat16)
    widened = screened.astype(jnp.float32)
    rounded = lax.optimization_barrier((2.0 * widened - jnp.swapaxes(widened, 2, 3)).astype(jnp.bfloat16))
    combined = rounded.astype(jnp.float32)

    def one_pair(index):
        column = lax.dynamic_index_in_dim(integrals, index, 1, keepdims=False).astype(jnp.float32)
        mask_cols = lax.dynamic_index_in_dim(int_mask, index, 1, keepdims=False)
        kept = column * spread(mask_cols)
        direct_term = jnp.einsum("ikac,kcb->iab", combined, kept, precision=lax.Precision.HIGHEST)
        swapped_term = jnp.einsum("ikac,kbc->iab", combined, kept, precision=lax.Precision.HIGHEST)
        energy = lax.dynamic_index_in_dim(eps_pair, index, 0, keepdims=False)
        denominator = eps_vir[None, :, None] + eps_vir[None, None, :] - eps_slab[:, None, None] - energy
        return (2.0 * direct_term - swapped_term) / denominator

    stacked = lax.map(one_pair, jnp.arange(J, dtype=jnp.int32))
    return jnp.transpose(stacked, (1, 2, 0, 3))
```

```python
import functools

import jax
import jax.numpy as jnp
from jax import lax
from jax.experimental import pallas as pl
from jax.experimental.pallas import tpu as pltpu
from jax.sharding import PartitionSpec as P

TILE = 64
LANES = 128
AMP_SLOTS = 46
INT_SLOTS = 160
VMEM_LIMIT = 60 * 1024 * 1024


def tile_mask(mask_tiles, row_start, row_count, tile_size):
    tile_count = mask_tiles.shape[-1]
    row_tiles = (row_start + jnp.arange(row_count, dtype=jnp.int32)) // tile_size
    select = (row_tiles[:, None] == jnp.arange(tile_count, dtype=jnp.int32)[None, :]).astype(
        jnp.float32
    )
    picked = jnp.einsum("ra,...ac->...rc", select, mask_tiles.astype(jnp.float32))
    return jnp.repeat(picked, tile_size, axis=-1)


def cycle_terms(combined, gathered):
    direct_term = jnp.einsum(
        "ikac,kjcb->iajb", combined, gathered, preferred_element_type=jnp.float32
    )
    swapped_term = jnp.einsum(
        "ikac,kjbc->iajb", combined, gathered, preferred_element_type=jnp.float32
    )
    return 2.0 * direct_term - swapped_term


def dense_shards(amplitudes, integrals, amp_mask, int_mask, eps_slab, eps_pair, eps_vir):
    row_count = amplitudes.shape[2]
    half_count = amplitudes.shape[1]
    pair_count = integrals.shape[1]
    row_start = lax.axis_index("vir") * row_count
    k_start = lax.axis_index("rep") * half_count
    j_start = lax.axis_index("occ") * pair_count
    zero_index = jnp.zeros((), jnp.int32)
    k_masks = lax.dynamic_slice_in_dim(amp_mask, k_start, half_count, 0)
    screened = (
        amplitudes.astype(jnp.float32) * tile_mask(k_masks, row_start, row_count, TILE)[None]
    ).astype(jnp.bfloat16)
    received = lax.all_to_all(screened, "vir", split_axis=3, concat_axis=2, tiled=True)
    combined = (
        2.0 * screened.astype(jnp.float32) - jnp.swapaxes(received, 2, 3).astype(jnp.float32)
    ).astype(jnp.bfloat16)
    pair_masks = lax.dynamic_slice(
        int_mask,
        (k_start, j_start, zero_index, zero_index),
        (half_count, pair_count, int_mask.shape[2], int_mask.shape[3]),
    )
    kept_local = (
        integrals.astype(jnp.float32) * tile_mask(pair_masks, row_start, row_count, TILE)
    ).astype(jnp.bfloat16)
    gathered = lax.all_gather(kept_local, "vir", axis=2, tiled=True)
    partial_cycle = cycle_terms(combined, gathered)
    cycle = lax.psum_scatter(partial_cycle, "rep", scatter_dimension=2, tiled=True)
    row_energy = lax.dynamic_slice_in_dim(eps_vir, row_start, row_count, 0)
    denominator = (
        row_energy[None, :, None, None]
        + eps_vir[None, None, None, :]
        - eps_slab[:, None, None, None]
        - eps_pair[None, None, :, None]
    )
    return cycle / denominator


def low_lanes(rows):
    return lax.broadcasted_iota(jnp.int32, (rows, LANES), 1) < TILE


def swap_halves(block):
    return pltpu.roll(block, TILE, 1)


def pack_int_kernel(meta, mask, own_ref, oth_ref, out_ref):
    v, r, j = meta[0], meta[2], meta[3]
    low = low_lanes(32)
    count = jnp.int32(0)
    for kk in range(4):
        k = lax.rem(kk + 2 * r, 4)

        def body(n, count, kk=kk, k=k):
            ap, cp = n // 8, n % 8
            col = pl.multiple_of(cp * LANES, LANES)
            for a2 in range(2):
                row = pl.multiple_of(ap * 128 + a2 * TILE, TILE)
                if kk < 2:
                    block = own_ref[kk, r, pl.ds(row, TILE), pl.ds(col, LANES)]
                else:
                    block = oth_ref[kk - 2, pl.ds(row, TILE), pl.ds(col, LANES)]
                top, bottom = block[:32], block[32:]
                turned_top, turned_bottom = swap_halves(top), swap_halves(bottom)
                at_row = 4 * v + 2 * ap + a2
                out_ref[jnp.minimum(count, INT_SLOTS - 1)] = jnp.where(low, top, turned_bottom)
                count = count + mask[k, j, at_row, 2 * cp]
                out_ref[jnp.minimum(count, INT_SLOTS - 1)] = jnp.where(low, turned_top, bottom)
                count = count + mask[k, j, at_row, 2 * cp + 1]
            return count

        count = lax.fori_loop(0, 16, body, count)


def pack_amp_kernel(meta, mask, own_ref, oth_ref, out_ref):
    v, r = meta[0], meta[2]
    low = low_lanes(TILE)
    for d in range(1, 4):
        dest = lax.rem(v + d, 4)
        count = jnp.int32(0)
        for kk in range(4):
            k = lax.rem(kk + 2 * r, 4)
            ref = own_ref if kk < 2 else oth_ref

            def body(n, count, d=d, kk=kk, k=k, ref=ref, dest=dest):
                ap, cp = n // 2, n % 2
                col = pl.multiple_of(dest * 256 + cp * LANES, LANES)
                tiles = []
                for a2 in range(2):
                    row = pl.multiple_of(ap * 128 + a2 * TILE, TILE)
                    x0 = ref[0, 0, 0, kk % 2, pl.ds(row, TILE), pl.ds(col, LANES)]
                    x1 = ref[0, 0, 1, kk % 2, pl.ds(row, TILE), pl.ds(col, LANES)]
                    tiles.append(
                        (jnp.where(low, x0, swap_halves(x1)), jnp.where(low, swap_halves(x0), x1))
                    )
                for c2 in range(2):
                    for a2 in range(2):
                        out_ref[d - 1, jnp.minimum(count, AMP_SLOTS - 1)] = tiles[a2][c2]
                        count = count + mask[k, 4 * v + 2 * ap + a2, 4 * dest + 2 * cp + c2]
                return count

            count = lax.fori_loop(0, 4, body, count)


def unpack_int_kernel(d, meta, mask, buf_ref, d_ref, t_ref, count_ref):
    v, r, j = meta[0], meta[2], meta[3]
    kk = pl.program_id(0)
    k = lax.rem(kk + 2 * r, 4)
    s = lax.rem(v + 4 - d, 4)
    low = low_lanes(32)
    zero = jnp.zeros((32, LANES), jnp.bfloat16)

    @pl.when(kk == 0)
    def _():
        count_ref[0] = 0

    def body(n, count):
        ap, cp = n // 8, n % 8
        parts = []
        for a2 in range(2):
            at_row = 4 * s + 2 * ap + a2
            m0, m1 = mask[k, j, at_row, 2 * cp], mask[k, j, at_row, 2 * cp + 1]
            y0 = buf_ref[jnp.minimum(count, INT_SLOTS - 1)]
            count = count + m0
            y1 = buf_ref[jnp.minimum(count, INT_SLOTS - 1)]
            count = count + m1
            y0 = jnp.where(m0 > 0, y0, zero)
            y1 = jnp.where(m1 > 0, y1, zero)
            parts.append(jnp.where(low, y0, swap_halves(y1)))
            parts.append(jnp.where(low, swap_halves(y0), y1))
        block = jnp.concatenate(parts, axis=0)
        row = pl.multiple_of(ap * 128, 128)
        col = pl.multiple_of(cp * LANES, LANES)
        d_ref[0, pl.ds(row, 128), pl.ds(col, LANES)] = block
        t_ref[0, pl.ds(col, LANES), pl.ds(row, 128)] = block.T
        return count

    count_ref[0] = lax.fori_loop(0, 16, body, count_ref[0])


def own_int_kernel(meta, mask, own_ref, oth_ref, d_ref, t_ref):
    v, r, j = meta[0], meta[2], meta[3]
    kk = pl.program_id(0)
    k = lax.rem(kk + 2 * r, 4)
    low = low_lanes(TILE)
    zero = jnp.zeros((TILE, LANES), jnp.bfloat16)

    def body(n, carry):
        ap, cp = n // 8, n % 8
        col = pl.multiple_of(cp * LANES, LANES)
        parts = []
        for a2 in range(2):
            at_row = 4 * v + 2 * ap + a2
            row = pl.multiple_of(ap * 128 + a2 * TILE, TILE)
            m0, m1 = mask[k, j, at_row, 2 * cp], mask[k, j, at_row, 2 * cp + 1]
            block = jnp.where(
                kk < 2,
                own_ref[0, 0, pl.ds(row, TILE), pl.ds(col, LANES)],
                oth_ref[0, pl.ds(row, TILE), pl.ds(col, LANES)],
            )
            parts.append(
                jnp.where(low, jnp.where(m0 > 0, block, zero), jnp.where(m1 > 0, block, zero))
            )
        block = jnp.concatenate(parts, axis=0)
        row = pl.multiple_of(ap * 128, 128)
        d_ref[0, pl.ds(row, 128), pl.ds(col, LANES)] = block
        t_ref[0, pl.ds(col, LANES), pl.ds(row, 128)] = block.T
        return carry

    lax.fori_loop(0, 16, body, 0)


def lane_scale(m0, m1, value):
    lane = lax.broadcasted_iota(jnp.int32, (1, LANES), 1)
    return value * jnp.where(lane < TILE, m0, m1).astype(jnp.float32)


def combine_kernel(d, meta, mask, own_ref, oth_ref, near_ref, far_ref, out_ref, count_ref):
    v, x, r = meta[0], meta[1], meta[2]
    kk = pl.program_id(0)
    k = lax.rem(kk + 2 * r, 4)
    s = lax.rem(v + 4 - d, 4)
    zero = jnp.zeros((TILE, LANES), jnp.bfloat16)

    @pl.when(kk == 0)
    def _():
        count_ref[0] = 0

    def body(n, count):
        ap, c = n // 4, n % 4
        arow = pl.multiple_of(c * TILE, TILE)
        ccol = pl.multiple_of(ap * 128, 128)
        slots, kept = [], []
        for a2 in range(2):
            m = mask[k, 4 * s + 2 * ap + a2, 4 * v + c]
            slots.append(jnp.minimum(count, AMP_SLOTS - 1))
            kept.append(m)
            count = count + m
        own_scale = lane_scale(
            mask[k, 4 * v + c, 4 * s + 2 * ap], mask[k, 4 * v + c, 4 * s + 2 * ap + 1], 2.0
        )
        for xx, buf in ((x, near_ref), (1 - x, far_ref)):
            stacked = jnp.concatenate(
                [jnp.where(kept[a2] > 0, buf[slots[a2]], zero) for a2 in range(2)], axis=0
            )
            turned = stacked.T.astype(jnp.float32)
            for ii in range(2):
                local = jnp.where(
                    kk < 2,
                    own_ref[xx, 0, ii, 0, pl.ds(arow, TILE), pl.ds(ccol, 128)],
                    oth_ref[xx, 0, ii, 0, pl.ds(arow, TILE), pl.ds(ccol, 128)],
                ).astype(jnp.float32)
                value = own_scale * local - turned[ii * TILE : (ii + 1) * TILE]
                out_ref[xx, ii, pl.ds(arow, TILE), pl.ds(ccol, 128)] = value.astype(jnp.bfloat16)
        return count

    count_ref[0] = lax.fori_loop(0, 8, body, count_ref[0])


def diagonal_kernel(meta, mask, own_ref, oth_ref, out_ref):
    v, r = meta[0], meta[2]
    kk = pl.program_id(0)
    k = lax.rem(kk + 2 * r, 4)

    def screened(xx, ii, a0, c0):
        rows = []
        for a2 in range(2):
            start = a0 * 128 + a2 * TILE
            block = jnp.where(
                kk < 2,
                own_ref[xx, 0, ii, 0, start : start + TILE, c0 * 128 : (c0 + 1) * 128],
                oth_ref[xx, 0, ii, 0, start : start + TILE, c0 * 128 : (c0 + 1) * 128],
            ).astype(jnp.float32)
            at_row = 4 * v + 2 * a0 + a2
            rows.append(
                block
                * lane_scale(
                    mask[k, at_row, 4 * v + 2 * c0], mask[k, at_row, 4 * v + 2 * c0 + 1], 1.0
                )
            )
        return jnp.concatenate(rows, axis=0)

    for xx in range(2):
        for ii in range(2):
            for a0 in range(2):
                for c0 in range(2):
                    value = 2.0 * screened(xx, ii, a0, c0) - screened(xx, ii, c0, a0).T
                    out_ref[xx, ii, a0 * 128 : (a0 + 1) * 128, c0 * 128 : (c0 + 1) * 128] = (
                        value.astype(jnp.bfloat16)
                    )


def contract_kernel(
    meta, eps_slab, eps_pair, eps_rows, eps_cols, *refs
):
    ints, own, oth, out_ref, w_ref = refs[:8], refs[8:12], refs[12:16], refs[16], refs[17]
    v, r = meta[0], meta[2]
    g = pl.program_id(0)

    @pl.when(g == 0)
    def _():
        for q in range(4):
            sq = lax.rem(v + 4 - q, 4)
            for p in range(4):
                sp = lax.rem(v + 4 - p, 4)
                col = pl.multiple_of(sp * 256, 256)
                row = pl.multiple_of(sq * 256, 256)

                def body(k, carry, q=q, p=p, col=col, row=row):
                    direct = ints[q][k, :, pl.ds(col, 256)].astype(jnp.float32)
                    swapped = ints[4 + p][k, pl.ds(row, 256), :].astype(jnp.float32)
                    w_ref[q, pl.ds(pl.multiple_of(k * 256, 256), 256), pl.ds(col, 256)] = (
                        2.0 * direct - swapped
                    ).astype(jnp.bfloat16)
                    return carry

                lax.fori_loop(0, 4, body, 0)

    def work(blocks, i):
        total = jnp.dot(blocks[0][0, 0], w_ref[0], preferred_element_type=jnp.float32)
        for q in range(1, 4):
            total += jnp.dot(blocks[q][0, 0], w_ref[q], preferred_element_type=jnp.float32)
        value = total / ((eps_rows[...] + eps_cols[...]) - eps_slab[i] - eps_pair[0])
        for n in range(8):
            out_ref[pl.ds(n, 256, stride=8), :] = value[:, n * 128 : (n + 1) * 128]

    @pl.when(g < 4)
    def _():
        work(own, 4 * (g // 2) + 2 * r + g % 2)

    @pl.when(g >= 4)
    def _():
        work(oth, 4 * ((g - 4) // 2) + 2 * (1 - r) + g % 2)


def smem():
    return pl.BlockSpec(memory_space=pltpu.SMEM)


def whole():
    return pl.BlockSpec(memory_space=pltpu.VMEM)


def params():
    return pltpu.CompilerParams(vmem_limit_bytes=VMEM_LIMIT)


def packed_shards(amplitudes, integrals, amp_mask, int_mask, eps_slab, eps_pair, eps_vir):
    v, x, r = lax.axis_index("vir"), lax.axis_index("occ"), lax.axis_index("rep")
    meta = jnp.stack([v, x, r, 2 * x + r]).astype(jnp.int32)
    swap = [(0, 1), (1, 0)]
    bf16 = jnp.bfloat16

    pairs = amp_mask.reshape(4, 4, 4, 4, 4).sum((0, 2, 4))
    pairs = jnp.where(jnp.eye(4, dtype=bool), 0, pairs)
    pieces = int_mask.reshape(4, 4, 4, 4, 16).sum((0, 3, 4))
    over = jnp.logical_or(jnp.max(pairs) > AMP_SLOTS - 1, jnp.max(pieces) > INT_SLOTS - 1)
    over = over.astype(jnp.int32).reshape(1)
    over = over + lax.ppermute(over, "frag", swap)

    int_oth = lax.ppermute(
        lax.dynamic_index_in_dim(integrals, 1 - r, 1, keepdims=False), "rep", swap
    )
    amps = amplitudes.reshape(2, 2, 2, 2, 256, 1024)
    amp_oth = lax.ppermute(lax.dynamic_slice_in_dim(amps, 1 - r, 1, 1), "rep", swap)

    packed_int = pl.pallas_call(
        pack_int_kernel,
        out_shape=jax.ShapeDtypeStruct((INT_SLOTS, 32, LANES), bf16),
        in_specs=[smem(), smem(), whole(), whole()],
        out_specs=whole(),
        compiler_params=params(),
        name="pack_int",
    )(meta, int_mask, integrals, int_oth)

    packed_amp = pl.pallas_call(
        pack_amp_kernel,
        grid_spec=pltpu.PrefetchScalarGridSpec(
            num_scalar_prefetch=2,
            grid=(1,),
            in_specs=[
                pl.BlockSpec((1, 1, 2, 2, 256, 1024), lambda g, meta, mask: (meta[1], meta[2], 0, 0, 0, 0)),
                pl.BlockSpec((1, 1, 2, 2, 256, 1024), lambda g, meta, mask: (meta[1], 0, 0, 0, 0, 0)),
            ],
            out_specs=pl.BlockSpec((3, AMP_SLOTS, TILE, LANES), lambda g, meta, mask: (0, 0, 0, 0)),
        ),
        out_shape=jax.ShapeDtypeStruct((3, AMP_SLOTS, TILE, LANES), bf16),
        compiler_params=params(),
        name="pack_amp",
    )(meta, amp_mask, amps, amp_oth)

    near = [
        lax.ppermute(packed_amp[d - 1], "vir", [(s, (s + d) % 4) for s in range(4)])
        for d in (1, 2, 3)
    ]
    far = [lax.ppermute(a, "occ", swap) for a in near]

    up1 = lax.ppermute(packed_int, "vir", [(0, 1), (1, 2), (2, 3)])
    down1 = lax.ppermute(packed_int, "vir", [(1, 0), (2, 1), (3, 2)])
    up2 = lax.ppermute(up1, "vir", [(1, 2), (2, 3)])
    down2 = lax.ppermute(down1, "vir", [(1, 0), (2, 1)])
    second = jnp.where(v < 2, down2, up2)
    third = lax.ppermute(second, "vir", [(1, 0), (2, 3)])
    arrived = {1: jnp.where(v == 0, third, up1), 2: second, 3: jnp.where(v == 3, third, down1)}

    def k_place(kk, r):
        return lax.rem(kk + 2 * r, 4)

    int_shapes = [
        jax.ShapeDtypeStruct((4, 256, 1024), bf16),
        jax.ShapeDtypeStruct((4, 1024, 256), bf16),
    ]
    int_outs = [
        pl.BlockSpec((1, 256, 1024), lambda kk, meta, mask: (k_place(kk, meta[2]), 0, 0)),
        pl.BlockSpec((1, 1024, 256), lambda kk, meta, mask: (k_place(kk, meta[2]), 0, 0)),
    ]
    rows, cols = [], []
    for d in range(4):
        if d == 0:
            kernel, scratch = own_int_kernel, []
            specs = [
                pl.BlockSpec((1, 1, 256, 1024), lambda kk, meta, mask: (jnp.minimum(kk, 1), meta[2], 0, 0)),
                pl.BlockSpec((1, 256, 1024), lambda kk, meta, mask: (jnp.maximum(kk - 2, 0), 0, 0)),
            ]
            operands = (integrals, int_oth)
        else:
            kernel, scratch = functools.partial(unpack_int_kernel, d), [pltpu.SMEM((1,), jnp.int32)]
            specs = [pl.BlockSpec((INT_SLOTS, 32, LANES), lambda kk, meta, mask: (0, 0, 0))]
            operands = (arrived[d],)
        direct, swapped = pl.pallas_call(
            kernel,
            grid_spec=pltpu.PrefetchScalarGridSpec(
                num_scalar_prefetch=2, grid=(4,), in_specs=specs, out_specs=int_outs, scratch_shapes=scratch
            ),
            out_shape=int_shapes,
            compiler_params=params(),
            name=f"ints_{d}",
        )(meta, int_mask, *operands)
        rows.append(direct)
        cols.append(swapped)

    combined = []
    for d in range(4):
        local_specs = [
            pl.BlockSpec(
                (2, 1, 2, 1, 256, 256),
                lambda kk, meta, mask, d=d: (0, meta[2], 0, jnp.minimum(kk, 1), 0, lax.rem(meta[0] + 4 - d, 4)),
            ),
            pl.BlockSpec(
                (2, 1, 2, 1, 256, 256),
                lambda kk, meta, mask, d=d: (0, 0, 0, jnp.maximum(kk - 2, 0), 0, lax.rem(meta[0] + 4 - d, 4)),
            ),
        ]
        if d == 0:
            kernel, scratch, specs, operands = diagonal_kernel, [], [], ()
        else:
            kernel, scratch = functools.partial(combine_kernel, d), [pltpu.SMEM((1,), jnp.int32)]
            specs = [pl.BlockSpec((AMP_SLOTS, TILE, LANES), lambda kk, meta, mask: (0, 0, 0))] * 2
            operands = (near[d - 1], far[d - 1])
        combined.append(
            pl.pallas_call(
                kernel,
                grid_spec=pltpu.PrefetchScalarGridSpec(
                    num_scalar_prefetch=2,
                    grid=(4,),
                    in_specs=local_specs + specs,
                    out_specs=pl.BlockSpec(
                        (2, 2, 256, 256), lambda kk, meta, mask: (0, 0, 0, k_place(kk, meta[2]))
                    ),
                    scratch_shapes=scratch,
                ),
                out_shape=jax.ShapeDtypeStruct((2, 2, 256, 1024), bf16),
                compiler_params=params(),
                name=f"combine_{d}",
            )(meta, amp_mask, amps, amp_oth, *operands)
        )
    combined_oth = [lax.ppermute(c, "rep", swap) for c in combined]

    row_energy = lax.dynamic_slice_in_dim(eps_vir, v * 256, 256, 0).reshape(256, 1)
    col_energy = eps_vir.reshape(1, 1024)

    def contract(ops):
        rows, cols, own, oth = ops
        resident = [
            pl.BlockSpec((4, 256, 1024), lambda g, *_: (0, 0, 0), pipeline_mode=pl.Buffered(1))
        ] * 4 + [
            pl.BlockSpec((4, 1024, 256), lambda g, *_: (0, 0, 0), pipeline_mode=pl.Buffered(1))
        ] * 4

        def own_at(g, *_):
            g = jnp.minimum(g, 3)
            return (g // 2, g % 2, 0, 0)

        def oth_at(g, *_):
            g = jnp.maximum(g - 4, 0)
            return (g // 2, g % 2, 0, 0)

        def out_at(g, meta, *_):
            r = jnp.where(g < 4, meta[2], 1 - meta[2])
            return (4 * ((g % 4) // 2) + 2 * r + g % 2, 0)

        out = pl.pallas_call(
            contract_kernel,
            grid_spec=pltpu.PrefetchScalarGridSpec(
                num_scalar_prefetch=3,
                grid=(8,),
                in_specs=[
                    pl.BlockSpec((256, 1), lambda g, *_: (0, 0)),
                    pl.BlockSpec((1, 1024), lambda g, *_: (0, 0)),
                ]
                + resident
                + [pl.BlockSpec((1, 1, 256, 1024), own_at)] * 4
                + [pl.BlockSpec((1, 1, 256, 1024), oth_at)] * 4,
                out_specs=pl.BlockSpec((2048, 128), out_at),
                scratch_shapes=[pltpu.VMEM((4, 1024, 1024), bf16)],
            ),
            out_shape=jax.ShapeDtypeStruct((8 * 2048, 128), jnp.float32),
            compiler_params=params(),
            name="contract",
        )(meta, eps_slab, eps_pair, row_energy, col_energy, *rows, *cols, *own, *oth)
        return out.reshape(8, 256, 1, 1024)

    def dense(ops):
        return dense_shards(amplitudes, integrals, amp_mask, int_mask, eps_slab, eps_pair, eps_vir)

    return lax.cond(over[0] > 0, dense, contract, (rows, cols, combined, combined_oth))


def shards(sizes, *args):
    amplitudes, integrals, amp_mask, int_mask = args[:4]
    fits = (
        sizes == {"frag": 2, "vir": 4, "occ": 2, "rep": 2}
        and amplitudes.shape == (8, 2, 256, 1024)
        and integrals.shape == (2, 2, 256, 1024)
        and amp_mask.shape == (4, 16, 16)
        and int_mask.shape == (4, 4, 16, 16)
    )
    return packed_shards(*args) if fits else dense_shards(*args)


def solution(mesh):
    in_specs = (
        P("frag", "rep", "vir", None),
        P(("frag", "rep"), "occ", "vir", None),
        P("frag", None, None),
        P("frag", None, None, None),
        P("frag"),
        P(("frag", "occ", "rep")),
        P("frag"),
    )
    out_specs = P("frag", "vir", ("occ", "rep"), None)
    return jax.shard_map(
        functools.partial(shards, dict(mesh.shape)),
        mesh=mesh,
        in_specs=in_specs,
        out_specs=out_specs,
        check_vma=False,
    )
```

```python
import functools

import jax
import jax.numpy as jnp
from jax import lax
from jax.experimental import pallas as pl
from jax.experimental.pallas import tpu as pltpu
from jax.sharding import PartitionSpec as P

TILE = 64
LANES = 128
AMP_SLOTS = 46
INT_SLOTS = 160
VMEM_LIMIT = 60 * 1024 * 1024
NO_COST = pl.CostEstimate(flops=1024, bytes_accessed=1024, transcendentals=0)


def tile_mask(mask_tiles, row_start, row_count, tile_size):
    tile_count = mask_tiles.shape[-1]
    row_tiles = (row_start + jnp.arange(row_count, dtype=jnp.int32)) // tile_size
    select = (row_tiles[:, None] == jnp.arange(tile_count, dtype=jnp.int32)[None, :]).astype(
        jnp.float32
    )
    picked = jnp.einsum("ra,...ac->...rc", select, mask_tiles.astype(jnp.float32))
    return jnp.repeat(picked, tile_size, axis=-1)


def cycle_terms(combined, gathered):
    direct_term = jnp.einsum(
        "ikac,kjcb->iajb", combined, gathered, preferred_element_type=jnp.float32
    )
    swapped_term = jnp.einsum(
        "ikac,kjbc->iajb", combined, gathered, preferred_element_type=jnp.float32
    )
    return 2.0 * direct_term - swapped_term


def dense_shards(amplitudes, integrals, amp_mask, int_mask, eps_slab, eps_pair, eps_vir):
    row_count = amplitudes.shape[2]
    half_count = amplitudes.shape[1]
    pair_count = integrals.shape[1]
    row_start = lax.axis_index("vir") * row_count
    k_start = lax.axis_index("rep") * half_count
    j_start = lax.axis_index("occ") * pair_count
    zero_index = jnp.zeros((), jnp.int32)
    k_masks = lax.dynamic_slice_in_dim(amp_mask, k_start, half_count, 0)
    screened = (
        amplitudes.astype(jnp.float32) * tile_mask(k_masks, row_start, row_count, TILE)[None]
    ).astype(jnp.bfloat16)
    received = lax.all_to_all(screened, "vir", split_axis=3, concat_axis=2, tiled=True)
    combined = (
        2.0 * screened.astype(jnp.float32) - jnp.swapaxes(received, 2, 3).astype(jnp.float32)
    ).astype(jnp.bfloat16)
    pair_masks = lax.dynamic_slice(
        int_mask,
        (k_start, j_start, zero_index, zero_index),
        (half_count, pair_count, int_mask.shape[2], int_mask.shape[3]),
    )
    kept_local = (
        integrals.astype(jnp.float32) * tile_mask(pair_masks, row_start, row_count, TILE)
    ).astype(jnp.bfloat16)
    gathered = lax.all_gather(kept_local, "vir", axis=2, tiled=True)
    partial_cycle = cycle_terms(combined, gathered)
    cycle = lax.psum_scatter(partial_cycle, "rep", scatter_dimension=2, tiled=True)
    row_energy = lax.dynamic_slice_in_dim(eps_vir, row_start, row_count, 0)
    denominator = (
        row_energy[None, :, None, None]
        + eps_vir[None, None, None, :]
        - eps_slab[:, None, None, None]
        - eps_pair[None, None, :, None]
    )
    return cycle / denominator


def low_lanes(rows):
    return lax.broadcasted_iota(jnp.int32, (rows, LANES), 1) < TILE


def swap_halves(block):
    return pltpu.roll(block, TILE, 1)


def fill(buf, choices):
    for chosen, ref in choices:

        @pl.when(chosen)
        def _(ref=ref):
            pltpu.sync_copy(ref, buf)


def pack_int_kernel(meta, mask, own_ref, oth_ref, out_ref):
    v, r, j = meta[0], meta[2], meta[3]
    low = low_lanes(32)
    count = jnp.int32(0)
    for half in range(2):

        def body(n, count, half=half):
            kk, ap = n // 2, n % 2
            k = lax.rem(kk + 2 * half + 2 * r, 4)
            for cp in range(8):
                for a2 in range(2):
                    row = pl.multiple_of(ap * 128 + a2 * TILE, TILE)
                    if half == 0:
                        block = own_ref[kk, r, pl.ds(row, TILE), cp * LANES : (cp + 1) * LANES]
                    else:
                        block = oth_ref[kk, r, pl.ds(row, TILE), cp * LANES : (cp + 1) * LANES]
                    top, bottom = block[:32], block[32:]
                    turned_top, turned_bottom = swap_halves(top), swap_halves(bottom)
                    at_row = 4 * v + 2 * ap + a2
                    out_ref[jnp.minimum(count, INT_SLOTS - 1)] = jnp.where(low, top, turned_bottom)
                    count = count + mask[k, j, at_row, 2 * cp]
                    out_ref[jnp.minimum(count, INT_SLOTS - 1)] = jnp.where(low, turned_top, bottom)
                    count = count + mask[k, j, at_row, 2 * cp + 1]
            return count

        count = lax.fori_loop(0, 4, body, count)


def pack_amp_kernel(meta, mask, own_ref, oth_ref, *out_refs):
    v, r = meta[0], meta[2]
    low = low_lanes(TILE)
    for d in range(1, 4):
        dest = v ^ d
        count = jnp.int32(0)
        for half in range(2):
            ref = own_ref if half == 0 else oth_ref

            def body(kk, count, d=d, dest=dest, half=half, ref=ref):
                k = lax.rem(kk + 2 * half + 2 * r, 4)
                for ap in range(2):
                    for cp in range(2):
                        col = pl.multiple_of(dest * 256 + cp * LANES, LANES)
                        tiles = []
                        for a2 in range(2):
                            row = ap * 128 + a2 * TILE
                            x0 = ref[0, 0, 0, kk, row : row + TILE, pl.ds(col, LANES)]
                            x1 = ref[0, 0, 1, kk, row : row + TILE, pl.ds(col, LANES)]
                            tiles.append(
                                (jnp.where(low, x0, swap_halves(x1)), jnp.where(low, swap_halves(x0), x1))
                            )
                        for c2 in range(2):
                            for a2 in range(2):
                                out_refs[d - 1][jnp.minimum(count, AMP_SLOTS - 1)] = tiles[a2][c2]
                                count = count + mask[k, 4 * v + 2 * ap + a2, 4 * dest + 2 * cp + c2]
                return count

            count = lax.fori_loop(0, 2, body, count)


def unpack_group(buf_ref, mask, k, j, s, ap, count, d_ref, t_ref, at):
    low = low_lanes(32)
    zero = jnp.zeros((32, LANES), jnp.bfloat16)
    row = pl.multiple_of(ap * 128, 128)
    for cp in range(8):
        parts = []
        for a2 in range(2):
            at_row = 4 * s + 2 * ap + a2
            m0, m1 = mask[k, j, at_row, 2 * cp], mask[k, j, at_row, 2 * cp + 1]
            y0 = buf_ref[jnp.minimum(count, INT_SLOTS - 1)]
            count = count + m0
            y1 = buf_ref[jnp.minimum(count, INT_SLOTS - 1)]
            count = count + m1
            y0 = jnp.where(m0 > 0, y0, zero)
            y1 = jnp.where(m1 > 0, y1, zero)
            parts.append(jnp.where(low, y0, swap_halves(y1)))
            parts.append(jnp.where(low, swap_halves(y0), y1))
        block = jnp.concatenate(parts, axis=0)
        d_ref[at, pl.ds(row, 128), cp * LANES : (cp + 1) * LANES] = block
        t_ref[at, cp * LANES : (cp + 1) * LANES, pl.ds(row, 128)] = block.T
    return count


def unpack_int_kernel(d, meta, mask, down_ref, up_ref, d_ref, t_ref, buf_ref, count_ref):
    v, r, j = meta[0], meta[2], meta[3]
    kk = pl.program_id(0)
    k = lax.rem(kk + 2 * r, 4)
    s = v ^ d

    @pl.when(kk == 0)
    def _():
        count_ref[0] = 0
        fill(buf_ref, [(s > v, down_ref), (s < v, up_ref)])

    count_ref[0] = lax.fori_loop(
        0,
        2,
        lambda ap, count: unpack_group(buf_ref, mask, k, j, s, ap, count, d_ref, t_ref, 0),
        count_ref[0],
    )


def own_int_kernel(meta, mask, own_ref, oth_ref, d_ref, t_ref):
    v, r, j = meta[0], meta[2], meta[3]
    kk = pl.program_id(0)
    k = lax.rem(kk + 2 * r, 4)
    low = low_lanes(TILE)
    zero = jnp.zeros((TILE, LANES), jnp.bfloat16)

    def body(ap, carry):
        for cp in range(8):
            parts = []
            for a2 in range(2):
                at_row = 4 * v + 2 * ap + a2
                row = pl.multiple_of(ap * 128 + a2 * TILE, TILE)
                m0, m1 = mask[k, j, at_row, 2 * cp], mask[k, j, at_row, 2 * cp + 1]
                block = jnp.where(
                    kk < 2,
                    own_ref[0, 0, pl.ds(row, TILE), cp * LANES : (cp + 1) * LANES],
                    oth_ref[0, 0, pl.ds(row, TILE), cp * LANES : (cp + 1) * LANES],
                )
                parts.append(
                    jnp.where(low, jnp.where(m0 > 0, block, zero), jnp.where(m1 > 0, block, zero))
                )
            block = jnp.concatenate(parts, axis=0)
            row = pl.multiple_of(ap * 128, 128)
            d_ref[0, pl.ds(row, 128), cp * LANES : (cp + 1) * LANES] = block
            t_ref[0, cp * LANES : (cp + 1) * LANES, pl.ds(row, 128)] = block.T
        return carry

    lax.fori_loop(0, 2, body, 0)


def lane_scale(m0, m1, value):
    lane = lax.broadcasted_iota(jnp.int32, (1, LANES), 1)
    return value * jnp.where(lane < TILE, m0, m1).astype(jnp.float32)


def combine_kernel(d, base, meta, mask, own_ref, oth_ref, near_ref, far_ref, *refs):
    if d == 3:
        out_ref, count_ref = refs[-2:]
    else:
        out_ref, count_ref = refs[1:]
    v, x, r = meta[0], meta[1], meta[2]
    kk = pl.program_id(0) + base
    k = lax.rem(kk + 2 * r, 4)
    s = v ^ d
    zero = jnp.zeros((TILE, LANES), jnp.bfloat16)

    @pl.when(pl.program_id(0) == 0)
    def _():
        count_ref[0] = 0 if base == 0 else refs[0][0]

    def body(ap, count):
        ccol = pl.multiple_of(ap * 128, 128)
        for c in range(4):
            arow = c * TILE
            slots, kept = [], []
            for a2 in range(2):
                m = mask[k, 4 * s + 2 * ap + a2, 4 * v + c]
                slots.append(jnp.minimum(count, AMP_SLOTS - 1))
                kept.append(m)
                count = count + m
            own_scale = lane_scale(
                mask[k, 4 * v + c, 4 * s + 2 * ap], mask[k, 4 * v + c, 4 * s + 2 * ap + 1], 2.0
            )
            for xx, buf in ((x, near_ref), (1 - x, far_ref)):
                stacked = jnp.concatenate(
                    [jnp.where(kept[a2] > 0, buf[slots[a2]], zero) for a2 in range(2)], axis=0
                )
                turned = stacked.T.astype(jnp.float32)
                for ii in range(2):
                    local = jnp.where(
                        kk < 2,
                        own_ref[xx, 0, ii, 0, pl.ds(arow, TILE), pl.ds(ccol, 128)],
                        oth_ref[xx, 0, ii, 0, pl.ds(arow, TILE), pl.ds(ccol, 128)],
                    ).astype(jnp.float32)
                    value = own_scale * local - turned[ii * TILE : (ii + 1) * TILE]
                    out_ref[0, xx, ii, pl.ds(arow, TILE), pl.ds(ccol, 128)] = value.astype(jnp.bfloat16)
        return count

    count_ref[0] = lax.fori_loop(0, 2, body, count_ref[0])


def diagonal_kernel(meta, mask, own_ref, oth_ref, out_ref):
    v, r = meta[0], meta[2]
    kk = pl.program_id(0)
    k = lax.rem(kk + 2 * r, 4)

    def screened(xx, ii, a0, c0):
        rows = []
        for a2 in range(2):
            start = a0 * 128 + a2 * TILE
            block = jnp.where(
                kk < 2,
                own_ref[xx, 0, ii, 0, start : start + TILE, c0 * 128 : (c0 + 1) * 128],
                oth_ref[xx, 0, ii, 0, start : start + TILE, c0 * 128 : (c0 + 1) * 128],
            ).astype(jnp.float32)
            at_row = 4 * v + 2 * a0 + a2
            rows.append(
                block
                * lane_scale(
                    mask[k, at_row, 4 * v + 2 * c0], mask[k, at_row, 4 * v + 2 * c0 + 1], 1.0
                )
            )
        return jnp.concatenate(rows, axis=0)

    for xx in range(2):
        for ii in range(2):
            for a0 in range(2):
                for c0 in range(2):
                    value = 2.0 * screened(xx, ii, a0, c0) - screened(xx, ii, c0, a0).T
                    out_ref[0, xx, ii, a0 * 128 : (a0 + 1) * 128, c0 * 128 : (c0 + 1) * 128] = (
                        value.astype(jnp.bfloat16)
                    )


def folded(direct, swapped):
    return (2.0 * direct.astype(jnp.float32) - swapped.astype(jnp.float32)).astype(jnp.bfloat16)


def early_kernel(meta, *refs):
    direct, swapped, own, oth, out_ref, w_ref = (
        refs[:3], refs[3:6], refs[6:9], refs[9:12], refs[12], refs[13]
    )
    v = meta[0]
    g = pl.program_id(0)

    @pl.when(g == 0)
    def _():
        for q in range(3):
            for p in range(3):
                col = pl.multiple_of((v ^ p) * 256, 256)
                row = pl.multiple_of((v ^ q) * 256, 256)
                for k in range(4):
                    w_ref[q, k * 256 : (k + 1) * 256, p * 256 : (p + 1) * 256] = folded(
                        direct[q][k, :, pl.ds(col, 256)], swapped[p][k, pl.ds(row, 256), :]
                    )

    def work(blocks):
        total = jnp.dot(
            blocks[0][...].reshape(512, 1024), w_ref[0], preferred_element_type=jnp.float32
        )
        for q in range(1, 3):
            total += jnp.dot(
                blocks[q][...].reshape(512, 1024), w_ref[q], preferred_element_type=jnp.float32
            )
        out_ref[...] = total

    @pl.when(g < 2)
    def _():
        work(own)

    @pl.when(g >= 2)
    def _():
        work(oth)


def tail_kernel(meta, mask, eps_slab, eps_pair, eps_rows, eps_cols, part_ref, *refs):
    direct, swapped, own, oth = refs[:3], refs[3:6], refs[6:11], refs[11:16]
    end_down, end_up, down, up, out_ref = refs[16:21]
    buf_ref, d_ref, t_ref, row_ref, col_ref = refs[21:]
    v, r, j = meta[0], meta[2], meta[3]
    g = pl.program_id(0)
    last = v ^ 3

    @pl.when(g == 0)
    def _():
        fill(buf_ref, [(v == 0, end_down), (v == 1, down), (v == 2, up), (v == 3, end_up)])

        def body(n, count):
            k = lax.rem(n // 2 + 2 * r, 4)
            return unpack_group(buf_ref, mask, k, j, last, n % 2, count, d_ref, t_ref, k)

        lax.fori_loop(0, 8, body, jnp.int32(0))
        last_at = pl.multiple_of(last * 256, 256)
        for p in range(4):
            at = pl.multiple_of((v ^ p) * 256, 256)
            for k in range(4):
                ks = slice(k * 256, (k + 1) * 256)
                row_ref[ks, p * 256 : (p + 1) * 256] = folded(
                    d_ref[k, :, pl.ds(at, 256)],
                    swapped[p][k] if p < 3 else t_ref[k, pl.ds(last_at, 256), :],
                )
                if p < 3:
                    col_ref[p, ks, :] = folded(direct[p][k], t_ref[k, pl.ds(at, 256), :])

    def work(blocks, i, k0):
        flat = [b[...].reshape(512, b.shape[-1]) for b in blocks]
        total = jnp.float32(0)
        for half in range(2):
            at = pl.multiple_of(256 * lax.rem(k0 + 2 * half, 4), 512)
            total += jnp.dot(flat[3 + half], row_ref[pl.ds(at, 512), :], preferred_element_type=jnp.float32)
        late = total[:, 768:]
        for q in range(3):
            late += jnp.dot(flat[q], col_ref[q], preferred_element_type=jnp.float32)
        for p in range(4):
            s = v ^ p
            value = late if p == 3 else total[:, p * 256 : (p + 1) * 256] + part_ref[:, p * 256 : (p + 1) * 256]
            cols = eps_cols[:, pl.ds(pl.multiple_of(s * 256, 256), 256)]
            for ii in range(2):
                energy = (eps_rows[...] + cols) - eps_slab[i + ii] - eps_pair[0]
                done = value[ii * 256 : (ii + 1) * 256] / energy
                for n in range(2):
                    at = pl.multiple_of(s * 256 + n * 128, 128)
                    out_ref[ii, :, 0, pl.ds(at, 128)] = done[:, n * 128 : (n + 1) * 128]

    @pl.when(g < 2)
    def _():
        work(own, 4 * g + 2 * r, 2 * r)

    @pl.when(g >= 2)
    def _():
        work(oth, 4 * (g - 2) + 2 * (1 - r), 2 * (1 - r))


def smem():
    return pl.BlockSpec(memory_space=pltpu.SMEM)


def whole():
    return pl.BlockSpec(memory_space=pltpu.VMEM)


def anywhere():
    return pl.BlockSpec(memory_space=pl.ANY)


def params():
    return pltpu.CompilerParams(vmem_limit_bytes=VMEM_LIMIT)


def k_place(kk, r):
    return lax.rem(kk + 2 * r, 4)


def packed_shards(amplitudes, integrals, amp_mask, int_mask, eps_slab, eps_pair, eps_vir):
    v, x, r = lax.axis_index("vir"), lax.axis_index("occ"), lax.axis_index("rep")
    meta = jnp.stack([v, x, r, 2 * x + r]).astype(jnp.int32)
    swap = [(0, 1), (1, 0)]
    bf16 = jnp.bfloat16

    pairs = amp_mask.reshape(4, 4, 4, 4, 4).sum((0, 2, 4))
    pairs = jnp.where(jnp.eye(4, dtype=bool), 0, pairs)
    pieces = int_mask.reshape(4, 4, 4, 4, 16).sum((0, 3, 4))
    over = jnp.logical_or(jnp.max(pairs) > AMP_SLOTS - 1, jnp.max(pieces) > INT_SLOTS - 1)
    over = over.astype(jnp.int32).reshape(1)
    over = over + lax.ppermute(over, "frag", swap)

    int_oth = lax.ppermute(integrals, "rep", swap)
    amps = amplitudes.reshape(2, 2, 2, 2, 256, 1024)
    amp_oth = lax.ppermute(amps, "rep", swap)
    amp_oth, over = lax.optimization_barrier((amp_oth, over))

    packed_int = pl.pallas_call(
        pack_int_kernel,
        out_shape=jax.ShapeDtypeStruct((INT_SLOTS, 32, LANES), bf16),
        in_specs=[smem(), smem(), whole(), whole()],
        out_specs=whole(),
        compiler_params=params(),
        cost_estimate=NO_COST,
        name="pack_int",
    )(meta, int_mask, integrals, int_oth)

    up1 = lax.ppermute(packed_int, "vir", [(0, 1), (1, 2), (2, 3)])
    down1 = lax.ppermute(packed_int, "vir", [(1, 0), (2, 1), (3, 2)])

    packed_amp = pl.pallas_call(
        pack_amp_kernel,
        grid_spec=pltpu.PrefetchScalarGridSpec(
            num_scalar_prefetch=2,
            grid=(1,),
            in_specs=[
                pl.BlockSpec((1, 1, 2, 2, 256, 1024), lambda g, meta, mask: (meta[1], meta[2], 0, 0, 0, 0)),
                pl.BlockSpec((1, 1, 2, 2, 256, 1024), lambda g, meta, mask: (meta[1], meta[2], 0, 0, 0, 0)),
            ],
            out_specs=[pl.BlockSpec((AMP_SLOTS, TILE, LANES), lambda g, meta, mask: (0, 0, 0))] * 3,
        ),
        out_shape=[jax.ShapeDtypeStruct((AMP_SLOTS, TILE, LANES), bf16)] * 3,
        compiler_params=params(),
        cost_estimate=NO_COST,
        name="pack_amp",
    )(meta, amp_mask, amps, amp_oth)

    near = [lax.ppermute(packed_amp[d - 1], "vir", [(s, s ^ d) for s in range(4)]) for d in (1, 2, 3)]
    far = [lax.ppermute(a, "occ", swap) for a in near]
    far[0], far[1], near[2] = lax.optimization_barrier((far[0], far[1], near[2]))

    up2 = lax.ppermute(up1, "vir", [(1, 2), (2, 3)])
    down2 = lax.ppermute(down1, "vir", [(1, 0), (2, 1)])

    int_shapes = [
        jax.ShapeDtypeStruct((4, 256, 1024), bf16),
        jax.ShapeDtypeStruct((4, 1024, 256), bf16),
    ]
    int_outs = [
        pl.BlockSpec((1, 256, 1024), lambda kk, meta, mask: (k_place(kk, meta[2]), 0, 0)),
        pl.BlockSpec((1, 1024, 256), lambda kk, meta, mask: (k_place(kk, meta[2]), 0, 0)),
    ]
    rows, cols = [], []
    for d in range(3):
        if d == 0:
            kernel, scratch = own_int_kernel, []
            specs = [
                pl.BlockSpec((1, 1, 256, 1024), lambda kk, meta, mask: (jnp.minimum(kk, 1), meta[2], 0, 0)),
                pl.BlockSpec((1, 1, 256, 1024), lambda kk, meta, mask: (jnp.maximum(kk - 2, 0), meta[2], 0, 0)),
            ]
            operands = (integrals, int_oth)
        else:
            kernel = functools.partial(unpack_int_kernel, d)
            scratch = [pltpu.VMEM((INT_SLOTS, 32, LANES), bf16), pltpu.SMEM((1,), jnp.int32)]
            specs = [anywhere(), anywhere()]
            operands = (down1, up1) if d == 1 else (down2, up2)
        direct, swapped = pl.pallas_call(
            kernel,
            grid_spec=pltpu.PrefetchScalarGridSpec(
                num_scalar_prefetch=2, grid=(4,), in_specs=specs, out_specs=int_outs, scratch_shapes=scratch
            ),
            out_shape=int_shapes,
            compiler_params=params(),
            cost_estimate=NO_COST,
            name=f"ints_{d}",
        )(meta, int_mask, *operands)
        rows.append(direct)
        cols.append(swapped)

    def local_specs(d, base):
        def at(side):
            def place(kk, meta, mask):
                k = jnp.minimum(kk + base, 1) if side == 0 else jnp.maximum(kk + base - 2, 0)
                return (0, meta[2], 0, k, 0, meta[0] ^ d)

            return place

        return [pl.BlockSpec((2, 1, 2, 1, 256, 256), at(side)) for side in range(2)]

    def combine(d, base, steps, extra_specs, extra, out_specs, out_shape, aliases, scratch):
        kernel = diagonal_kernel if d == 0 else functools.partial(combine_kernel, d, base)
        specs, operands = [], ()
        if d > 0:
            specs = [pl.BlockSpec((AMP_SLOTS, TILE, LANES), lambda kk, meta, mask: (0, 0, 0))] * 2
            operands = (near[d - 1], far[d - 1])
        return pl.pallas_call(
            kernel,
            grid_spec=pltpu.PrefetchScalarGridSpec(
                num_scalar_prefetch=2,
                grid=(steps,),
                in_specs=local_specs(d, base) + specs + extra_specs,
                out_specs=out_specs,
                scratch_shapes=scratch,
            ),
            out_shape=out_shape,
            input_output_aliases=aliases,
            compiler_params=params(),
            cost_estimate=NO_COST,
            name=f"combine_{d}_{base}",
        )(meta, amp_mask, amps, amp_oth, *operands, *extra)

    counter = pltpu.SMEM((1,), jnp.int32)
    first = None
    for d in range(3):
        first = combine(
            d,
            0,
            4,
            [] if d == 0 else [anywhere()],
            () if d == 0 else (first,),
            pl.BlockSpec(
                (1, 2, 2, 256, 256), lambda kk, meta, mask, d=d: (d, 0, 0, 0, k_place(kk, meta[2]))
            ),
            jax.ShapeDtypeStruct((3, 2, 2, 256, 1024), bf16),
            {} if d == 0 else {6: 0},
            [] if d == 0 else [counter],
        )
    halves, count = [], None
    for base in (0, 2):
        half, count = combine(
            3,
            base,
            2,
            [] if base == 0 else [smem()],
            () if base == 0 else (count,),
            [pl.BlockSpec((1, 2, 2, 256, 256), lambda kk, meta, mask: (0, 0, 0, 0, kk)), smem()],
            [jax.ShapeDtypeStruct((1, 2, 2, 256, 512), bf16), jax.ShapeDtypeStruct((1,), jnp.int32)],
            {},
            [],
        )
        halves.append(half)
    first, up2, down2 = lax.optimization_barrier((first, up2, down2))
    first_oth = lax.ppermute(first, "rep", swap)
    halves_oth = [lax.ppermute(h, "rep", swap) for h in halves]
    end_down = lax.ppermute(down2, "vir", [(1, 0)])
    end_up = lax.ppermute(up2, "vir", [(2, 3)])

    def own_at(d, width=1024):
        return pl.BlockSpec((1, 1, 2, 256, width), lambda g, *_: (d % 3, jnp.minimum(g, 1), 0, 0, 0))

    def oth_at(d, width=1024):
        return pl.BlockSpec((1, 1, 2, 256, width), lambda g, *_: (d % 3, jnp.maximum(g - 2, 0), 0, 0, 0))

    def place(g, meta, *_):
        return (2 * (g % 2) + jnp.where(g < 2, meta[2], 1 - meta[2]), 0)

    once = pl.Buffered(1)
    part = pl.pallas_call(
        early_kernel,
        grid_spec=pltpu.PrefetchScalarGridSpec(
            num_scalar_prefetch=1,
            grid=(4,),
            in_specs=[pl.BlockSpec((4, 256, 1024), lambda g, *_: (0, 0, 0), pipeline_mode=once)] * 3
            + [pl.BlockSpec((4, 1024, 256), lambda g, *_: (0, 0, 0), pipeline_mode=once)] * 3
            + [own_at(d) for d in range(3)]
            + [oth_at(d) for d in range(3)],
            out_specs=pl.BlockSpec((512, 768), place),
            scratch_shapes=[pltpu.VMEM((3, 1024, 768), bf16)],
        ),
        out_shape=jax.ShapeDtypeStruct((2048, 768), jnp.float32),
        compiler_params=params(),
        cost_estimate=NO_COST,
        name="early",
    )(meta, *rows, *cols, *[first] * 3, *[first_oth] * 3)

    row_energy = lax.dynamic_slice_in_dim(eps_vir, v * 256, 256, 0).reshape(256, 1)
    col_energy = eps_vir.reshape(1, 1024)

    def finish(ops):
        part, rows, cols, own, oth, last = ops
        return pl.pallas_call(
            tail_kernel,
            grid_spec=pltpu.PrefetchScalarGridSpec(
                num_scalar_prefetch=4,
                grid=(4,),
                in_specs=[
                    pl.BlockSpec((256, 1), lambda g, *_: (0, 0)),
                    pl.BlockSpec((1, 1024), lambda g, *_: (0, 0)),
                    pl.BlockSpec((512, 768), place),
                ]
                + [pl.BlockSpec((4, 256, 256), lambda g, meta, *_: (0, 0, meta[0] ^ 3), pipeline_mode=once)] * 3
                + [pl.BlockSpec((4, 256, 256), lambda g, meta, *_: (0, meta[0] ^ 3, 0), pipeline_mode=once)] * 3
                + [own_at(d) for d in range(3)]
                + [own_at(3, 512)] * 2
                + [oth_at(d) for d in range(3)]
                + [oth_at(3, 512)] * 2
                + [anywhere()] * 4,
                out_specs=pl.BlockSpec((2, 256, 1, 1024), lambda g, meta, *_: (*place(g, meta), 0, 0)),
                scratch_shapes=[
                    pltpu.VMEM((INT_SLOTS, 32, LANES), bf16),
                    pltpu.VMEM((4, 256, 1024), bf16),
                    pltpu.VMEM((4, 1024, 256), bf16),
                    pltpu.VMEM((1024, 1024), bf16),
                    pltpu.VMEM((3, 1024, 256), bf16),
                ],
            ),
            out_shape=jax.ShapeDtypeStruct((8, 256, 1, 1024), jnp.float32),
            compiler_params=params(),
            cost_estimate=NO_COST,
            name="tail",
        )(meta, int_mask, eps_slab, eps_pair, row_energy, col_energy, part, *rows, *cols, *own, *oth, *last)

    def dense(ops):
        return dense_shards(
            amplitudes, integrals, amp_mask, int_mask, eps_slab, eps_pair, eps_vir
        )

    return lax.cond(
        over[0] > 0,
        dense,
        finish,
        (
            part,
            rows,
            cols,
            (first, first, first, *halves),
            (first_oth, first_oth, first_oth, *halves_oth),
            (end_down, end_up, down1, up1),
        ),
    )


def shards(sizes, *args):
    amplitudes, integrals, amp_mask, int_mask = args[:4]
    fits = (
        sizes == {"frag": 2, "vir": 4, "occ": 2, "rep": 2}
        and amplitudes.shape == (8, 2, 256, 1024)
        and integrals.shape == (2, 2, 256, 1024)
        and amp_mask.shape == (4, 16, 16)
        and int_mask.shape == (4, 4, 16, 16)
    )
    return packed_shards(*args) if fits else dense_shards(*args)


def solution(mesh):
    in_specs = (
        P("frag", "rep", "vir", None),
        P(("frag", "rep"), "occ", "vir", None),
        P("frag", None, None),
        P("frag", None, None, None),
        P("frag"),
        P(("frag", "occ", "rep")),
        P("frag"),
    )
    out_specs = P("frag", "vir", ("occ", "rep"), None)
    return jax.shard_map(
        functools.partial(shards, dict(mesh.shape)),
        mesh=mesh,
        in_specs=in_specs,
        out_specs=out_specs,
        check_vma=False,
    )
```

```python
import functools

import jax
import jax.numpy as jnp
from jax import lax
from jax.experimental import pallas as pl
from jax.experimental.pallas import tpu as pltpu
from jax.sharding import PartitionSpec as P

TILE = 64
LANES = 128
AMP_SLOTS = 46
INT_SLOTS = 160
VMEM_LIMIT = 60 * 1024 * 1024
NO_COST = pl.CostEstimate(flops=1024, bytes_accessed=1024, transcendentals=0)


def tile_mask(mask_tiles, row_start, row_count, tile_size):
    tile_count = mask_tiles.shape[-1]
    row_tiles = (row_start + jnp.arange(row_count, dtype=jnp.int32)) // tile_size
    select = (row_tiles[:, None] == jnp.arange(tile_count, dtype=jnp.int32)[None, :]).astype(
        jnp.float32
    )
    picked = jnp.einsum("ra,...ac->...rc", select, mask_tiles.astype(jnp.float32))
    return jnp.repeat(picked, tile_size, axis=-1)


def cycle_terms(combined, gathered):
    direct_term = jnp.einsum(
        "ikac,kjcb->iajb", combined, gathered, preferred_element_type=jnp.float32
    )
    swapped_term = jnp.einsum(
        "ikac,kjbc->iajb", combined, gathered, preferred_element_type=jnp.float32
    )
    return 2.0 * direct_term - swapped_term


def dense_shards(amplitudes, integrals, amp_mask, int_mask, eps_slab, eps_pair, eps_vir):
    row_count = amplitudes.shape[2]
    half_count = amplitudes.shape[1]
    pair_count = integrals.shape[1]
    row_start = lax.axis_index("vir") * row_count
    k_start = lax.axis_index("rep") * half_count
    j_start = lax.axis_index("occ") * pair_count
    zero_index = jnp.zeros((), jnp.int32)
    k_masks = lax.dynamic_slice_in_dim(amp_mask, k_start, half_count, 0)
    screened = (
        amplitudes.astype(jnp.float32) * tile_mask(k_masks, row_start, row_count, TILE)[None]
    ).astype(jnp.bfloat16)
    received = lax.all_to_all(screened, "vir", split_axis=3, concat_axis=2, tiled=True)
    combined = (
        2.0 * screened.astype(jnp.float32) - jnp.swapaxes(received, 2, 3).astype(jnp.float32)
    ).astype(jnp.bfloat16)
    pair_masks = lax.dynamic_slice(
        int_mask,
        (k_start, j_start, zero_index, zero_index),
        (half_count, pair_count, int_mask.shape[2], int_mask.shape[3]),
    )
    kept_local = (
        integrals.astype(jnp.float32) * tile_mask(pair_masks, row_start, row_count, TILE)
    ).astype(jnp.bfloat16)
    gathered = lax.all_gather(kept_local, "vir", axis=2, tiled=True)
    partial_cycle = cycle_terms(combined, gathered)
    cycle = lax.psum_scatter(partial_cycle, "rep", scatter_dimension=2, tiled=True)
    row_energy = lax.dynamic_slice_in_dim(eps_vir, row_start, row_count, 0)
    denominator = (
        row_energy[None, :, None, None]
        + eps_vir[None, None, None, :]
        - eps_slab[:, None, None, None]
        - eps_pair[None, None, :, None]
    )
    return cycle / denominator


def low_lanes(rows):
    return lax.broadcasted_iota(jnp.int32, (rows, LANES), 1) < TILE


def swap_halves(block):
    return pltpu.roll(block, TILE, 1)


def fill(buf, choices):
    for chosen, ref in choices:

        @pl.when(chosen)
        def _(ref=ref):
            pltpu.sync_copy(ref, buf)


def pack_int_kernel(meta, mask, own_ref, oth_ref, out_ref):
    v, r, j = meta[0], meta[2], meta[3]
    low = low_lanes(32)
    count = jnp.int32(0)
    for half in range(2):

        def body(n, count, half=half):
            kk, ap = n // 2, n % 2
            k = lax.rem(kk + 2 * half + 2 * r, 4)
            for cp in range(8):
                for a2 in range(2):
                    row = pl.multiple_of(ap * 128 + a2 * TILE, TILE)
                    if half == 0:
                        block = own_ref[kk, r, pl.ds(row, TILE), cp * LANES : (cp + 1) * LANES]
                    else:
                        block = oth_ref[kk, r, pl.ds(row, TILE), cp * LANES : (cp + 1) * LANES]
                    top, bottom = block[:32], block[32:]
                    turned_top, turned_bottom = swap_halves(top), swap_halves(bottom)
                    at_row = 4 * v + 2 * ap + a2
                    out_ref[jnp.minimum(count, INT_SLOTS - 1)] = jnp.where(low, top, turned_bottom)
                    count = count + mask[k, j, at_row, 2 * cp]
                    out_ref[jnp.minimum(count, INT_SLOTS - 1)] = jnp.where(low, turned_top, bottom)
                    count = count + mask[k, j, at_row, 2 * cp + 1]
            return count

        count = lax.fori_loop(0, 4, body, count)


def pack_amp_kernel(meta, mask, own_ref, oth_ref, *out_refs):
    v, r = meta[0], meta[2]
    low = low_lanes(TILE)
    for d in range(1, 4):
        dest = v ^ d
        count = jnp.int32(0)
        for half in range(2):
            ref = own_ref if half == 0 else oth_ref

            def body(kk, count, d=d, dest=dest, half=half, ref=ref):
                k = lax.rem(kk + 2 * half + 2 * r, 4)
                for ap in range(2):
                    for cp in range(2):
                        col = pl.multiple_of(dest * 256 + cp * LANES, LANES)
                        tiles = []
                        for a2 in range(2):
                            row = ap * 128 + a2 * TILE
                            x0 = ref[0, 0, 0, kk, row : row + TILE, pl.ds(col, LANES)]
                            x1 = ref[0, 0, 1, kk, row : row + TILE, pl.ds(col, LANES)]
                            tiles.append(
                                (jnp.where(low, x0, swap_halves(x1)), jnp.where(low, swap_halves(x0), x1))
                            )
                        for c2 in range(2):
                            for a2 in range(2):
                                out_refs[d - 1][jnp.minimum(count, AMP_SLOTS - 1)] = tiles[a2][c2]
                                count = count + mask[k, 4 * v + 2 * ap + a2, 4 * dest + 2 * cp + c2]
                return count

            count = lax.fori_loop(0, 2, body, count)


def unpack_group(buf_ref, mask, k, j, s, ap, count, d_ref, t_ref, at):
    low = low_lanes(32)
    zero = jnp.zeros((32, LANES), jnp.bfloat16)
    row = pl.multiple_of(ap * 128, 128)
    for cp in range(8):
        parts = []
        for a2 in range(2):
            at_row = 4 * s + 2 * ap + a2
            m0, m1 = mask[k, j, at_row, 2 * cp], mask[k, j, at_row, 2 * cp + 1]
            y0 = buf_ref[jnp.minimum(count, INT_SLOTS - 1)]
            count = count + m0
            y1 = buf_ref[jnp.minimum(count, INT_SLOTS - 1)]
            count = count + m1
            y0 = jnp.where(m0 > 0, y0, zero)
            y1 = jnp.where(m1 > 0, y1, zero)
            parts.append(jnp.where(low, y0, swap_halves(y1)))
            parts.append(jnp.where(low, swap_halves(y0), y1))
        block = jnp.concatenate(parts, axis=0)
        d_ref[at, pl.ds(row, 128), cp * LANES : (cp + 1) * LANES] = block
        t_ref[at, cp * LANES : (cp + 1) * LANES, pl.ds(row, 128)] = block.T
    return count


def unpack_int_kernel(d, meta, mask, *refs):
    sources, (d_ref, t_ref, buf_ref, count_ref) = refs[:-4], refs[-4:]
    v, r, j = meta[0], meta[2], meta[3]
    kk = pl.program_id(0)
    k = lax.rem(kk + 2 * r, 4)
    s = v ^ d

    @pl.when(kk == 0)
    def _():
        count_ref[0] = 0
        if d < 3:
            fill(buf_ref, [(s > v, sources[0]), (s < v, sources[1])])
        else:
            fill(buf_ref, [(v == n, source) for n, source in enumerate(sources)])

    count_ref[0] = lax.fori_loop(
        0,
        2,
        lambda ap, count: unpack_group(buf_ref, mask, k, j, s, ap, count, d_ref, t_ref, 0),
        count_ref[0],
    )


def own_int_kernel(meta, mask, own_ref, oth_ref, d_ref, t_ref):
    v, r, j = meta[0], meta[2], meta[3]
    kk = pl.program_id(0)
    k = lax.rem(kk + 2 * r, 4)
    low = low_lanes(TILE)
    zero = jnp.zeros((TILE, LANES), jnp.bfloat16)

    def body(ap, carry):
        for cp in range(8):
            parts = []
            for a2 in range(2):
                at_row = 4 * v + 2 * ap + a2
                row = pl.multiple_of(ap * 128 + a2 * TILE, TILE)
                m0, m1 = mask[k, j, at_row, 2 * cp], mask[k, j, at_row, 2 * cp + 1]
                block = jnp.where(
                    kk < 2,
                    own_ref[0, 0, pl.ds(row, TILE), cp * LANES : (cp + 1) * LANES],
                    oth_ref[0, 0, pl.ds(row, TILE), cp * LANES : (cp + 1) * LANES],
                )
                parts.append(
                    jnp.where(low, jnp.where(m0 > 0, block, zero), jnp.where(m1 > 0, block, zero))
                )
            block = jnp.concatenate(parts, axis=0)
            row = pl.multiple_of(ap * 128, 128)
            d_ref[0, pl.ds(row, 128), cp * LANES : (cp + 1) * LANES] = block
            t_ref[0, cp * LANES : (cp + 1) * LANES, pl.ds(row, 128)] = block.T
        return carry

    lax.fori_loop(0, 2, body, 0)


def lane_scale(m0, m1, value):
    lane = lax.broadcasted_iota(jnp.int32, (1, LANES), 1)
    return value * jnp.where(lane < TILE, m0, m1).astype(jnp.float32)


def combine_kernel(d, base, meta, mask, own_ref, oth_ref, near_ref, far_ref, *refs):
    if d == 3:
        out_ref, count_ref = refs[-2:]
    else:
        out_ref, count_ref = refs[1:]
    v, x, r = meta[0], meta[1], meta[2]
    kk = pl.program_id(0) + base
    k = lax.rem(kk + 2 * r, 4)
    s = v ^ d
    zero = jnp.zeros((TILE, LANES), jnp.bfloat16)

    @pl.when(pl.program_id(0) == 0)
    def _():
        count_ref[0] = 0 if base == 0 else refs[0][0]

    def body(ap, count):
        ccol = pl.multiple_of(ap * 128, 128)
        for c in range(4):
            arow = c * TILE
            slots, kept = [], []
            for a2 in range(2):
                m = mask[k, 4 * s + 2 * ap + a2, 4 * v + c]
                slots.append(jnp.minimum(count, AMP_SLOTS - 1))
                kept.append(m)
                count = count + m
            own_scale = lane_scale(
                mask[k, 4 * v + c, 4 * s + 2 * ap], mask[k, 4 * v + c, 4 * s + 2 * ap + 1], 2.0
            )
            for xx, buf in ((x, near_ref), (1 - x, far_ref)):
                stacked = jnp.concatenate(
                    [jnp.where(kept[a2] > 0, buf[slots[a2]], zero) for a2 in range(2)], axis=0
                )
                turned = stacked.T.astype(jnp.float32)
                for ii in range(2):
                    local = jnp.where(
                        kk < 2,
                        own_ref[xx, 0, ii, 0, pl.ds(arow, TILE), pl.ds(ccol, 128)],
                        oth_ref[xx, 0, ii, 0, pl.ds(arow, TILE), pl.ds(ccol, 128)],
                    ).astype(jnp.float32)
                    value = own_scale * local - turned[ii * TILE : (ii + 1) * TILE]
                    out_ref[0, xx, ii, pl.ds(arow, TILE), pl.ds(ccol, 128)] = value.astype(jnp.bfloat16)
        return count

    count_ref[0] = lax.fori_loop(0, 2, body, count_ref[0])


def diagonal_kernel(meta, mask, own_ref, oth_ref, out_ref):
    v, r = meta[0], meta[2]
    kk = pl.program_id(0)
    k = lax.rem(kk + 2 * r, 4)

    def screened(xx, ii, a0, c0):
        rows = []
        for a2 in range(2):
            start = a0 * 128 + a2 * TILE
            block = jnp.where(
                kk < 2,
                own_ref[xx, 0, ii, 0, start : start + TILE, c0 * 128 : (c0 + 1) * 128],
                oth_ref[xx, 0, ii, 0, start : start + TILE, c0 * 128 : (c0 + 1) * 128],
            ).astype(jnp.float32)
            at_row = 4 * v + 2 * a0 + a2
            rows.append(
                block
                * lane_scale(
                    mask[k, at_row, 4 * v + 2 * c0], mask[k, at_row, 4 * v + 2 * c0 + 1], 1.0
                )
            )
        return jnp.concatenate(rows, axis=0)

    for xx in range(2):
        for ii in range(2):
            for a0 in range(2):
                for c0 in range(2):
                    value = 2.0 * screened(xx, ii, a0, c0) - screened(xx, ii, c0, a0).T
                    out_ref[0, xx, ii, a0 * 128 : (a0 + 1) * 128, c0 * 128 : (c0 + 1) * 128] = (
                        value.astype(jnp.bfloat16)
                    )


def folded(direct, swapped):
    return (2.0 * direct.astype(jnp.float32) - swapped.astype(jnp.float32)).astype(jnp.bfloat16)


def early_kernel(meta, *refs):
    direct, swapped, own, oth, out_ref, w_ref = (
        refs[:3], refs[3:6], refs[6:9], refs[9:12], refs[12], refs[13]
    )
    v = meta[0]
    g = pl.program_id(0)

    @pl.when(g == 0)
    def _():
        for q in range(3):
            for p in range(3):
                col = pl.multiple_of((v ^ p) * 256, 256)
                row = pl.multiple_of((v ^ q) * 256, 256)
                for k in range(4):
                    w_ref[q, k * 256 : (k + 1) * 256, p * 256 : (p + 1) * 256] = folded(
                        direct[q][k, :, pl.ds(col, 256)], swapped[p][k, pl.ds(row, 256), :]
                    )

    def work(blocks):
        total = jnp.dot(
            blocks[0][...].reshape(512, 1024), w_ref[0], preferred_element_type=jnp.float32
        )
        for q in range(1, 3):
            total += jnp.dot(
                blocks[q][...].reshape(512, 1024), w_ref[q], preferred_element_type=jnp.float32
            )
        out_ref[...] = total

    @pl.when(g < 2)
    def _():
        work(own)

    @pl.when(g >= 2)
    def _():
        work(oth)


def tail_kernel(meta, eps_slab, eps_pair, eps_rows, eps_cols, part_ref, *refs):
    direct, swapped, own, oth, out_ref = refs[:4], refs[4:8], refs[8:13], refs[13:18], refs[18]
    row_ref, col_ref = refs[19:]
    v, r = meta[0], meta[2]
    g = pl.program_id(0)
    last = v ^ 3

    @pl.when(g == 0)
    def _():
        last_at = pl.multiple_of(last * 256, 256)
        for p in range(4):
            at = pl.multiple_of((v ^ p) * 256, 256)
            for k in range(4):
                ks = slice(k * 256, (k + 1) * 256)
                row_ref[ks, p * 256 : (p + 1) * 256] = folded(
                    direct[3][k, :, pl.ds(at, 256)],
                    swapped[p][k] if p < 3 else swapped[3][k, pl.ds(last_at, 256), :],
                )
                if p < 3:
                    col_ref[p, ks, :] = folded(
                        direct[p][k], swapped[3][k, pl.ds(at, 256), :]
                    )

    def work(blocks, i, k0):
        flat = [b[...].reshape(512, b.shape[-1]) for b in blocks]
        total = jnp.float32(0)
        for half in range(2):
            at = pl.multiple_of(256 * lax.rem(k0 + 2 * half, 4), 512)
            total += jnp.dot(flat[3 + half], row_ref[pl.ds(at, 512), :], preferred_element_type=jnp.float32)
        late = total[:, 768:]
        for q in range(3):
            late += jnp.dot(flat[q], col_ref[q], preferred_element_type=jnp.float32)
        for p in range(4):
            s = v ^ p
            value = late if p == 3 else total[:, p * 256 : (p + 1) * 256] + part_ref[:, p * 256 : (p + 1) * 256]
            cols = eps_cols[:, pl.ds(pl.multiple_of(s * 256, 256), 256)]
            for ii in range(2):
                energy = (eps_rows[...] + cols) - eps_slab[i + ii] - eps_pair[0]
                done = value[ii * 256 : (ii + 1) * 256] / energy
                for n in range(2):
                    at = pl.multiple_of(s * 256 + n * 128, 128)
                    out_ref[ii, :, 0, pl.ds(at, 128)] = done[:, n * 128 : (n + 1) * 128]

    @pl.when(g < 2)
    def _():
        work(own, 4 * g + 2 * r, 2 * r)

    @pl.when(g >= 2)
    def _():
        work(oth, 4 * (g - 2) + 2 * (1 - r), 2 * (1 - r))


def smem():
    return pl.BlockSpec(memory_space=pltpu.SMEM)


def whole():
    return pl.BlockSpec(memory_space=pltpu.VMEM)


def anywhere():
    return pl.BlockSpec(memory_space=pl.ANY)


def params():
    return pltpu.CompilerParams(vmem_limit_bytes=VMEM_LIMIT)


def k_place(kk, r):
    return lax.rem(kk + 2 * r, 4)


def packed_shards(amplitudes, integrals, amp_mask, int_mask, eps_slab, eps_pair, eps_vir):
    v, x, r = lax.axis_index("vir"), lax.axis_index("occ"), lax.axis_index("rep")
    meta = jnp.stack([v, x, r, 2 * x + r]).astype(jnp.int32)
    swap = [(0, 1), (1, 0)]
    bf16 = jnp.bfloat16

    pairs = amp_mask.reshape(4, 4, 4, 4, 4).sum((0, 2, 4))
    pairs = jnp.where(jnp.eye(4, dtype=bool), 0, pairs)
    pieces = int_mask.reshape(4, 4, 4, 4, 16).sum((0, 3, 4))
    over = jnp.logical_or(jnp.max(pairs) > AMP_SLOTS - 1, jnp.max(pieces) > INT_SLOTS - 1)
    over = over.astype(jnp.int32).reshape(1)
    over = over + lax.ppermute(over, "frag", swap)

    int_oth = lax.ppermute(integrals, "rep", swap)
    amps = amplitudes.reshape(2, 2, 2, 2, 256, 1024)
    amp_oth = lax.ppermute(amps, "rep", swap)
    amp_oth, over = lax.optimization_barrier((amp_oth, over))

    packed_int = pl.pallas_call(
        pack_int_kernel,
        out_shape=jax.ShapeDtypeStruct((INT_SLOTS, 32, LANES), bf16),
        in_specs=[smem(), smem(), whole(), whole()],
        out_specs=whole(),
        compiler_params=params(),
        cost_estimate=NO_COST,
        name="pack_int",
    )(meta, int_mask, integrals, int_oth)

    up1 = lax.ppermute(packed_int, "vir", [(0, 1), (1, 2), (2, 3)])
    down1 = lax.ppermute(packed_int, "vir", [(1, 0), (2, 1), (3, 2)])

    packed_amp = pl.pallas_call(
        pack_amp_kernel,
        grid_spec=pltpu.PrefetchScalarGridSpec(
            num_scalar_prefetch=2,
            grid=(1,),
            in_specs=[
                pl.BlockSpec((1, 1, 2, 2, 256, 1024), lambda g, meta, mask: (meta[1], meta[2], 0, 0, 0, 0)),
                pl.BlockSpec((1, 1, 2, 2, 256, 1024), lambda g, meta, mask: (meta[1], meta[2], 0, 0, 0, 0)),
            ],
            out_specs=[pl.BlockSpec((AMP_SLOTS, TILE, LANES), lambda g, meta, mask: (0, 0, 0))] * 3,
        ),
        out_shape=[jax.ShapeDtypeStruct((AMP_SLOTS, TILE, LANES), bf16)] * 3,
        compiler_params=params(),
        cost_estimate=NO_COST,
        name="pack_amp",
    )(meta, amp_mask, amps, amp_oth)

    def across(d, packed):
        return lax.ppermute(packed, "vir", [(s, s ^ d) for s in range(4)])

    up2 = lax.ppermute(up1, "vir", [(1, 2), (2, 3)])
    down2 = lax.ppermute(down1, "vir", [(1, 0), (2, 1)])

    int_shapes = [
        jax.ShapeDtypeStruct((4, 256, 1024), bf16),
        jax.ShapeDtypeStruct((4, 1024, 256), bf16),
    ]
    int_outs = [
        pl.BlockSpec((1, 256, 1024), lambda kk, meta, mask: (k_place(kk, meta[2]), 0, 0)),
        pl.BlockSpec((1, 1024, 256), lambda kk, meta, mask: (k_place(kk, meta[2]), 0, 0)),
    ]
    def unpack(d, *operands):
        if d == 0:
            kernel, scratch = own_int_kernel, []
            specs = [
                pl.BlockSpec((1, 1, 256, 1024), lambda kk, meta, mask: (jnp.minimum(kk, 1), meta[2], 0, 0)),
                pl.BlockSpec((1, 1, 256, 1024), lambda kk, meta, mask: (jnp.maximum(kk - 2, 0), meta[2], 0, 0)),
            ]
        else:
            kernel = functools.partial(unpack_int_kernel, d)
            scratch = [pltpu.VMEM((INT_SLOTS, 32, LANES), bf16), pltpu.SMEM((1,), jnp.int32)]
            specs = [anywhere() for _ in operands]
        return pl.pallas_call(
            kernel,
            grid_spec=pltpu.PrefetchScalarGridSpec(
                num_scalar_prefetch=2, grid=(4,), in_specs=specs, out_specs=int_outs, scratch_shapes=scratch
            ),
            out_shape=int_shapes,
            compiler_params=params(),
            cost_estimate=NO_COST,
            name=f"ints_{d}",
        )(meta, int_mask, *operands)

    def local_specs(d, base):
        def at(side):
            def place(kk, meta, mask):
                k = jnp.minimum(kk + base, 1) if side == 0 else jnp.maximum(kk + base - 2, 0)
                return (0, meta[2], 0, k, 0, meta[0] ^ d)

            return place

        return [pl.BlockSpec((2, 1, 2, 1, 256, 256), at(side)) for side in range(2)]

    def combine(d, base, near, far, steps, extra_specs, extra, out_specs, out_shape, aliases, scratch):
        kernel = diagonal_kernel if d == 0 else functools.partial(combine_kernel, d, base)
        specs, operands = [], ()
        if d > 0:
            specs = [pl.BlockSpec((AMP_SLOTS, TILE, LANES), lambda kk, meta, mask: (0, 0, 0))] * 2
            operands = (near, far)
        return pl.pallas_call(
            kernel,
            grid_spec=pltpu.PrefetchScalarGridSpec(
                num_scalar_prefetch=2,
                grid=(steps,),
                in_specs=local_specs(d, base) + specs + extra_specs,
                out_specs=out_specs,
                scratch_shapes=scratch,
            ),
            out_shape=out_shape,
            input_output_aliases=aliases,
            compiler_params=params(),
            cost_estimate=NO_COST,
            name=f"combine_{d}_{base}",
        )(meta, amp_mask, amps, amp_oth, *operands, *extra)

    def combine_first(d, near, far, sofar):
        return combine(
            d,
            0,
            near,
            far,
            4,
            [] if d == 0 else [anywhere()],
            () if d == 0 else (sofar,),
            pl.BlockSpec(
                (1, 2, 2, 256, 256), lambda kk, meta, mask: (d, 0, 0, 0, k_place(kk, meta[2]))
            ),
            jax.ShapeDtypeStruct((3, 2, 2, 256, 1024), bf16),
            {} if d == 0 else {6: 0},
            [] if d == 0 else [pltpu.SMEM((1,), jnp.int32)],
        )

    def combine_half(base, near, far, *count):
        return combine(
            3,
            base,
            near,
            far,
            2,
            [smem() for _ in count],
            count,
            [pl.BlockSpec((1, 2, 2, 256, 256), lambda kk, meta, mask: (0, 0, 0, 0, kk)), smem()],
            [jax.ShapeDtypeStruct((1, 2, 2, 256, 512), bf16), jax.ShapeDtypeStruct((1,), jnp.int32)],
            {},
            [],
        )

    ready = lax.optimization_barrier
    ints = [unpack(0, integrals, int_oth)]
    first = combine_first(0, None, None, None)
    near1, near2 = across(1, packed_amp[0]), across(2, packed_amp[1])
    near1, ints[0], first = ready((near1, ints[0], first))
    far1, far2 = lax.ppermute(near1, "occ", swap), lax.ppermute(near2, "occ", swap)
    ints.append(unpack(1, down1, up1))
    ints[1], far1 = ready((ints[1], far1))
    first = combine_first(1, near1, far1, first)
    first = combine_first(2, near2, far2, first)
    up2, down2, first, packed3 = ready((up2, down2, first, packed_amp[2]))
    near3 = across(3, packed3)
    end_down = lax.ppermute(down2, "vir", [(1, 0)])
    end_up = lax.ppermute(up2, "vir", [(2, 3)])
    ints.append(unpack(2, down2, up2))
    first_oth = lax.ppermute(first, "rep", swap)

    def own_at(d, width=1024):
        return pl.BlockSpec((1, 1, 2, 256, width), lambda g, *_: (d % 3, jnp.minimum(g, 1), 0, 0, 0))

    def oth_at(d, width=1024):
        return pl.BlockSpec((1, 1, 2, 256, width), lambda g, *_: (d % 3, jnp.maximum(g - 2, 0), 0, 0, 0))

    def place(g, meta, *_):
        return (2 * (g % 2) + jnp.where(g < 2, meta[2], 1 - meta[2]), 0)

    once = pl.Buffered(1)
    part = pl.pallas_call(
        early_kernel,
        grid_spec=pltpu.PrefetchScalarGridSpec(
            num_scalar_prefetch=1,
            grid=(4,),
            in_specs=[pl.BlockSpec((4, 256, 1024), lambda g, *_: (0, 0, 0), pipeline_mode=once)] * 3
            + [pl.BlockSpec((4, 1024, 256), lambda g, *_: (0, 0, 0), pipeline_mode=once)] * 3
            + [own_at(d) for d in range(3)]
            + [oth_at(d) for d in range(3)],
            out_specs=pl.BlockSpec((512, 768), place),
            scratch_shapes=[pltpu.VMEM((3, 1024, 768), bf16)],
        ),
        out_shape=jax.ShapeDtypeStruct((2048, 768), jnp.float32),
        compiler_params=params(),
        cost_estimate=NO_COST,
        name="early",
    )(meta, *[d for d, _ in ints], *[t for _, t in ints], *[first] * 3, *[first_oth] * 3)

    near3, end_down, end_up, part = ready((near3, end_down, end_up, part))
    far3 = lax.ppermute(near3, "occ", swap)
    ints.append(unpack(3, end_down, down1, up1, end_up))
    far3, ints[3] = ready((far3, ints[3]))
    half0, count = combine_half(0, near3, far3)
    half1, _ = combine_half(2, near3, far3, count)
    halves = (half0, half1)
    halves_oth = tuple(lax.ppermute(h, "rep", swap) for h in halves)
    rows, cols = [d for d, _ in ints], [t for _, t in ints]

    row_energy = lax.dynamic_slice_in_dim(eps_vir, v * 256, 256, 0).reshape(256, 1)
    col_energy = eps_vir.reshape(1, 1024)

    def finish(ops):
        part, rows, cols, own, oth = ops
        return pl.pallas_call(
            tail_kernel,
            grid_spec=pltpu.PrefetchScalarGridSpec(
                num_scalar_prefetch=3,
                grid=(4,),
                in_specs=[
                    pl.BlockSpec((256, 1), lambda g, *_: (0, 0)),
                    pl.BlockSpec((1, 1024), lambda g, *_: (0, 0)),
                    pl.BlockSpec((512, 768), place),
                ]
                + [pl.BlockSpec((4, 256, 256), lambda g, meta, *_: (0, 0, meta[0] ^ 3), pipeline_mode=once)] * 3
                + [pl.BlockSpec((4, 256, 1024), lambda g, meta, *_: (0, 0, 0), pipeline_mode=once)]
                + [pl.BlockSpec((4, 256, 256), lambda g, meta, *_: (0, meta[0] ^ 3, 0), pipeline_mode=once)] * 3
                + [pl.BlockSpec((4, 1024, 256), lambda g, meta, *_: (0, 0, 0), pipeline_mode=once)]
                + [own_at(d) for d in range(3)]
                + [own_at(3, 512)] * 2
                + [oth_at(d) for d in range(3)]
                + [oth_at(3, 512)] * 2,
                out_specs=pl.BlockSpec((2, 256, 1, 1024), lambda g, meta, *_: (*place(g, meta), 0, 0)),
                scratch_shapes=[
                    pltpu.VMEM((1024, 1024), bf16),
                    pltpu.VMEM((3, 1024, 256), bf16),
                ],
            ),
            out_shape=jax.ShapeDtypeStruct((8, 256, 1, 1024), jnp.float32),
            compiler_params=params(),
            cost_estimate=NO_COST,
            name="tail",
        )(meta, eps_slab, eps_pair, row_energy, col_energy, part, *rows, *cols, *own, *oth)

    def dense(ops):
        return dense_shards(
            amplitudes, integrals, amp_mask, int_mask, eps_slab, eps_pair, eps_vir
        )

    return lax.cond(
        over[0] > 0,
        dense,
        finish,
        (
            part,
            rows,
            cols,
            (first, first, first, *halves),
            (first_oth, first_oth, first_oth, *halves_oth),
        ),
    )


def shards(sizes, *args):
    amplitudes, integrals, amp_mask, int_mask = args[:4]
    fits = (
        sizes == {"frag": 2, "vir": 4, "occ": 2, "rep": 2}
        and amplitudes.shape == (8, 2, 256, 1024)
        and integrals.shape == (2, 2, 256, 1024)
        and amp_mask.shape == (4, 16, 16)
        and int_mask.shape == (4, 4, 16, 16)
    )
    return packed_shards(*args) if fits else dense_shards(*args)


def solution(mesh):
    in_specs = (
        P("frag", "rep", "vir", None),
        P(("frag", "rep"), "occ", "vir", None),
        P("frag", None, None),
        P("frag", None, None, None),
        P("frag"),
        P(("frag", "occ", "rep")),
        P("frag"),
    )
    out_specs = P("frag", "vir", ("occ", "rep"), None)
    return jax.shard_map(
        functools.partial(shards, dict(mesh.shape)),
        mesh=mesh,
        in_specs=in_specs,
        out_specs=out_specs,
        check_vma=False,
    )
```

```python
import functools

import jax
import jax.numpy as jnp
from jax import lax
from jax.experimental import pallas as pl
from jax.experimental.pallas import tpu as pltpu
from jax.sharding import PartitionSpec as P

TILE = 64
LANES = 128
AMP_SLOTS = 46
INT_SLOTS = 160
VMEM_LIMIT = 60 * 1024 * 1024
NO_COST = pl.CostEstimate(flops=1024, bytes_accessed=1024, transcendentals=0)


def tile_mask(mask_tiles, row_start, row_count, tile_size):
    tile_count = mask_tiles.shape[-1]
    row_tiles = (row_start + jnp.arange(row_count, dtype=jnp.int32)) // tile_size
    select = (row_tiles[:, None] == jnp.arange(tile_count, dtype=jnp.int32)[None, :]).astype(
        jnp.float32
    )
    picked = jnp.einsum("ra,...ac->...rc", select, mask_tiles.astype(jnp.float32))
    return jnp.repeat(picked, tile_size, axis=-1)


def cycle_terms(combined, gathered):
    direct_term = jnp.einsum(
        "ikac,kjcb->iajb", combined, gathered, preferred_element_type=jnp.float32
    )
    swapped_term = jnp.einsum(
        "ikac,kjbc->iajb", combined, gathered, preferred_element_type=jnp.float32
    )
    return 2.0 * direct_term - swapped_term


def dense_shards(amplitudes, integrals, amp_mask, int_mask, eps_slab, eps_pair, eps_vir):
    row_count = amplitudes.shape[2]
    half_count = amplitudes.shape[1]
    pair_count = integrals.shape[1]
    row_start = lax.axis_index("vir") * row_count
    k_start = lax.axis_index("rep") * half_count
    j_start = lax.axis_index("occ") * pair_count
    zero_index = jnp.zeros((), jnp.int32)
    k_masks = lax.dynamic_slice_in_dim(amp_mask, k_start, half_count, 0)
    screened = (
        amplitudes.astype(jnp.float32) * tile_mask(k_masks, row_start, row_count, TILE)[None]
    ).astype(jnp.bfloat16)
    received = lax.all_to_all(screened, "vir", split_axis=3, concat_axis=2, tiled=True)
    combined = (
        2.0 * screened.astype(jnp.float32) - jnp.swapaxes(received, 2, 3).astype(jnp.float32)
    ).astype(jnp.bfloat16)
    pair_masks = lax.dynamic_slice(
        int_mask,
        (k_start, j_start, zero_index, zero_index),
        (half_count, pair_count, int_mask.shape[2], int_mask.shape[3]),
    )
    kept_local = (
        integrals.astype(jnp.float32) * tile_mask(pair_masks, row_start, row_count, TILE)
    ).astype(jnp.bfloat16)
    gathered = lax.all_gather(kept_local, "vir", axis=2, tiled=True)
    partial_cycle = cycle_terms(combined, gathered)
    cycle = lax.psum_scatter(partial_cycle, "rep", scatter_dimension=2, tiled=True)
    row_energy = lax.dynamic_slice_in_dim(eps_vir, row_start, row_count, 0)
    denominator = (
        row_energy[None, :, None, None]
        + eps_vir[None, None, None, :]
        - eps_slab[:, None, None, None]
        - eps_pair[None, None, :, None]
    )
    return cycle / denominator


def low_lanes(rows):
    return lax.broadcasted_iota(jnp.int32, (rows, LANES), 1) < TILE


def swap_halves(block):
    return pltpu.roll(block, TILE, 1)


def fill(buf, choices):
    for chosen, ref in choices:

        @pl.when(chosen)
        def _(ref=ref):
            pltpu.sync_copy(ref, buf)


def pack_int_kernel(meta, mask, own_ref, oth_ref, out_ref):
    v, r, j = meta[0], meta[2], meta[3]
    low = low_lanes(32)
    count = jnp.int32(0)
    for half in range(2):

        def body(n, count, half=half):
            kk, ap = n // 2, n % 2
            k = lax.rem(kk + 2 * half + 2 * r, 4)
            for cp in range(8):
                for a2 in range(2):
                    row = pl.multiple_of(ap * 128 + a2 * TILE, TILE)
                    if half == 0:
                        block = own_ref[kk, r, pl.ds(row, TILE), cp * LANES : (cp + 1) * LANES]
                    else:
                        block = oth_ref[kk, r, pl.ds(row, TILE), cp * LANES : (cp + 1) * LANES]
                    top, bottom = block[:32], block[32:]
                    turned_top, turned_bottom = swap_halves(top), swap_halves(bottom)
                    at_row = 4 * v + 2 * ap + a2
                    out_ref[jnp.minimum(count, INT_SLOTS - 1)] = jnp.where(low, top, turned_bottom)
                    count = count + mask[k, j, at_row, 2 * cp]
                    out_ref[jnp.minimum(count, INT_SLOTS - 1)] = jnp.where(low, turned_top, bottom)
                    count = count + mask[k, j, at_row, 2 * cp + 1]
            return count

        count = lax.fori_loop(0, 4, body, count)


def pack_amp_kernel(meta, mask, own_ref, oth_ref, *out_refs):
    v, r = meta[0], meta[2]
    low = low_lanes(TILE)
    for d in range(1, 4):
        dest = v ^ d
        count = jnp.int32(0)
        for half in range(2):
            ref = own_ref if half == 0 else oth_ref

            def body(kk, count, d=d, dest=dest, half=half, ref=ref):
                k = lax.rem(kk + 2 * half + 2 * r, 4)
                for ap in range(2):
                    for cp in range(2):
                        col = pl.multiple_of(dest * 256 + cp * LANES, LANES)
                        tiles = []
                        for a2 in range(2):
                            row = ap * 128 + a2 * TILE
                            x0 = ref[0, 0, 0, kk, row : row + TILE, pl.ds(col, LANES)]
                            x1 = ref[0, 0, 1, kk, row : row + TILE, pl.ds(col, LANES)]
                            tiles.append(
                                (jnp.where(low, x0, swap_halves(x1)), jnp.where(low, swap_halves(x0), x1))
                            )
                        for c2 in range(2):
                            for a2 in range(2):
                                out_refs[d - 1][jnp.minimum(count, AMP_SLOTS - 1)] = tiles[a2][c2]
                                count = count + mask[k, 4 * v + 2 * ap + a2, 4 * dest + 2 * cp + c2]
                return count

            count = lax.fori_loop(0, 2, body, count)


def unpack_group(buf_ref, mask, k, j, s, ap, count, d_ref, t_ref, at):
    low = low_lanes(32)
    zero = jnp.zeros((32, LANES), jnp.bfloat16)
    row = pl.multiple_of(ap * 128, 128)
    for cp in range(8):
        parts = []
        for a2 in range(2):
            at_row = 4 * s + 2 * ap + a2
            m0, m1 = mask[k, j, at_row, 2 * cp], mask[k, j, at_row, 2 * cp + 1]
            y0 = buf_ref[jnp.minimum(count, INT_SLOTS - 1)]
            count = count + m0
            y1 = buf_ref[jnp.minimum(count, INT_SLOTS - 1)]
            count = count + m1
            y0 = jnp.where(m0 > 0, y0, zero)
            y1 = jnp.where(m1 > 0, y1, zero)
            parts.append(jnp.where(low, y0, swap_halves(y1)))
            parts.append(jnp.where(low, swap_halves(y0), y1))
        block = jnp.concatenate(parts, axis=0)
        d_ref[at, pl.ds(row, 128), cp * LANES : (cp + 1) * LANES] = block
        t_ref[at, cp * LANES : (cp + 1) * LANES, pl.ds(row, 128)] = block.T
    return count


def unpack_int_kernel(d, meta, mask, *refs):
    sources, (d_ref, t_ref, buf_ref, count_ref) = refs[:-4], refs[-4:]
    v, r, j = meta[0], meta[2], meta[3]
    kk = pl.program_id(0)
    k = lax.rem(kk + 2 * r, 4)
    s = v ^ d

    @pl.when(kk == 0)
    def _():
        count_ref[0] = 0
        if d < 3:
            fill(buf_ref, [(s > v, sources[0]), (s < v, sources[1])])
        else:
            fill(buf_ref, [(v == n, source) for n, source in enumerate(sources)])

    count_ref[0] = lax.fori_loop(
        0,
        2,
        lambda ap, count: unpack_group(buf_ref, mask, k, j, s, ap, count, d_ref, t_ref, 0),
        count_ref[0],
    )


def own_int_kernel(meta, mask, own_ref, oth_ref, d_ref, t_ref):
    v, r, j = meta[0], meta[2], meta[3]
    kk = pl.program_id(0)
    k = lax.rem(kk + 2 * r, 4)
    low = low_lanes(TILE)
    zero = jnp.zeros((TILE, LANES), jnp.bfloat16)

    def body(ap, carry):
        for cp in range(8):
            parts = []
            for a2 in range(2):
                at_row = 4 * v + 2 * ap + a2
                row = pl.multiple_of(ap * 128 + a2 * TILE, TILE)
                m0, m1 = mask[k, j, at_row, 2 * cp], mask[k, j, at_row, 2 * cp + 1]
                block = jnp.where(
                    kk < 2,
                    own_ref[0, 0, pl.ds(row, TILE), cp * LANES : (cp + 1) * LANES],
                    oth_ref[0, 0, pl.ds(row, TILE), cp * LANES : (cp + 1) * LANES],
                )
                parts.append(
                    jnp.where(low, jnp.where(m0 > 0, block, zero), jnp.where(m1 > 0, block, zero))
                )
            block = jnp.concatenate(parts, axis=0)
            row = pl.multiple_of(ap * 128, 128)
            d_ref[0, pl.ds(row, 128), cp * LANES : (cp + 1) * LANES] = block
            t_ref[0, cp * LANES : (cp + 1) * LANES, pl.ds(row, 128)] = block.T
        return carry

    lax.fori_loop(0, 2, body, 0)


def lane_scale(m0, m1, value):
    lane = lax.broadcasted_iota(jnp.int32, (1, LANES), 1)
    return value * jnp.where(lane < TILE, m0, m1).astype(jnp.float32)


def combine_kernel(d, base, meta, mask, own_ref, oth_ref, near_ref, far_ref, *refs):
    if d == 3:
        out_ref, count_ref = refs[-2:]
    else:
        out_ref, count_ref = refs[1:]
    v, x, r = meta[0], meta[1], meta[2]
    kk = pl.program_id(0) + base
    k = lax.rem(kk + 2 * r, 4)
    s = v ^ d
    zero = jnp.zeros((TILE, LANES), jnp.bfloat16)

    @pl.when(pl.program_id(0) == 0)
    def _():
        count_ref[0] = 0 if base == 0 else refs[0][0]

    def body(ap, count):
        ccol = pl.multiple_of(ap * 128, 128)
        for c in range(4):
            arow = c * TILE
            slots, kept = [], []
            for a2 in range(2):
                m = mask[k, 4 * s + 2 * ap + a2, 4 * v + c]
                slots.append(jnp.minimum(count, AMP_SLOTS - 1))
                kept.append(m)
                count = count + m
            own_scale = lane_scale(
                mask[k, 4 * v + c, 4 * s + 2 * ap], mask[k, 4 * v + c, 4 * s + 2 * ap + 1], 2.0
            )
            for xx, buf in ((x, near_ref), (1 - x, far_ref)):
                stacked = jnp.concatenate(
                    [jnp.where(kept[a2] > 0, buf[slots[a2]], zero) for a2 in range(2)], axis=0
                )
                turned = stacked.T.astype(jnp.float32)
                for ii in range(2):
                    local = jnp.where(
                        kk < 2,
                        own_ref[xx, 0, ii, 0, pl.ds(arow, TILE), pl.ds(ccol, 128)],
                        oth_ref[xx, 0, ii, 0, pl.ds(arow, TILE), pl.ds(ccol, 128)],
                    ).astype(jnp.float32)
                    value = own_scale * local - turned[ii * TILE : (ii + 1) * TILE]
                    out_ref[0, xx, ii, pl.ds(arow, TILE), pl.ds(ccol, 128)] = value.astype(jnp.bfloat16)
        return count

    count_ref[0] = lax.fori_loop(0, 2, body, count_ref[0])


def diagonal_kernel(meta, mask, own_ref, oth_ref, out_ref):
    v, r = meta[0], meta[2]
    kk = pl.program_id(0)
    k = lax.rem(kk + 2 * r, 4)

    def screened(xx, ii, a0, c0):
        rows = []
        for a2 in range(2):
            start = a0 * 128 + a2 * TILE
            block = jnp.where(
                kk < 2,
                own_ref[xx, 0, ii, 0, start : start + TILE, c0 * 128 : (c0 + 1) * 128],
                oth_ref[xx, 0, ii, 0, start : start + TILE, c0 * 128 : (c0 + 1) * 128],
            ).astype(jnp.float32)
            at_row = 4 * v + 2 * a0 + a2
            rows.append(
                block
                * lane_scale(
                    mask[k, at_row, 4 * v + 2 * c0], mask[k, at_row, 4 * v + 2 * c0 + 1], 1.0
                )
            )
        return jnp.concatenate(rows, axis=0)

    for xx in range(2):
        for ii in range(2):
            for a0 in range(2):
                for c0 in range(2):
                    value = 2.0 * screened(xx, ii, a0, c0) - screened(xx, ii, c0, a0).T
                    out_ref[0, xx, ii, a0 * 128 : (a0 + 1) * 128, c0 * 128 : (c0 + 1) * 128] = (
                        value.astype(jnp.bfloat16)
                    )


def folded(direct, swapped):
    return (2.0 * direct.astype(jnp.float32) - swapped.astype(jnp.float32)).astype(jnp.bfloat16)


def early_kernel(meta, *refs):
    direct, swapped, own, oth, out_ref, w_ref = (
        refs[:3], refs[3:6], refs[6:9], refs[9:12], refs[12], refs[13]
    )
    v = meta[0]
    g = pl.program_id(0)

    @pl.when(g == 0)
    def _():
        for q in range(3):
            for p in range(3):
                col = pl.multiple_of((v ^ p) * 256, 256)
                row = pl.multiple_of((v ^ q) * 256, 256)
                for k in range(4):
                    w_ref[q, k * 256 : (k + 1) * 256, p * 256 : (p + 1) * 256] = folded(
                        direct[q][k, :, pl.ds(col, 256)], swapped[p][k, pl.ds(row, 256), :]
                    )

    def work(blocks):
        total = jnp.dot(
            blocks[0][...].reshape(512, 1024), w_ref[0], preferred_element_type=jnp.float32
        )
        for q in range(1, 3):
            total += jnp.dot(
                blocks[q][...].reshape(512, 1024), w_ref[q], preferred_element_type=jnp.float32
            )
        out_ref[...] = total

    @pl.when(g < 2)
    def _():
        work(own)

    @pl.when(g >= 2)
    def _():
        work(oth)


def late_kernel(meta, *refs):
    direct, swapped, own, oth = refs[:4], refs[4:8], refs[8:11], refs[11:14]
    row_ref, out_ref, col_ref = refs[14:]
    v = meta[0]
    g = pl.program_id(0)
    last_at = pl.multiple_of((v ^ 3) * 256, 256)

    for p in range(4):
        at = pl.multiple_of((v ^ p) * 256, 256)
        row_ref[:, p * 256 : (p + 1) * 256] = folded(
            direct[3][g, :, pl.ds(at, 256)],
            swapped[p][g] if p < 3 else swapped[3][g, pl.ds(last_at, 256), :],
        )

    @pl.when(g == 0)
    def _():
        for p in range(3):
            at = pl.multiple_of((v ^ p) * 256, 256)
            for k in range(4):
                col_ref[p, k * 256 : (k + 1) * 256, :] = folded(
                    direct[p][k], swapped[3][k, pl.ds(at, 256), :]
                )

    def work(blocks):
        total = jnp.dot(
            blocks[0][...].reshape(512, 1024), col_ref[0], preferred_element_type=jnp.float32
        )
        for q in range(1, 3):
            total += jnp.dot(
                blocks[q][...].reshape(512, 1024), col_ref[q], preferred_element_type=jnp.float32
            )
        out_ref[...] = total

    @pl.when(g < 2)
    def _():
        work(own)

    @pl.when(g >= 2)
    def _():
        work(oth)


def tail_kernel(meta, eps_slab, eps_pair, eps_rows, eps_cols, part_ref, late_ref, row_ref, *refs):
    own, oth, out_ref = refs[:2], refs[2:4], refs[4]
    v, r = meta[0], meta[2]
    g = pl.program_id(0)

    def work(blocks, i, k0):
        total = jnp.float32(0)
        for half in range(2):
            at = pl.multiple_of(256 * lax.rem(k0 + 2 * half, 4), 512)
            total += jnp.dot(
                blocks[half][...].reshape(512, 512),
                row_ref[pl.ds(at, 512), :],
                preferred_element_type=jnp.float32,
            )
        for p in range(4):
            s = v ^ p
            before = late_ref[...] if p == 3 else part_ref[:, p * 256 : (p + 1) * 256]
            value = total[:, p * 256 : (p + 1) * 256] + before
            cols = eps_cols[:, pl.ds(pl.multiple_of(s * 256, 256), 256)]
            for ii in range(2):
                energy = (eps_rows[...] + cols) - eps_slab[i + ii] - eps_pair[0]
                done = value[ii * 256 : (ii + 1) * 256] / energy
                for n in range(2):
                    at = pl.multiple_of(s * 256 + n * 128, 128)
                    out_ref[ii, :, 0, pl.ds(at, 128)] = done[:, n * 128 : (n + 1) * 128]

    @pl.when(g < 2)
    def _():
        work(own, 4 * g + 2 * r, 2 * r)

    @pl.when(g >= 2)
    def _():
        work(oth, 4 * (g - 2) + 2 * (1 - r), 2 * (1 - r))


def smem():
    return pl.BlockSpec(memory_space=pltpu.SMEM)


def whole():
    return pl.BlockSpec(memory_space=pltpu.VMEM)


def anywhere():
    return pl.BlockSpec(memory_space=pl.ANY)


def params():
    return pltpu.CompilerParams(vmem_limit_bytes=VMEM_LIMIT)


def k_place(kk, r):
    return lax.rem(kk + 2 * r, 4)


def packed_shards(amplitudes, integrals, amp_mask, int_mask, eps_slab, eps_pair, eps_vir):
    v, x, r = lax.axis_index("vir"), lax.axis_index("occ"), lax.axis_index("rep")
    meta = jnp.stack([v, x, r, 2 * x + r]).astype(jnp.int32)
    swap = [(0, 1), (1, 0)]
    bf16 = jnp.bfloat16

    pairs = amp_mask.reshape(4, 4, 4, 4, 4).sum((0, 2, 4))
    pairs = jnp.where(jnp.eye(4, dtype=bool), 0, pairs)
    pieces = int_mask.reshape(4, 4, 4, 4, 16).sum((0, 3, 4))
    over = jnp.logical_or(jnp.max(pairs) > AMP_SLOTS - 1, jnp.max(pieces) > INT_SLOTS - 1)
    over = over.astype(jnp.int32).reshape(1)

    int_oth = lax.ppermute(integrals, "rep", swap)
    amps = amplitudes.reshape(2, 2, 2, 2, 256, 1024)
    int_oth, later = lax.optimization_barrier((int_oth, amps))
    amp_oth = lax.ppermute(later, "rep", swap)

    packed_int = pl.pallas_call(
        pack_int_kernel,
        out_shape=jax.ShapeDtypeStruct((INT_SLOTS, 32, LANES), bf16),
        in_specs=[smem(), smem(), whole(), whole()],
        out_specs=whole(),
        compiler_params=params(),
        cost_estimate=NO_COST,
        name="pack_int",
    )(meta, int_mask, integrals, int_oth)

    up1 = lax.ppermute(packed_int, "vir", [(0, 1), (1, 2), (2, 3)])
    down1 = lax.ppermute(packed_int, "vir", [(1, 0), (2, 1), (3, 2)])

    packed_amp = pl.pallas_call(
        pack_amp_kernel,
        grid_spec=pltpu.PrefetchScalarGridSpec(
            num_scalar_prefetch=2,
            grid=(1,),
            in_specs=[
                pl.BlockSpec((1, 1, 2, 2, 256, 1024), lambda g, meta, mask: (meta[1], meta[2], 0, 0, 0, 0)),
                pl.BlockSpec((1, 1, 2, 2, 256, 1024), lambda g, meta, mask: (meta[1], meta[2], 0, 0, 0, 0)),
            ],
            out_specs=[pl.BlockSpec((AMP_SLOTS, TILE, LANES), lambda g, meta, mask: (0, 0, 0))] * 3,
        ),
        out_shape=[jax.ShapeDtypeStruct((AMP_SLOTS, TILE, LANES), bf16)] * 3,
        compiler_params=params(),
        cost_estimate=NO_COST,
        name="pack_amp",
    )(meta, amp_mask, amps, amp_oth)

    def across(d, packed):
        return lax.ppermute(packed, "vir", [(s, s ^ d) for s in range(4)])

    up2 = lax.ppermute(up1, "vir", [(1, 2), (2, 3)])
    down2 = lax.ppermute(down1, "vir", [(1, 0), (2, 1)])

    int_shapes = [
        jax.ShapeDtypeStruct((4, 256, 1024), bf16),
        jax.ShapeDtypeStruct((4, 1024, 256), bf16),
    ]
    int_outs = [
        pl.BlockSpec((1, 256, 1024), lambda kk, meta, mask: (k_place(kk, meta[2]), 0, 0)),
        pl.BlockSpec((1, 1024, 256), lambda kk, meta, mask: (k_place(kk, meta[2]), 0, 0)),
    ]
    def unpack(d, *operands):
        if d == 0:
            kernel, scratch = own_int_kernel, []
            specs = [
                pl.BlockSpec((1, 1, 256, 1024), lambda kk, meta, mask: (jnp.minimum(kk, 1), meta[2], 0, 0)),
                pl.BlockSpec((1, 1, 256, 1024), lambda kk, meta, mask: (jnp.maximum(kk - 2, 0), meta[2], 0, 0)),
            ]
        else:
            kernel = functools.partial(unpack_int_kernel, d)
            scratch = [pltpu.VMEM((INT_SLOTS, 32, LANES), bf16), pltpu.SMEM((1,), jnp.int32)]
            specs = [anywhere() for _ in operands]
        return pl.pallas_call(
            kernel,
            grid_spec=pltpu.PrefetchScalarGridSpec(
                num_scalar_prefetch=2, grid=(4,), in_specs=specs, out_specs=int_outs, scratch_shapes=scratch
            ),
            out_shape=int_shapes,
            compiler_params=params(),
            cost_estimate=NO_COST,
            name=f"ints_{d}",
        )(meta, int_mask, *operands)

    def local_specs(d, base):
        def at(side):
            def place(kk, meta, mask):
                k = jnp.minimum(kk + base, 1) if side == 0 else jnp.maximum(kk + base - 2, 0)
                return (0, meta[2], 0, k, 0, meta[0] ^ d)

            return place

        return [pl.BlockSpec((2, 1, 2, 1, 256, 256), at(side)) for side in range(2)]

    def combine(d, base, near, far, steps, extra_specs, extra, out_specs, out_shape, aliases, scratch):
        kernel = diagonal_kernel if d == 0 else functools.partial(combine_kernel, d, base)
        specs, operands = [], ()
        if d > 0:
            specs = [pl.BlockSpec((AMP_SLOTS, TILE, LANES), lambda kk, meta, mask: (0, 0, 0))] * 2
            operands = (near, far)
        return pl.pallas_call(
            kernel,
            grid_spec=pltpu.PrefetchScalarGridSpec(
                num_scalar_prefetch=2,
                grid=(steps,),
                in_specs=local_specs(d, base) + specs + extra_specs,
                out_specs=out_specs,
                scratch_shapes=scratch,
            ),
            out_shape=out_shape,
            input_output_aliases=aliases,
            compiler_params=params(),
            cost_estimate=NO_COST,
            name=f"combine_{d}_{base}",
        )(meta, amp_mask, amps, amp_oth, *operands, *extra)

    def combine_first(d, near, far, sofar):
        return combine(
            d,
            0,
            near,
            far,
            4,
            [] if d == 0 else [anywhere()],
            () if d == 0 else (sofar,),
            pl.BlockSpec(
                (1, 2, 2, 256, 256), lambda kk, meta, mask: (d, 0, 0, 0, k_place(kk, meta[2]))
            ),
            jax.ShapeDtypeStruct((3, 2, 2, 256, 1024), bf16),
            {} if d == 0 else {6: 0},
            [] if d == 0 else [pltpu.SMEM((1,), jnp.int32)],
        )

    def combine_half(base, near, far, *count):
        return combine(
            3,
            base,
            near,
            far,
            2,
            [smem() for _ in count],
            count,
            [pl.BlockSpec((1, 2, 2, 256, 256), lambda kk, meta, mask: (0, 0, 0, 0, kk)), smem()],
            [jax.ShapeDtypeStruct((1, 2, 2, 256, 512), bf16), jax.ShapeDtypeStruct((1,), jnp.int32)],
            {},
            [],
        )

    ready = lax.optimization_barrier
    ints = [unpack(0, integrals, int_oth)]
    first = combine_first(0, None, None, None)
    near1, near2 = across(1, packed_amp[0]), across(2, packed_amp[1])
    near1, ints[0], first = ready((near1, ints[0], first))
    near2, over = ready((near2, over))
    far1, far2 = lax.ppermute(near1, "occ", swap), lax.ppermute(near2, "occ", swap)
    ints.append(unpack(1, down1, up1))
    over = over + lax.ppermute(over, "frag", swap)
    ints[1], far1, over = ready((ints[1], far1, over))
    first = combine_first(1, near1, far1, first)
    first = combine_first(2, near2, far2, first)
    up2, down2, first, packed3 = ready((up2, down2, first, packed_amp[2]))
    near3 = across(3, packed3)
    end_down = lax.ppermute(down2, "vir", [(1, 0)])
    end_up = lax.ppermute(up2, "vir", [(2, 3)])
    ints.append(unpack(2, down2, up2))
    first_oth = lax.ppermute(first, "rep", swap)

    def own_at(d, width=1024):
        return pl.BlockSpec((1, 1, 2, 256, width), lambda g, *_: (d % 3, jnp.minimum(g, 1), 0, 0, 0))

    def oth_at(d, width=1024):
        return pl.BlockSpec((1, 1, 2, 256, width), lambda g, *_: (d % 3, jnp.maximum(g - 2, 0), 0, 0, 0))

    def place(g, meta, *_):
        return (2 * (g % 2) + jnp.where(g < 2, meta[2], 1 - meta[2]), 0)

    once = pl.Buffered(1)
    part = pl.pallas_call(
        early_kernel,
        grid_spec=pltpu.PrefetchScalarGridSpec(
            num_scalar_prefetch=1,
            grid=(4,),
            in_specs=[pl.BlockSpec((4, 256, 1024), lambda g, *_: (0, 0, 0), pipeline_mode=once)] * 3
            + [pl.BlockSpec((4, 1024, 256), lambda g, *_: (0, 0, 0), pipeline_mode=once)] * 3
            + [own_at(d) for d in range(3)]
            + [oth_at(d) for d in range(3)],
            out_specs=pl.BlockSpec((512, 768), place),
            scratch_shapes=[pltpu.VMEM((3, 1024, 768), bf16)],
        ),
        out_shape=jax.ShapeDtypeStruct((2048, 768), jnp.float32),
        compiler_params=params(),
        cost_estimate=NO_COST,
        name="early",
    )(meta, *[d for d, _ in ints], *[t for _, t in ints], *[first] * 3, *[first_oth] * 3)

    near3, part = ready((near3, part))
    far3 = lax.ppermute(near3, "occ", swap)
    ints.append(unpack(3, end_down, down1, up1, end_up))
    rows, cols = [d for d, _ in ints], [t for _, t in ints]
    last_row, late = pl.pallas_call(
        late_kernel,
        grid_spec=pltpu.PrefetchScalarGridSpec(
            num_scalar_prefetch=1,
            grid=(4,),
            in_specs=[pl.BlockSpec((4, 256, 256), lambda g, meta: (0, 0, meta[0] ^ 3), pipeline_mode=once)] * 3
            + [pl.BlockSpec((4, 256, 1024), lambda g, meta: (0, 0, 0), pipeline_mode=once)]
            + [pl.BlockSpec((4, 256, 256), lambda g, meta: (0, meta[0] ^ 3, 0), pipeline_mode=once)] * 3
            + [pl.BlockSpec((4, 1024, 256), lambda g, meta: (0, 0, 0), pipeline_mode=once)]
            + [own_at(d) for d in range(3)]
            + [oth_at(d) for d in range(3)],
            out_specs=[
                pl.BlockSpec((256, 1024), lambda g, meta: (g, 0)),
                pl.BlockSpec((512, 256), place),
            ],
            scratch_shapes=[pltpu.VMEM((3, 1024, 256), bf16)],
        ),
        out_shape=[
            jax.ShapeDtypeStruct((1024, 1024), bf16),
            jax.ShapeDtypeStruct((2048, 256), jnp.float32),
        ],
        compiler_params=params(),
        cost_estimate=NO_COST,
        name="late",
    )(meta, *rows, *cols, *[first] * 3, *[first_oth] * 3)
    far3, late = ready((far3, late))
    half0, count = combine_half(0, near3, far3)
    half1, _ = combine_half(2, near3, far3, count)
    halves = (half0, half1)
    halves_oth = tuple(lax.ppermute(h, "rep", swap) for h in halves)
    row_energy = lax.dynamic_slice_in_dim(eps_vir, v * 256, 256, 0).reshape(256, 1)
    col_energy = eps_vir.reshape(1, 1024)

    def finish(ops):
        part, late, last_row, own, oth = ops
        return pl.pallas_call(
            tail_kernel,
            grid_spec=pltpu.PrefetchScalarGridSpec(
                num_scalar_prefetch=3,
                grid=(4,),
                in_specs=[
                    pl.BlockSpec((256, 1), lambda g, *_: (0, 0)),
                    pl.BlockSpec((1, 1024), lambda g, *_: (0, 0)),
                    pl.BlockSpec((512, 768), place),
                    pl.BlockSpec((512, 256), place),
                    pl.BlockSpec((1024, 1024), lambda g, *_: (0, 0), pipeline_mode=once),
                ]
                + [own_at(3, 512)] * 2
                + [oth_at(3, 512)] * 2,
                out_specs=pl.BlockSpec((2, 256, 1, 1024), lambda g, meta, *_: (*place(g, meta), 0, 0)),
            ),
            out_shape=jax.ShapeDtypeStruct((8, 256, 1, 1024), jnp.float32),
            compiler_params=params(),
            cost_estimate=NO_COST,
            name="tail",
        )(meta, eps_slab, eps_pair, row_energy, col_energy, part, late, last_row, *own, *oth)

    def dense(ops):
        return dense_shards(
            amplitudes, integrals, amp_mask, int_mask, eps_slab, eps_pair, eps_vir
        )

    return lax.cond(
        over[0] > 0,
        dense,
        finish,
        (part, late, last_row, halves, halves_oth),
    )


def shards(sizes, *args):
    amplitudes, integrals, amp_mask, int_mask = args[:4]
    fits = (
        sizes == {"frag": 2, "vir": 4, "occ": 2, "rep": 2}
        and amplitudes.shape == (8, 2, 256, 1024)
        and integrals.shape == (2, 2, 256, 1024)
        and amp_mask.shape == (4, 16, 16)
        and int_mask.shape == (4, 4, 16, 16)
    )
    return packed_shards(*args) if fits else dense_shards(*args)


def solution(mesh):
    in_specs = (
        P("frag", "rep", "vir", None),
        P(("frag", "rep"), "occ", "vir", None),
        P("frag", None, None),
        P("frag", None, None, None),
        P("frag"),
        P(("frag", "occ", "rep")),
        P("frag"),
    )
    out_specs = P("frag", "vir", ("occ", "rep"), None)
    return jax.shard_map(
        functools.partial(shards, dict(mesh.shape)),
        mesh=mesh,
        in_specs=in_specs,
        out_specs=out_specs,
        check_vma=False,
    )
```

```python
import functools

import jax
import jax.numpy as jnp
from jax import lax
from jax.experimental import pallas as pl
from jax.experimental.pallas import tpu as pltpu
from jax.sharding import PartitionSpec as P

TILE = 64
LANES = 128
AMP_SLOTS = 46
INT_SLOTS = 160
VMEM_LIMIT = 60 * 1024 * 1024
NO_COST = pl.CostEstimate(flops=1024, bytes_accessed=1024, transcendentals=0)


def tile_mask(mask_tiles, row_start, row_count, tile_size):
    tile_count = mask_tiles.shape[-1]
    row_tiles = (row_start + jnp.arange(row_count, dtype=jnp.int32)) // tile_size
    select = (row_tiles[:, None] == jnp.arange(tile_count, dtype=jnp.int32)[None, :]).astype(
        jnp.float32
    )
    picked = jnp.einsum("ra,...ac->...rc", select, mask_tiles.astype(jnp.float32))
    return jnp.repeat(picked, tile_size, axis=-1)


def cycle_terms(combined, gathered):
    direct_term = jnp.einsum(
        "ikac,kjcb->iajb", combined, gathered, preferred_element_type=jnp.float32
    )
    swapped_term = jnp.einsum(
        "ikac,kjbc->iajb", combined, gathered, preferred_element_type=jnp.float32
    )
    return 2.0 * direct_term - swapped_term


def dense_shards(amplitudes, integrals, amp_mask, int_mask, eps_slab, eps_pair, eps_vir):
    row_count = amplitudes.shape[2]
    half_count = amplitudes.shape[1]
    pair_count = integrals.shape[1]
    row_start = lax.axis_index("vir") * row_count
    k_start = lax.axis_index("rep") * half_count
    j_start = lax.axis_index("occ") * pair_count
    zero_index = jnp.zeros((), jnp.int32)
    k_masks = lax.dynamic_slice_in_dim(amp_mask, k_start, half_count, 0)
    screened = (
        amplitudes.astype(jnp.float32) * tile_mask(k_masks, row_start, row_count, TILE)[None]
    ).astype(jnp.bfloat16)
    received = lax.all_to_all(screened, "vir", split_axis=3, concat_axis=2, tiled=True)
    combined = (
        2.0 * screened.astype(jnp.float32) - jnp.swapaxes(received, 2, 3).astype(jnp.float32)
    ).astype(jnp.bfloat16)
    pair_masks = lax.dynamic_slice(
        int_mask,
        (k_start, j_start, zero_index, zero_index),
        (half_count, pair_count, int_mask.shape[2], int_mask.shape[3]),
    )
    kept_local = (
        integrals.astype(jnp.float32) * tile_mask(pair_masks, row_start, row_count, TILE)
    ).astype(jnp.bfloat16)
    gathered = lax.all_gather(kept_local, "vir", axis=2, tiled=True)
    partial_cycle = cycle_terms(combined, gathered)
    cycle = lax.psum_scatter(partial_cycle, "rep", scatter_dimension=2, tiled=True)
    row_energy = lax.dynamic_slice_in_dim(eps_vir, row_start, row_count, 0)
    denominator = (
        row_energy[None, :, None, None]
        + eps_vir[None, None, None, :]
        - eps_slab[:, None, None, None]
        - eps_pair[None, None, :, None]
    )
    return cycle / denominator


def low_lanes(rows):
    return lax.broadcasted_iota(jnp.int32, (rows, LANES), 1) < TILE


def swap_halves(block):
    return pltpu.roll(block, TILE, 1)


def fill(buf, choices):
    for chosen, ref in choices:

        @pl.when(chosen)
        def _(ref=ref):
            pltpu.sync_copy(ref, buf)


def pack_int_kernel(meta, mask, own_ref, oth_ref, out_ref):
    v, r, j = meta[0], meta[2], meta[3]
    low = low_lanes(32)
    count = jnp.int32(0)
    for half in range(2):

        def body(n, count, half=half):
            kk, ap = n // 2, n % 2
            k = lax.rem(kk + 2 * half + 2 * r, 4)
            for cp in range(8):
                for a2 in range(2):
                    row = pl.multiple_of(ap * 128 + a2 * TILE, TILE)
                    if half == 0:
                        block = own_ref[kk, r, pl.ds(row, TILE), cp * LANES : (cp + 1) * LANES]
                    else:
                        block = oth_ref[kk, r, pl.ds(row, TILE), cp * LANES : (cp + 1) * LANES]
                    top, bottom = block[:32], block[32:]
                    turned_top, turned_bottom = swap_halves(top), swap_halves(bottom)
                    at_row = 4 * v + 2 * ap + a2
                    out_ref[jnp.minimum(count, INT_SLOTS - 1)] = jnp.where(low, top, turned_bottom)
                    count = count + mask[k, j, at_row, 2 * cp]
                    out_ref[jnp.minimum(count, INT_SLOTS - 1)] = jnp.where(low, turned_top, bottom)
                    count = count + mask[k, j, at_row, 2 * cp + 1]
            return count

        count = lax.fori_loop(0, 4, body, count)


def pack_amp_kernel(meta, mask, own_ref, oth_ref, *out_refs):
    v, r = meta[0], meta[2]
    low = low_lanes(TILE)
    for d in range(1, 4):
        dest = v ^ d
        count = jnp.int32(0)
        for half in range(2):
            ref = own_ref if half == 0 else oth_ref

            def body(kk, count, d=d, dest=dest, half=half, ref=ref):
                k = lax.rem(kk + 2 * half + 2 * r, 4)
                for ap in range(2):
                    for cp in range(2):
                        col = pl.multiple_of(dest * 256 + cp * LANES, LANES)
                        tiles = []
                        for a2 in range(2):
                            row = ap * 128 + a2 * TILE
                            x0 = ref[0, 0, 0, kk, row : row + TILE, pl.ds(col, LANES)]
                            x1 = ref[0, 0, 1, kk, row : row + TILE, pl.ds(col, LANES)]
                            tiles.append(
                                (jnp.where(low, x0, swap_halves(x1)), jnp.where(low, swap_halves(x0), x1))
                            )
                        for c2 in range(2):
                            for a2 in range(2):
                                out_refs[d - 1][jnp.minimum(count, AMP_SLOTS - 1)] = tiles[a2][c2]
                                count = count + mask[k, 4 * v + 2 * ap + a2, 4 * dest + 2 * cp + c2]
                return count

            count = lax.fori_loop(0, 2, body, count)


def unpack_group(buf_ref, mask, k, j, s, ap, count, d_ref, t_ref, at):
    low = low_lanes(32)
    zero = jnp.zeros((32, LANES), jnp.bfloat16)
    row = pl.multiple_of(ap * 128, 128)
    for cp in range(8):
        parts = []
        for a2 in range(2):
            at_row = 4 * s + 2 * ap + a2
            m0, m1 = mask[k, j, at_row, 2 * cp], mask[k, j, at_row, 2 * cp + 1]
            y0 = buf_ref[jnp.minimum(count, INT_SLOTS - 1)]
            count = count + m0
            y1 = buf_ref[jnp.minimum(count, INT_SLOTS - 1)]
            count = count + m1
            y0 = jnp.where(m0 > 0, y0, zero)
            y1 = jnp.where(m1 > 0, y1, zero)
            parts.append(jnp.where(low, y0, swap_halves(y1)))
            parts.append(jnp.where(low, swap_halves(y0), y1))
        block = jnp.concatenate(parts, axis=0)
        d_ref[at, pl.ds(row, 128), cp * LANES : (cp + 1) * LANES] = block
        t_ref[at, cp * LANES : (cp + 1) * LANES, pl.ds(row, 128)] = block.T
    return count


def unpack_int_kernel(d, meta, mask, *refs):
    sources, (d_ref, t_ref, buf_ref, count_ref) = refs[:-4], refs[-4:]
    v, r, j = meta[0], meta[2], meta[3]
    kk = pl.program_id(0)
    k = lax.rem(kk + 2 * r, 4)
    s = v ^ d

    @pl.when(kk == 0)
    def _():
        count_ref[0] = 0
        if d < 3:
            fill(buf_ref, [(s > v, sources[0]), (s < v, sources[1])])
        else:
            fill(buf_ref, [(v == n, source) for n, source in enumerate(sources)])

    count_ref[0] = lax.fori_loop(
        0,
        2,
        lambda ap, count: unpack_group(buf_ref, mask, k, j, s, ap, count, d_ref, t_ref, 0),
        count_ref[0],
    )


def own_int_kernel(meta, mask, own_ref, oth_ref, d_ref, t_ref):
    v, r, j = meta[0], meta[2], meta[3]
    kk = pl.program_id(0)
    k = lax.rem(kk + 2 * r, 4)
    low = low_lanes(TILE)
    zero = jnp.zeros((TILE, LANES), jnp.bfloat16)

    def body(ap, carry):
        for cp in range(8):
            parts = []
            for a2 in range(2):
                at_row = 4 * v + 2 * ap + a2
                row = pl.multiple_of(ap * 128 + a2 * TILE, TILE)
                m0, m1 = mask[k, j, at_row, 2 * cp], mask[k, j, at_row, 2 * cp + 1]
                block = jnp.where(
                    kk < 2,
                    own_ref[0, 0, pl.ds(row, TILE), cp * LANES : (cp + 1) * LANES],
                    oth_ref[0, 0, pl.ds(row, TILE), cp * LANES : (cp + 1) * LANES],
                )
                parts.append(
                    jnp.where(low, jnp.where(m0 > 0, block, zero), jnp.where(m1 > 0, block, zero))
                )
            block = jnp.concatenate(parts, axis=0)
            row = pl.multiple_of(ap * 128, 128)
            d_ref[0, pl.ds(row, 128), cp * LANES : (cp + 1) * LANES] = block
            t_ref[0, cp * LANES : (cp + 1) * LANES, pl.ds(row, 128)] = block.T
        return carry

    lax.fori_loop(0, 2, body, 0)


def lane_scale(m0, m1, value):
    lane = lax.broadcasted_iota(jnp.int32, (1, LANES), 1)
    return value * jnp.where(lane < TILE, m0, m1).astype(jnp.float32)


def combine_kernel(d, base, meta, mask, own_ref, oth_ref, near_ref, far_ref, *refs):
    if d == 3:
        out_ref, count_ref = refs[-2:]
    else:
        out_ref, count_ref = refs[1:]
    v, x, r = meta[0], meta[1], meta[2]
    kk = pl.program_id(0) + base
    k = lax.rem(kk + 2 * r, 4)
    s = v ^ d
    zero = jnp.zeros((TILE, LANES), jnp.bfloat16)

    @pl.when(pl.program_id(0) == 0)
    def _():
        count_ref[0] = 0 if base == 0 else refs[0][0]

    def body(ap, count):
        ccol = pl.multiple_of(ap * 128, 128)
        for c in range(4):
            arow = c * TILE
            slots, kept = [], []
            for a2 in range(2):
                m = mask[k, 4 * s + 2 * ap + a2, 4 * v + c]
                slots.append(jnp.minimum(count, AMP_SLOTS - 1))
                kept.append(m)
                count = count + m
            own_scale = lane_scale(
                mask[k, 4 * v + c, 4 * s + 2 * ap], mask[k, 4 * v + c, 4 * s + 2 * ap + 1], 2.0
            )
            for xx, buf in ((x, near_ref), (1 - x, far_ref)):
                stacked = jnp.concatenate(
                    [jnp.where(kept[a2] > 0, buf[slots[a2]], zero) for a2 in range(2)], axis=0
                )
                turned = stacked.T.astype(jnp.float32)
                for ii in range(2):
                    local = jnp.where(
                        kk < 2,
                        own_ref[xx, 0, ii, 0, pl.ds(arow, TILE), pl.ds(ccol, 128)],
                        oth_ref[xx, 0, ii, 0, pl.ds(arow, TILE), pl.ds(ccol, 128)],
                    ).astype(jnp.float32)
                    value = own_scale * local - turned[ii * TILE : (ii + 1) * TILE]
                    out_ref[0, xx, ii, pl.ds(arow, TILE), pl.ds(ccol, 128)] = value.astype(jnp.bfloat16)
        return count

    count_ref[0] = lax.fori_loop(0, 2, body, count_ref[0])


def diagonal_kernel(meta, mask, own_ref, oth_ref, out_ref):
    v, r = meta[0], meta[2]
    kk = pl.program_id(0)
    k = lax.rem(kk + 2 * r, 4)

    def screened(xx, ii, a0, c0):
        rows = []
        for a2 in range(2):
            start = a0 * 128 + a2 * TILE
            block = jnp.where(
                kk < 2,
                own_ref[xx, 0, ii, 0, start : start + TILE, c0 * 128 : (c0 + 1) * 128],
                oth_ref[xx, 0, ii, 0, start : start + TILE, c0 * 128 : (c0 + 1) * 128],
            ).astype(jnp.float32)
            at_row = 4 * v + 2 * a0 + a2
            rows.append(
                block
                * lane_scale(
                    mask[k, at_row, 4 * v + 2 * c0], mask[k, at_row, 4 * v + 2 * c0 + 1], 1.0
                )
            )
        return jnp.concatenate(rows, axis=0)

    for xx in range(2):
        for ii in range(2):
            for a0 in range(2):
                for c0 in range(2):
                    value = 2.0 * screened(xx, ii, a0, c0) - screened(xx, ii, c0, a0).T
                    out_ref[0, xx, ii, a0 * 128 : (a0 + 1) * 128, c0 * 128 : (c0 + 1) * 128] = (
                        value.astype(jnp.bfloat16)
                    )


def folded(direct, swapped):
    return (2.0 * direct.astype(jnp.float32) - swapped.astype(jnp.float32)).astype(jnp.bfloat16)


def early_kernel(meta, *refs):
    direct, swapped, own, oth, out_ref, w_ref = (
        refs[:3], refs[3:6], refs[6:9], refs[9:12], refs[12], refs[13]
    )
    v = meta[0]
    g = pl.program_id(0)

    @pl.when(g == 0)
    def _():
        for q in range(3):
            for p in range(3):
                col = pl.multiple_of((v ^ p) * 256, 256)
                row = pl.multiple_of((v ^ q) * 256, 256)
                for k in range(4):
                    w_ref[q, k * 256 : (k + 1) * 256, p * 256 : (p + 1) * 256] = folded(
                        direct[q][k, :, pl.ds(col, 256)], swapped[p][k, pl.ds(row, 256), :]
                    )

    def work(blocks):
        total = jnp.dot(
            blocks[0][...].reshape(512, 1024), w_ref[0], preferred_element_type=jnp.float32
        )
        for q in range(1, 3):
            total += jnp.dot(
                blocks[q][...].reshape(512, 1024), w_ref[q], preferred_element_type=jnp.float32
            )
        out_ref[...] = total

    @pl.when(g < 2)
    def _():
        work(own)

    @pl.when(g >= 2)
    def _():
        work(oth)


def late_kernel(meta, *refs):
    direct, swapped, own, oth = refs[:4], refs[4:8], refs[8:11], refs[11:14]
    row_ref, out_ref, col_ref = refs[14:]
    v = meta[0]
    g = pl.program_id(0)
    last_at = pl.multiple_of((v ^ 3) * 256, 256)

    for p in range(4):
        at = pl.multiple_of((v ^ p) * 256, 256)
        row_ref[:, p * 256 : (p + 1) * 256] = folded(
            direct[3][g, :, pl.ds(at, 256)],
            swapped[p][g] if p < 3 else swapped[3][g, pl.ds(last_at, 256), :],
        )

    @pl.when(g == 0)
    def _():
        for p in range(3):
            at = pl.multiple_of((v ^ p) * 256, 256)
            for k in range(4):
                col_ref[p, k * 256 : (k + 1) * 256, :] = folded(
                    direct[p][k], swapped[3][k, pl.ds(at, 256), :]
                )

    def work(blocks):
        total = jnp.dot(
            blocks[0][...].reshape(512, 1024), col_ref[0], preferred_element_type=jnp.float32
        )
        for q in range(1, 3):
            total += jnp.dot(
                blocks[q][...].reshape(512, 1024), col_ref[q], preferred_element_type=jnp.float32
            )
        out_ref[...] = total

    @pl.when(g < 2)
    def _():
        work(own)

    @pl.when(g >= 2)
    def _():
        work(oth)


def tail_kernel(meta, eps_slab, eps_pair, eps_rows, eps_cols, part_ref, late_ref, row_ref, *refs):
    own, oth, out_ref = refs[:2], refs[2:4], refs[4]
    v, r = meta[0], meta[2]
    g = pl.program_id(0)

    def work(blocks, i, k0):
        total = jnp.float32(0)
        for half in range(2):
            at = pl.multiple_of(256 * lax.rem(k0 + 2 * half, 4), 512)
            total += jnp.dot(
                blocks[half][...].reshape(512, 512),
                row_ref[pl.ds(at, 512), :],
                preferred_element_type=jnp.float32,
            )
        for p in range(4):
            s = v ^ p
            before = late_ref[...] if p == 3 else part_ref[:, p * 256 : (p + 1) * 256]
            value = total[:, p * 256 : (p + 1) * 256] + before
            cols = eps_cols[:, pl.ds(pl.multiple_of(s * 256, 256), 256)]
            for ii in range(2):
                energy = (eps_rows[...] + cols) - eps_slab[i + ii] - eps_pair[0]
                done = value[ii * 256 : (ii + 1) * 256] / energy
                for n in range(2):
                    at = pl.multiple_of(s * 256 + n * 128, 128)
                    out_ref[ii, :, 0, pl.ds(at, 128)] = done[:, n * 128 : (n + 1) * 128]

    @pl.when(g < 2)
    def _():
        work(own, 4 * g + 2 * r, 2 * r)

    @pl.when(g >= 2)
    def _():
        work(oth, 4 * (g - 2) + 2 * (1 - r), 2 * (1 - r))


def smem():
    return pl.BlockSpec(memory_space=pltpu.SMEM)


def whole():
    return pl.BlockSpec(memory_space=pltpu.VMEM)


def anywhere():
    return pl.BlockSpec(memory_space=pl.ANY)


def params():
    return pltpu.CompilerParams(vmem_limit_bytes=VMEM_LIMIT)


def as_is(array):
    def kernel(from_ref, to_ref):
        pltpu.sync_copy(from_ref, to_ref)

    return pl.pallas_call(
        kernel,
        out_shape=jax.ShapeDtypeStruct(array.shape, array.dtype),
        in_specs=[anywhere()],
        out_specs=anywhere(),
        name="as_is",
    )(array)


def k_place(kk, r):
    return lax.rem(kk + 2 * r, 4)


def packed_shards(amplitudes, integrals, amp_mask, int_mask, eps_slab, eps_pair, eps_vir):
    v, x, r = lax.axis_index("vir"), lax.axis_index("occ"), lax.axis_index("rep")
    meta = jnp.stack([v, x, r, 2 * x + r]).astype(jnp.int32)
    swap = [(0, 1), (1, 0)]
    bf16 = jnp.bfloat16

    pairs = amp_mask.reshape(4, 4, 4, 4, 4).sum((0, 2, 4))
    pairs = jnp.where(jnp.eye(4, dtype=bool), 0, pairs)
    pieces = int_mask.reshape(4, 4, 4, 4, 16).sum((0, 3, 4))
    over = jnp.logical_or(jnp.max(pairs) > AMP_SLOTS - 1, jnp.max(pieces) > INT_SLOTS - 1)
    over = over.astype(jnp.int32).reshape(1)

    int_oth = lax.ppermute(integrals, "rep", swap)
    amps = amplitudes.reshape(2, 2, 2, 2, 256, 1024)
    int_oth, later = lax.optimization_barrier((int_oth, amps))
    amp_oth = lax.ppermute(later, "rep", swap)

    packed_int = pl.pallas_call(
        pack_int_kernel,
        out_shape=jax.ShapeDtypeStruct((INT_SLOTS, 32, LANES), bf16),
        in_specs=[smem(), smem(), whole(), whole()],
        out_specs=whole(),
        compiler_params=params(),
        cost_estimate=NO_COST,
        name="pack_int",
    )(meta, int_mask, integrals, int_oth)

    up1 = lax.ppermute(packed_int, "vir", [(0, 1), (1, 2), (2, 3)])
    down1 = lax.ppermute(packed_int, "vir", [(1, 0), (2, 1), (3, 2)])

    packed_amp = pl.pallas_call(
        pack_amp_kernel,
        grid_spec=pltpu.PrefetchScalarGridSpec(
            num_scalar_prefetch=2,
            grid=(1,),
            in_specs=[
                pl.BlockSpec((1, 1, 2, 2, 256, 1024), lambda g, meta, mask: (meta[1], meta[2], 0, 0, 0, 0)),
                pl.BlockSpec((1, 1, 2, 2, 256, 1024), lambda g, meta, mask: (meta[1], meta[2], 0, 0, 0, 0)),
            ],
            out_specs=[pl.BlockSpec((AMP_SLOTS, TILE, LANES), lambda g, meta, mask: (0, 0, 0))] * 3,
        ),
        out_shape=[jax.ShapeDtypeStruct((AMP_SLOTS, TILE, LANES), bf16)] * 3,
        compiler_params=params(),
        cost_estimate=NO_COST,
        name="pack_amp",
    )(meta, amp_mask, amps, amp_oth)

    def across(d, packed):
        return lax.ppermute(packed, "vir", [(s, s ^ d) for s in range(4)])

    packed3, over = lax.optimization_barrier((packed_amp[2], over))
    over = over + lax.ppermute(over, "frag", swap)
    up1, down1, over = lax.optimization_barrier((up1, down1, over))
    up2 = lax.ppermute(up1, "vir", [(1, 2), (2, 3)])
    down2 = lax.ppermute(down1, "vir", [(1, 0), (2, 1)])

    int_shapes = [
        jax.ShapeDtypeStruct((4, 256, 1024), bf16),
        jax.ShapeDtypeStruct((4, 1024, 256), bf16),
    ]
    int_outs = [
        pl.BlockSpec((1, 256, 1024), lambda kk, meta, mask: (k_place(kk, meta[2]), 0, 0)),
        pl.BlockSpec((1, 1024, 256), lambda kk, meta, mask: (k_place(kk, meta[2]), 0, 0)),
    ]
    def unpack(d, *operands):
        if d == 0:
            kernel, scratch = own_int_kernel, []
            specs = [
                pl.BlockSpec((1, 1, 256, 1024), lambda kk, meta, mask: (jnp.minimum(kk, 1), meta[2], 0, 0)),
                pl.BlockSpec((1, 1, 256, 1024), lambda kk, meta, mask: (jnp.maximum(kk - 2, 0), meta[2], 0, 0)),
            ]
        else:
            kernel = functools.partial(unpack_int_kernel, d)
            scratch = [pltpu.VMEM((INT_SLOTS, 32, LANES), bf16), pltpu.SMEM((1,), jnp.int32)]
            specs = [anywhere() for _ in operands]
        return pl.pallas_call(
            kernel,
            grid_spec=pltpu.PrefetchScalarGridSpec(
                num_scalar_prefetch=2, grid=(4,), in_specs=specs, out_specs=int_outs, scratch_shapes=scratch
            ),
            out_shape=int_shapes,
            compiler_params=params(),
            cost_estimate=NO_COST,
            name=f"ints_{d}",
        )(meta, int_mask, *operands)

    def local_specs(d, base):
        def at(side):
            def place(kk, meta, mask):
                k = jnp.minimum(kk + base, 1) if side == 0 else jnp.maximum(kk + base - 2, 0)
                return (0, meta[2], 0, k, 0, meta[0] ^ d)

            return place

        return [pl.BlockSpec((2, 1, 2, 1, 256, 256), at(side)) for side in range(2)]

    def combine(d, base, near, far, steps, extra_specs, extra, out_specs, out_shape, aliases, scratch):
        kernel = diagonal_kernel if d == 0 else functools.partial(combine_kernel, d, base)
        specs, operands = [], ()
        if d > 0:
            specs = [pl.BlockSpec((AMP_SLOTS, TILE, LANES), lambda kk, meta, mask: (0, 0, 0))] * 2
            operands = (near, far)
        return pl.pallas_call(
            kernel,
            grid_spec=pltpu.PrefetchScalarGridSpec(
                num_scalar_prefetch=2,
                grid=(steps,),
                in_specs=local_specs(d, base) + specs + extra_specs,
                out_specs=out_specs,
                scratch_shapes=scratch,
            ),
            out_shape=out_shape,
            input_output_aliases=aliases,
            compiler_params=params(),
            cost_estimate=NO_COST,
            name=f"combine_{d}_{base}",
        )(meta, amp_mask, amps, amp_oth, *operands, *extra)

    def combine_first(d, near, far, sofar):
        return combine(
            d,
            0,
            near,
            far,
            4,
            [] if d == 0 else [anywhere()],
            () if d == 0 else (sofar,),
            pl.BlockSpec(
                (1, 2, 2, 256, 256), lambda kk, meta, mask: (d, 0, 0, 0, k_place(kk, meta[2]))
            ),
            jax.ShapeDtypeStruct((3, 2, 2, 256, 1024), bf16),
            {} if d == 0 else {6: 0},
            [] if d == 0 else [pltpu.SMEM((1,), jnp.int32)],
        )

    def combine_half(base, near, far, *count):
        return combine(
            3,
            base,
            near,
            far,
            2,
            [smem() for _ in count],
            count,
            [pl.BlockSpec((1, 2, 2, 256, 256), lambda kk, meta, mask: (0, 0, 0, 0, kk)), smem()],
            [jax.ShapeDtypeStruct((1, 2, 2, 256, 512), bf16), jax.ShapeDtypeStruct((1,), jnp.int32)],
            {},
            [],
        )

    ready = lax.optimization_barrier
    ints = [unpack(0, integrals, int_oth)]
    first = combine_first(0, None, None, None)
    near1, near2 = across(1, packed_amp[0]), across(2, packed_amp[1])
    near1, ints[0], first = ready((near1, ints[0], first))
    far1, far2 = lax.ppermute(near1, "occ", swap), lax.ppermute(near2, "occ", swap)
    ints.append(unpack(1, down1, up1))
    ints[1], far1 = ready((ints[1], far1))
    first = combine_first(1, near1, far1, first)
    first = combine_first(2, near2, far2, first)
    near3 = across(3, packed3)
    up2, down2, near3, first = ready((up2, down2, near3, first))
    end_down = lax.ppermute(down2, "vir", [(1, 0)])
    end_up = lax.ppermute(up2, "vir", [(2, 3)])
    ints.append(unpack(2, down2, up2))
    first_oth = lax.ppermute(first, "rep", swap)

    def own_at(d, width=1024):
        return pl.BlockSpec((1, 1, 2, 256, width), lambda g, *_: (d % 3, jnp.minimum(g, 1), 0, 0, 0))

    def oth_at(d, width=1024):
        return pl.BlockSpec((1, 1, 2, 256, width), lambda g, *_: (d % 3, jnp.maximum(g - 2, 0), 0, 0, 0))

    def place(g, meta, *_):
        return (2 * (g % 2) + jnp.where(g < 2, meta[2], 1 - meta[2]), 0)

    once = pl.Buffered(1)
    part = pl.pallas_call(
        early_kernel,
        grid_spec=pltpu.PrefetchScalarGridSpec(
            num_scalar_prefetch=1,
            grid=(4,),
            in_specs=[pl.BlockSpec((4, 256, 1024), lambda g, *_: (0, 0, 0), pipeline_mode=once)] * 3
            + [pl.BlockSpec((4, 1024, 256), lambda g, *_: (0, 0, 0), pipeline_mode=once)] * 3
            + [own_at(d) for d in range(3)]
            + [oth_at(d) for d in range(3)],
            out_specs=pl.BlockSpec((512, 768), place),
            scratch_shapes=[pltpu.VMEM((3, 1024, 768), bf16)],
        ),
        out_shape=jax.ShapeDtypeStruct((2048, 768), jnp.float32),
        compiler_params=params(),
        cost_estimate=NO_COST,
        name="early",
    )(meta, *[d for d, _ in ints], *[t for _, t in ints], *[first] * 3, *[first_oth] * 3)

    far3 = lax.ppermute(near3, "occ", swap)
    far3, part = ready((far3, part))
    half0, count = combine_half(0, near3, far3)
    half1, _ = combine_half(2, near3, far3, count)
    halves = (half0, half1)
    halves_oth = tuple(lax.ppermute(h, "rep", swap) for h in halves)
    end_down, end_up, half1 = ready((end_down, end_up, half1))
    ints.append(unpack(3, end_down, down1, up1, end_up))
    rows, cols = [d for d, _ in ints], [t for _, t in ints]
    last_row, late = pl.pallas_call(
        late_kernel,
        grid_spec=pltpu.PrefetchScalarGridSpec(
            num_scalar_prefetch=1,
            grid=(4,),
            in_specs=[pl.BlockSpec((4, 256, 256), lambda g, meta: (0, 0, meta[0] ^ 3), pipeline_mode=once)] * 3
            + [pl.BlockSpec((4, 256, 1024), lambda g, meta: (0, 0, 0), pipeline_mode=once)]
            + [pl.BlockSpec((4, 256, 256), lambda g, meta: (0, meta[0] ^ 3, 0), pipeline_mode=once)] * 3
            + [pl.BlockSpec((4, 1024, 256), lambda g, meta: (0, 0, 0), pipeline_mode=once)]
            + [own_at(d) for d in range(3)]
            + [oth_at(d) for d in range(3)],
            out_specs=[
                pl.BlockSpec((256, 1024), lambda g, meta: (g, 0)),
                pl.BlockSpec((512, 256), place),
            ],
            scratch_shapes=[pltpu.VMEM((3, 1024, 256), bf16)],
        ),
        out_shape=[
            jax.ShapeDtypeStruct((1024, 1024), bf16),
            jax.ShapeDtypeStruct((2048, 256), jnp.float32),
        ],
        compiler_params=params(),
        cost_estimate=NO_COST,
        name="late",
    )(meta, *rows, *cols, *[first] * 3, *[first_oth] * 3)
    row_energy = lax.dynamic_slice_in_dim(eps_vir, v * 256, 256, 0).reshape(256, 1)
    col_energy = eps_vir.reshape(1, 1024)

    def finish(ops):
        part, late, last_row, own, oth = ops
        return pl.pallas_call(
            tail_kernel,
            grid_spec=pltpu.PrefetchScalarGridSpec(
                num_scalar_prefetch=3,
                grid=(4,),
                in_specs=[
                    pl.BlockSpec((256, 1), lambda g, *_: (0, 0)),
                    pl.BlockSpec((1, 1024), lambda g, *_: (0, 0)),
                    pl.BlockSpec((512, 768), place),
                    pl.BlockSpec((512, 256), place),
                    pl.BlockSpec((1024, 1024), lambda g, *_: (0, 0), pipeline_mode=once),
                ]
                + [own_at(3, 512)] * 2
                + [oth_at(3, 512)] * 2,
                out_specs=pl.BlockSpec((2, 256, 1, 1024), lambda g, meta, *_: (*place(g, meta), 0, 0)),
            ),
            out_shape=jax.ShapeDtypeStruct((8, 256, 1, 1024), jnp.float32),
            compiler_params=params(),
            cost_estimate=NO_COST,
            name="tail",
        )(meta, eps_slab, eps_pair, row_energy, col_energy, part, late, last_row, *own, *oth)

    def dense(state):
        out = dense_shards(
            as_is(amplitudes), as_is(integrals), amp_mask, int_mask, eps_slab, eps_pair, eps_vir
        )
        return as_is(out), jnp.zeros((), jnp.int32)

    out = finish((part, late, last_row, halves, halves_oth))
    return lax.while_loop(lambda state: state[1] > 0, dense, (out, over[0]))[0]


def shards(sizes, *args):
    amplitudes, integrals, amp_mask, int_mask = args[:4]
    fits = (
        sizes == {"frag": 2, "vir": 4, "occ": 2, "rep": 2}
        and amplitudes.shape == (8, 2, 256, 1024)
        and integrals.shape == (2, 2, 256, 1024)
        and amp_mask.shape == (4, 16, 16)
        and int_mask.shape == (4, 4, 16, 16)
    )
    return packed_shards(*args) if fits else dense_shards(*args)


def solution(mesh):
    in_specs = (
        P("frag", "rep", "vir", None),
        P(("frag", "rep"), "occ", "vir", None),
        P("frag", None, None),
        P("frag", None, None, None),
        P("frag"),
        P(("frag", "occ", "rep")),
        P("frag"),
    )
    out_specs = P("frag", "vir", ("occ", "rep"), None)
    return jax.shard_map(
        functools.partial(shards, dict(mesh.shape)),
        mesh=mesh,
        in_specs=in_specs,
        out_specs=out_specs,
        check_vma=False,
    )
```

```python
import functools

import jax
import jax.numpy as jnp
from jax import lax
from jax.experimental import pallas as pl
from jax.experimental.pallas import tpu as pltpu
from jax.sharding import PartitionSpec as P

TILE = 64
LANES = 128
AMP_SLOTS = 46
INT_SLOTS = 160
VMEM_LIMIT = 60 * 1024 * 1024
NO_COST = pl.CostEstimate(flops=1024, bytes_accessed=1024, transcendentals=0)


def tile_mask(mask_tiles, row_start, row_count, tile_size):
    tile_count = mask_tiles.shape[-1]
    row_tiles = (row_start + jnp.arange(row_count, dtype=jnp.int32)) // tile_size
    select = (row_tiles[:, None] == jnp.arange(tile_count, dtype=jnp.int32)[None, :]).astype(
        jnp.float32
    )
    picked = jnp.einsum("ra,...ac->...rc", select, mask_tiles.astype(jnp.float32))
    return jnp.repeat(picked, tile_size, axis=-1)


def cycle_terms(combined, gathered):
    direct_term = jnp.einsum(
        "ikac,kjcb->iajb", combined, gathered, preferred_element_type=jnp.float32
    )
    swapped_term = jnp.einsum(
        "ikac,kjbc->iajb", combined, gathered, preferred_element_type=jnp.float32
    )
    return 2.0 * direct_term - swapped_term


def dense_shards(amplitudes, integrals, amp_mask, int_mask, eps_slab, eps_pair, eps_vir):
    row_count = amplitudes.shape[2]
    half_count = amplitudes.shape[1]
    pair_count = integrals.shape[1]
    row_start = lax.axis_index("vir") * row_count
    k_start = lax.axis_index("rep") * half_count
    j_start = lax.axis_index("occ") * pair_count
    zero_index = jnp.zeros((), jnp.int32)
    k_masks = lax.dynamic_slice_in_dim(amp_mask, k_start, half_count, 0)
    screened = (
        amplitudes.astype(jnp.float32) * tile_mask(k_masks, row_start, row_count, TILE)[None]
    ).astype(jnp.bfloat16)
    received = lax.all_to_all(screened, "vir", split_axis=3, concat_axis=2, tiled=True)
    combined = (
        2.0 * screened.astype(jnp.float32) - jnp.swapaxes(received, 2, 3).astype(jnp.float32)
    ).astype(jnp.bfloat16)
    pair_masks = lax.dynamic_slice(
        int_mask,
        (k_start, j_start, zero_index, zero_index),
        (half_count, pair_count, int_mask.shape[2], int_mask.shape[3]),
    )
    kept_local = (
        integrals.astype(jnp.float32) * tile_mask(pair_masks, row_start, row_count, TILE)
    ).astype(jnp.bfloat16)
    gathered = lax.all_gather(kept_local, "vir", axis=2, tiled=True)
    partial_cycle = cycle_terms(combined, gathered)
    cycle = lax.psum_scatter(partial_cycle, "rep", scatter_dimension=2, tiled=True)
    row_energy = lax.dynamic_slice_in_dim(eps_vir, row_start, row_count, 0)
    denominator = (
        row_energy[None, :, None, None]
        + eps_vir[None, None, None, :]
        - eps_slab[:, None, None, None]
        - eps_pair[None, None, :, None]
    )
    return cycle / denominator


def low_lanes(rows):
    return lax.broadcasted_iota(jnp.int32, (rows, LANES), 1) < TILE


def swap_halves(block):
    return pltpu.roll(block, TILE, 1)


def fill(buf, choices):
    for chosen, ref in choices:

        @pl.when(chosen)
        def _(ref=ref):
            pltpu.sync_copy(ref, buf)


def pack_int_kernel(meta, mask, own_ref, oth_ref, out_ref):
    v, r, j = meta[0], meta[2], meta[3]
    low = low_lanes(32)
    count = jnp.int32(0)
    for half in range(2):

        def body(n, count, half=half):
            kk, ap = n // 2, n % 2
            k = lax.rem(kk + 2 * half + 2 * r, 4)
            for cp in range(8):
                for a2 in range(2):
                    row = pl.multiple_of(ap * 128 + a2 * TILE, TILE)
                    if half == 0:
                        block = own_ref[kk, r, pl.ds(row, TILE), cp * LANES : (cp + 1) * LANES]
                    else:
                        block = oth_ref[kk, r, pl.ds(row, TILE), cp * LANES : (cp + 1) * LANES]
                    top, bottom = block[:32], block[32:]
                    turned_top, turned_bottom = swap_halves(top), swap_halves(bottom)
                    at_row = 4 * v + 2 * ap + a2
                    out_ref[jnp.minimum(count, INT_SLOTS - 1)] = jnp.where(low, top, turned_bottom)
                    count = count + mask[k, j, at_row, 2 * cp]
                    out_ref[jnp.minimum(count, INT_SLOTS - 1)] = jnp.where(low, turned_top, bottom)
                    count = count + mask[k, j, at_row, 2 * cp + 1]
            return count

        count = lax.fori_loop(0, 4, body, count)


def pack_amp_kernel(meta, mask, own_ref, oth_ref, *out_refs):
    v, r = meta[0], meta[2]
    low = low_lanes(TILE)
    for d in range(1, 4):
        dest = v ^ d
        count = jnp.int32(0)
        for half in range(2):
            ref = own_ref if half == 0 else oth_ref

            def body(kk, count, d=d, dest=dest, half=half, ref=ref):
                k = lax.rem(kk + 2 * half + 2 * r, 4)
                for ap in range(2):
                    for cp in range(2):
                        col = pl.multiple_of(dest * 256 + cp * LANES, LANES)
                        tiles = []
                        for a2 in range(2):
                            row = ap * 128 + a2 * TILE
                            x0 = ref[0, 0, 0, kk, row : row + TILE, pl.ds(col, LANES)]
                            x1 = ref[0, 0, 1, kk, row : row + TILE, pl.ds(col, LANES)]
                            tiles.append(
                                (jnp.where(low, x0, swap_halves(x1)), jnp.where(low, swap_halves(x0), x1))
                            )
                        for c2 in range(2):
                            for a2 in range(2):
                                out_refs[d - 1][jnp.minimum(count, AMP_SLOTS - 1)] = tiles[a2][c2]
                                count = count + mask[k, 4 * v + 2 * ap + a2, 4 * dest + 2 * cp + c2]
                return count

            count = lax.fori_loop(0, 2, body, count)


def unpack_group(buf_ref, mask, k, j, s, ap, count, d_ref, t_ref, at):
    low = low_lanes(32)
    zero = jnp.zeros((32, LANES), jnp.bfloat16)
    row = pl.multiple_of(ap * 128, 128)
    for cp in range(8):
        parts = []
        for a2 in range(2):
            at_row = 4 * s + 2 * ap + a2
            m0, m1 = mask[k, j, at_row, 2 * cp], mask[k, j, at_row, 2 * cp + 1]
            y0 = buf_ref[jnp.minimum(count, INT_SLOTS - 1)]
            count = count + m0
            y1 = buf_ref[jnp.minimum(count, INT_SLOTS - 1)]
            count = count + m1
            y0 = jnp.where(m0 > 0, y0, zero)
            y1 = jnp.where(m1 > 0, y1, zero)
            parts.append(jnp.where(low, y0, swap_halves(y1)))
            parts.append(jnp.where(low, swap_halves(y0), y1))
        block = jnp.concatenate(parts, axis=0)
        d_ref[at, pl.ds(row, 128), cp * LANES : (cp + 1) * LANES] = block
        t_ref[at, cp * LANES : (cp + 1) * LANES, pl.ds(row, 128)] = block.T
    return count


def unpack_int_kernel(d, meta, mask, *refs):
    sources, (d_ref, t_ref, buf_ref, count_ref) = refs[:-4], refs[-4:]
    v, r, j = meta[0], meta[2], meta[3]
    kk = pl.program_id(0)
    k = lax.rem(kk + 2 * r, 4)
    s = v ^ d

    @pl.when(kk == 0)
    def _():
        count_ref[0] = 0
        if d < 3:
            fill(buf_ref, [(s > v, sources[0]), (s < v, sources[1])])
        else:
            fill(buf_ref, [(v == n, source) for n, source in enumerate(sources)])

    count_ref[0] = lax.fori_loop(
        0,
        2,
        lambda ap, count: unpack_group(buf_ref, mask, k, j, s, ap, count, d_ref, t_ref, 0),
        count_ref[0],
    )


def own_int_kernel(meta, mask, own_ref, oth_ref, d_ref, t_ref):
    v, r, j = meta[0], meta[2], meta[3]
    kk = pl.program_id(0)
    k = lax.rem(kk + 2 * r, 4)
    low = low_lanes(TILE)
    zero = jnp.zeros((TILE, LANES), jnp.bfloat16)

    def body(ap, carry):
        for cp in range(8):
            parts = []
            for a2 in range(2):
                at_row = 4 * v + 2 * ap + a2
                row = pl.multiple_of(ap * 128 + a2 * TILE, TILE)
                m0, m1 = mask[k, j, at_row, 2 * cp], mask[k, j, at_row, 2 * cp + 1]
                block = jnp.where(
                    kk < 2,
                    own_ref[0, 0, pl.ds(row, TILE), cp * LANES : (cp + 1) * LANES],
                    oth_ref[0, 0, pl.ds(row, TILE), cp * LANES : (cp + 1) * LANES],
                )
                parts.append(
                    jnp.where(low, jnp.where(m0 > 0, block, zero), jnp.where(m1 > 0, block, zero))
                )
            block = jnp.concatenate(parts, axis=0)
            row = pl.multiple_of(ap * 128, 128)
            d_ref[0, pl.ds(row, 128), cp * LANES : (cp + 1) * LANES] = block
            t_ref[0, cp * LANES : (cp + 1) * LANES, pl.ds(row, 128)] = block.T
        return carry

    lax.fori_loop(0, 2, body, 0)


def lane_scale(m0, m1, value):
    lane = lax.broadcasted_iota(jnp.int32, (1, LANES), 1)
    return value * jnp.where(lane < TILE, m0, m1).astype(jnp.float32)


def combine_kernel(d, base, meta, mask, own_ref, oth_ref, near_ref, far_ref, *refs):
    if d == 3:
        out_ref, count_ref = refs[-2:]
    else:
        out_ref, count_ref = refs[1:]
    v, x, r = meta[0], meta[1], meta[2]
    kk = pl.program_id(0) + base
    k = lax.rem(kk + 2 * r, 4)
    s = v ^ d
    zero = jnp.zeros((TILE, LANES), jnp.bfloat16)

    @pl.when(pl.program_id(0) == 0)
    def _():
        count_ref[0] = 0 if base == 0 else refs[0][0]

    def body(ap, count):
        ccol = pl.multiple_of(ap * 128, 128)
        for c in range(4):
            arow = c * TILE
            slots, kept = [], []
            for a2 in range(2):
                m = mask[k, 4 * s + 2 * ap + a2, 4 * v + c]
                slots.append(jnp.minimum(count, AMP_SLOTS - 1))
                kept.append(m)
                count = count + m
            own_scale = lane_scale(
                mask[k, 4 * v + c, 4 * s + 2 * ap], mask[k, 4 * v + c, 4 * s + 2 * ap + 1], 2.0
            )
            for xx, buf in ((x, near_ref), (1 - x, far_ref)):
                stacked = jnp.concatenate(
                    [jnp.where(kept[a2] > 0, buf[slots[a2]], zero) for a2 in range(2)], axis=0
                )
                turned = stacked.T.astype(jnp.float32)
                for ii in range(2):
                    local = jnp.where(
                        kk < 2,
                        own_ref[xx, 0, ii, 0, pl.ds(arow, TILE), pl.ds(ccol, 128)],
                        oth_ref[xx, 0, ii, 0, pl.ds(arow, TILE), pl.ds(ccol, 128)],
                    ).astype(jnp.float32)
                    value = own_scale * local - turned[ii * TILE : (ii + 1) * TILE]
                    out_ref[0, xx, ii, pl.ds(arow, TILE), pl.ds(ccol, 128)] = value.astype(jnp.bfloat16)
        return count

    count_ref[0] = lax.fori_loop(0, 2, body, count_ref[0])


def diagonal_kernel(meta, mask, own_ref, oth_ref, out_ref):
    v, r = meta[0], meta[2]
    kk = pl.program_id(0)
    k = lax.rem(kk + 2 * r, 4)

    def screened(xx, ii, a0, c0):
        rows = []
        for a2 in range(2):
            start = a0 * 128 + a2 * TILE
            block = jnp.where(
                kk < 2,
                own_ref[xx, 0, ii, 0, start : start + TILE, c0 * 128 : (c0 + 1) * 128],
                oth_ref[xx, 0, ii, 0, start : start + TILE, c0 * 128 : (c0 + 1) * 128],
            ).astype(jnp.float32)
            at_row = 4 * v + 2 * a0 + a2
            rows.append(
                block
                * lane_scale(
                    mask[k, at_row, 4 * v + 2 * c0], mask[k, at_row, 4 * v + 2 * c0 + 1], 1.0
                )
            )
        return jnp.concatenate(rows, axis=0)

    for xx in range(2):
        for ii in range(2):
            for a0 in range(2):
                for c0 in range(2):
                    value = 2.0 * screened(xx, ii, a0, c0) - screened(xx, ii, c0, a0).T
                    out_ref[0, xx, ii, a0 * 128 : (a0 + 1) * 128, c0 * 128 : (c0 + 1) * 128] = (
                        value.astype(jnp.bfloat16)
                    )


def folded(direct, swapped):
    return (2.0 * direct.astype(jnp.float32) - swapped.astype(jnp.float32)).astype(jnp.bfloat16)


def fold_kernel(meta, *refs):
    direct, swapped, w_ref = refs[:3], refs[3:6], refs[6]
    v = meta[0]
    for q in range(3):
        for p in range(3):
            col = pl.multiple_of((v ^ p) * 256, 256)
            row = pl.multiple_of((v ^ q) * 256, 256)
            w_ref[q, :, p * 256 : (p + 1) * 256] = folded(
                direct[q][0, :, pl.ds(col, 256)], swapped[p][0, pl.ds(row, 256), :]
            )


def early_kernel(meta, w_ref, *refs):
    blocks, out_ref = refs[:3], refs[-1]
    total = jnp.dot(
        blocks[0][...].reshape(512, 1024), w_ref[0], preferred_element_type=jnp.float32
    )
    for q in range(1, 3):
        total += jnp.dot(
            blocks[q][...].reshape(512, 1024), w_ref[q], preferred_element_type=jnp.float32
        )
    out_ref[...] = total


def late_kernel(meta, *refs):
    direct, swapped, own, oth = refs[:4], refs[4:8], refs[8:11], refs[11:14]
    row_ref, out_ref, col_ref = refs[14:]
    v = meta[0]
    g = pl.program_id(0)
    last_at = pl.multiple_of((v ^ 3) * 256, 256)

    for p in range(4):
        at = pl.multiple_of((v ^ p) * 256, 256)
        row_ref[:, p * 256 : (p + 1) * 256] = folded(
            direct[3][g, :, pl.ds(at, 256)],
            swapped[p][g] if p < 3 else swapped[3][g, pl.ds(last_at, 256), :],
        )

    @pl.when(g == 0)
    def _():
        for p in range(3):
            at = pl.multiple_of((v ^ p) * 256, 256)
            for k in range(4):
                col_ref[p, k * 256 : (k + 1) * 256, :] = folded(
                    direct[p][k], swapped[3][k, pl.ds(at, 256), :]
                )

    def work(blocks):
        total = jnp.dot(
            blocks[0][...].reshape(512, 1024), col_ref[0], preferred_element_type=jnp.float32
        )
        for q in range(1, 3):
            total += jnp.dot(
                blocks[q][...].reshape(512, 1024), col_ref[q], preferred_element_type=jnp.float32
            )
        out_ref[...] = total

    @pl.when(g < 2)
    def _():
        work(own)

    @pl.when(g >= 2)
    def _():
        work(oth)


def tail_kernel(meta, eps_slab, eps_pair, eps_rows, eps_cols, part_ref, late_ref, row_ref, *refs):
    own, oth, out_ref = refs[:2], refs[2:4], refs[4]
    v, r = meta[0], meta[2]
    g = pl.program_id(0)

    def work(blocks, i, k0):
        total = jnp.float32(0)
        for half in range(2):
            at = pl.multiple_of(256 * lax.rem(k0 + 2 * half, 4), 512)
            total += jnp.dot(
                blocks[half][...].reshape(512, 512),
                row_ref[pl.ds(at, 512), :],
                preferred_element_type=jnp.float32,
            )
        for p in range(4):
            s = v ^ p
            before = late_ref[...] if p == 3 else part_ref[:, p * 256 : (p + 1) * 256]
            value = total[:, p * 256 : (p + 1) * 256] + before
            cols = eps_cols[:, pl.ds(pl.multiple_of(s * 256, 256), 256)]
            for ii in range(2):
                energy = (eps_rows[...] + cols) - eps_slab[i + ii] - eps_pair[0]
                done = value[ii * 256 : (ii + 1) * 256] / energy
                for n in range(2):
                    at = pl.multiple_of(s * 256 + n * 128, 128)
                    out_ref[ii, :, 0, pl.ds(at, 128)] = done[:, n * 128 : (n + 1) * 128]

    @pl.when(g < 2)
    def _():
        work(own, 4 * g + 2 * r, 2 * r)

    @pl.when(g >= 2)
    def _():
        work(oth, 4 * (g - 2) + 2 * (1 - r), 2 * (1 - r))


def smem():
    return pl.BlockSpec(memory_space=pltpu.SMEM)


def whole():
    return pl.BlockSpec(memory_space=pltpu.VMEM)


def anywhere():
    return pl.BlockSpec(memory_space=pl.ANY)


def params():
    return pltpu.CompilerParams(vmem_limit_bytes=VMEM_LIMIT)


def as_is(array):
    def kernel(from_ref, to_ref):
        pltpu.sync_copy(from_ref, to_ref)

    return pl.pallas_call(
        kernel,
        out_shape=jax.ShapeDtypeStruct(array.shape, array.dtype),
        in_specs=[anywhere()],
        out_specs=anywhere(),
        name="as_is",
    )(array)


def k_place(kk, r):
    return lax.rem(kk + 2 * r, 4)


def packed_shards(amplitudes, integrals, amp_mask, int_mask, eps_slab, eps_pair, eps_vir):
    v, x, r = lax.axis_index("vir"), lax.axis_index("occ"), lax.axis_index("rep")
    meta = jnp.stack([v, x, r, 2 * x + r]).astype(jnp.int32)
    swap = [(0, 1), (1, 0)]
    bf16 = jnp.bfloat16

    pairs = amp_mask.reshape(4, 4, 4, 4, 4).sum((0, 2, 4))
    pairs = jnp.where(jnp.eye(4, dtype=bool), 0, pairs)
    pieces = int_mask.reshape(4, 4, 4, 4, 16).sum((0, 3, 4))
    over = jnp.logical_or(jnp.max(pairs) > AMP_SLOTS - 1, jnp.max(pieces) > INT_SLOTS - 1)
    over = over.astype(jnp.int32).reshape(1)

    int_oth = lax.ppermute(integrals, "rep", swap)
    amps = amplitudes.reshape(2, 2, 2, 2, 256, 1024)
    int_oth, later = lax.optimization_barrier((int_oth, amps))
    amp_oth = lax.ppermute(later, "rep", swap)

    packed_int = pl.pallas_call(
        pack_int_kernel,
        out_shape=jax.ShapeDtypeStruct((INT_SLOTS, 32, LANES), bf16),
        in_specs=[smem(), smem(), whole(), whole()],
        out_specs=whole(),
        compiler_params=params(),
        cost_estimate=NO_COST,
        name="pack_int",
    )(meta, int_mask, integrals, int_oth)

    up1 = lax.ppermute(packed_int, "vir", [(0, 1), (1, 2), (2, 3)])
    down1 = lax.ppermute(packed_int, "vir", [(1, 0), (2, 1), (3, 2)])

    packed_amp = pl.pallas_call(
        pack_amp_kernel,
        grid_spec=pltpu.PrefetchScalarGridSpec(
            num_scalar_prefetch=2,
            grid=(1,),
            in_specs=[
                pl.BlockSpec((1, 1, 2, 2, 256, 1024), lambda g, meta, mask: (meta[1], meta[2], 0, 0, 0, 0)),
                pl.BlockSpec((1, 1, 2, 2, 256, 1024), lambda g, meta, mask: (meta[1], meta[2], 0, 0, 0, 0)),
            ],
            out_specs=[pl.BlockSpec((AMP_SLOTS, TILE, LANES), lambda g, meta, mask: (0, 0, 0))] * 3,
        ),
        out_shape=[jax.ShapeDtypeStruct((AMP_SLOTS, TILE, LANES), bf16)] * 3,
        compiler_params=params(),
        cost_estimate=NO_COST,
        name="pack_amp",
    )(meta, amp_mask, amps, amp_oth)

    def across(d, packed):
        return lax.ppermute(packed, "vir", [(s, s ^ d) for s in range(4)])

    packed3, over = lax.optimization_barrier((packed_amp[2], over))
    over = over + lax.ppermute(over, "frag", swap)
    up1, down1, over = lax.optimization_barrier((up1, down1, over))
    up2 = lax.ppermute(up1, "vir", [(1, 2), (2, 3)])
    down2 = lax.ppermute(down1, "vir", [(1, 0), (2, 1)])

    int_shapes = [
        jax.ShapeDtypeStruct((4, 256, 1024), bf16),
        jax.ShapeDtypeStruct((4, 1024, 256), bf16),
    ]
    int_outs = [
        pl.BlockSpec((1, 256, 1024), lambda kk, meta, mask: (k_place(kk, meta[2]), 0, 0)),
        pl.BlockSpec((1, 1024, 256), lambda kk, meta, mask: (k_place(kk, meta[2]), 0, 0)),
    ]
    def unpack(d, *operands):
        if d == 0:
            kernel, scratch = own_int_kernel, []
            specs = [
                pl.BlockSpec((1, 1, 256, 1024), lambda kk, meta, mask: (jnp.minimum(kk, 1), meta[2], 0, 0)),
                pl.BlockSpec((1, 1, 256, 1024), lambda kk, meta, mask: (jnp.maximum(kk - 2, 0), meta[2], 0, 0)),
            ]
        else:
            kernel = functools.partial(unpack_int_kernel, d)
            scratch = [pltpu.VMEM((INT_SLOTS, 32, LANES), bf16), pltpu.SMEM((1,), jnp.int32)]
            specs = [anywhere() for _ in operands]
        return pl.pallas_call(
            kernel,
            grid_spec=pltpu.PrefetchScalarGridSpec(
                num_scalar_prefetch=2, grid=(4,), in_specs=specs, out_specs=int_outs, scratch_shapes=scratch
            ),
            out_shape=int_shapes,
            compiler_params=params(),
            cost_estimate=NO_COST,
            name=f"ints_{d}",
        )(meta, int_mask, *operands)

    def local_specs(d, base):
        def at(side):
            def place(kk, meta, mask):
                k = jnp.minimum(kk + base, 1) if side == 0 else jnp.maximum(kk + base - 2, 0)
                return (0, meta[2], 0, k, 0, meta[0] ^ d)

            return place

        return [pl.BlockSpec((2, 1, 2, 1, 256, 256), at(side)) for side in range(2)]

    def combine(d, base, near, far, steps, extra_specs, extra, out_specs, out_shape, aliases, scratch):
        kernel = diagonal_kernel if d == 0 else functools.partial(combine_kernel, d, base)
        specs, operands = [], ()
        if d > 0:
            specs = [pl.BlockSpec((AMP_SLOTS, TILE, LANES), lambda kk, meta, mask: (0, 0, 0))] * 2
            operands = (near, far)
        return pl.pallas_call(
            kernel,
            grid_spec=pltpu.PrefetchScalarGridSpec(
                num_scalar_prefetch=2,
                grid=(steps,),
                in_specs=local_specs(d, base) + specs + extra_specs,
                out_specs=out_specs,
                scratch_shapes=scratch,
            ),
            out_shape=out_shape,
            input_output_aliases=aliases,
            compiler_params=params(),
            cost_estimate=NO_COST,
            name=f"combine_{d}_{base}",
        )(meta, amp_mask, amps, amp_oth, *operands, *extra)

    def combine_first(d, near, far, sofar):
        return combine(
            d,
            0,
            near,
            far,
            4,
            [] if d == 0 else [anywhere()],
            () if d == 0 else (sofar,),
            pl.BlockSpec(
                (1, 2, 2, 256, 256), lambda kk, meta, mask: (d, 0, 0, 0, k_place(kk, meta[2]))
            ),
            jax.ShapeDtypeStruct((3, 2, 2, 256, 1024), bf16),
            {} if d == 0 else {6: 0},
            [] if d == 0 else [pltpu.SMEM((1,), jnp.int32)],
        )

    def combine_half(base, near, far, *count):
        return combine(
            3,
            base,
            near,
            far,
            2,
            [smem() for _ in count],
            count,
            [pl.BlockSpec((1, 2, 2, 256, 256), lambda kk, meta, mask: (0, 0, 0, 0, kk)), smem()],
            [jax.ShapeDtypeStruct((1, 2, 2, 256, 512), bf16), jax.ShapeDtypeStruct((1,), jnp.int32)],
            {},
            [],
        )

    ready = lax.optimization_barrier
    ints = [unpack(0, integrals, int_oth)]
    first = combine_first(0, None, None, None)
    near1, near2 = across(1, packed_amp[0]), across(2, packed_amp[1])
    near1, ints[0], first = ready((near1, ints[0], first))
    far1, far2 = lax.ppermute(near1, "occ", swap), lax.ppermute(near2, "occ", swap)
    ints.append(unpack(1, down1, up1))
    ints[1], far1 = ready((ints[1], far1))
    first = combine_first(1, near1, far1, first)
    first = combine_first(2, near2, far2, first)
    near3 = across(3, packed3)
    up2, down2, first = ready((up2, down2, first))
    ints.append(unpack(2, down2, up2))
    folded_w = pl.pallas_call(
        fold_kernel,
        grid_spec=pltpu.PrefetchScalarGridSpec(
            num_scalar_prefetch=1,
            grid=(4,),
            in_specs=[pl.BlockSpec((1, 256, 1024), lambda k, meta: (k, 0, 0))] * 3
            + [pl.BlockSpec((1, 1024, 256), lambda k, meta: (k, 0, 0))] * 3,
            out_specs=pl.BlockSpec((3, 256, 768), lambda k, meta: (0, k, 0)),
        ),
        out_shape=jax.ShapeDtypeStruct((3, 1024, 768), bf16),
        compiler_params=params(),
        cost_estimate=NO_COST,
        name="fold",
    )(meta, *[d for d, _ in ints], *[t for _, t in ints])
    up2, down2, near3, first, folded_w = ready((up2, down2, near3, first, folded_w))
    end_down = lax.ppermute(down2, "vir", [(1, 0)])
    end_up = lax.ppermute(up2, "vir", [(2, 3)])
    first_oth = lax.ppermute(first, "rep", swap)

    def own_at(d, width=1024):
        return pl.BlockSpec((1, 1, 2, 256, width), lambda g, *_: (d % 3, jnp.minimum(g, 1), 0, 0, 0))

    def oth_at(d, width=1024):
        return pl.BlockSpec((1, 1, 2, 256, width), lambda g, *_: (d % 3, jnp.maximum(g - 2, 0), 0, 0, 0))

    def place(g, meta, *_):
        return (2 * (g % 2) + jnp.where(g < 2, meta[2], 1 - meta[2]), 0)

    once = pl.Buffered(1)
    def early(c, other, *sofar):
        def at(d):
            return pl.BlockSpec((1, 1, 2, 256, 1024), lambda g, *_: (d, g, 0, 0, 0))

        return pl.pallas_call(
            early_kernel,
            grid_spec=pltpu.PrefetchScalarGridSpec(
                num_scalar_prefetch=1,
                grid=(2,),
                in_specs=[pl.BlockSpec((3, 1024, 768), lambda g, *_: (0, 0, 0), pipeline_mode=once)]
                + [at(d) for d in range(3)]
                + [anywhere() for _ in sofar],
                out_specs=pl.BlockSpec((512, 768), lambda g, meta: place(g + 2 * other, meta)),
            ),
            out_shape=jax.ShapeDtypeStruct((2048, 768), jnp.float32),
            input_output_aliases={5: 0} if sofar else {},
            compiler_params=params(),
            cost_estimate=NO_COST,
            name=f"early_{other}",
        )(meta, folded_w, c, c, c, *sofar)

    part = early(first_oth, 1, early(first, 0))

    far3 = lax.ppermute(near3, "occ", swap)
    far3, part = ready((far3, part))
    half0, count = combine_half(0, near3, far3)
    half1, _ = combine_half(2, near3, far3, count)
    halves = (half0, half1)
    halves_oth = tuple(lax.ppermute(h, "rep", swap) for h in halves)
    end_down, end_up, half1 = ready((end_down, end_up, half1))
    ints.append(unpack(3, end_down, down1, up1, end_up))
    rows, cols = [d for d, _ in ints], [t for _, t in ints]
    last_row, late = pl.pallas_call(
        late_kernel,
        grid_spec=pltpu.PrefetchScalarGridSpec(
            num_scalar_prefetch=1,
            grid=(4,),
            in_specs=[pl.BlockSpec((4, 256, 256), lambda g, meta: (0, 0, meta[0] ^ 3), pipeline_mode=once)] * 3
            + [pl.BlockSpec((4, 256, 1024), lambda g, meta: (0, 0, 0), pipeline_mode=once)]
            + [pl.BlockSpec((4, 256, 256), lambda g, meta: (0, meta[0] ^ 3, 0), pipeline_mode=once)] * 3
            + [pl.BlockSpec((4, 1024, 256), lambda g, meta: (0, 0, 0), pipeline_mode=once)]
            + [own_at(d) for d in range(3)]
            + [oth_at(d) for d in range(3)],
            out_specs=[
                pl.BlockSpec((256, 1024), lambda g, meta: (g, 0)),
                pl.BlockSpec((512, 256), place),
            ],
            scratch_shapes=[pltpu.VMEM((3, 1024, 256), bf16)],
        ),
        out_shape=[
            jax.ShapeDtypeStruct((1024, 1024), bf16),
            jax.ShapeDtypeStruct((2048, 256), jnp.float32),
        ],
        compiler_params=params(),
        cost_estimate=NO_COST,
        name="late",
    )(meta, *rows, *cols, *[first] * 3, *[first_oth] * 3)
    row_energy = lax.dynamic_slice_in_dim(eps_vir, v * 256, 256, 0).reshape(256, 1)
    col_energy = eps_vir.reshape(1, 1024)

    def finish(ops):
        part, late, last_row, own, oth = ops
        return pl.pallas_call(
            tail_kernel,
            grid_spec=pltpu.PrefetchScalarGridSpec(
                num_scalar_prefetch=3,
                grid=(4,),
                in_specs=[
                    pl.BlockSpec((256, 1), lambda g, *_: (0, 0)),
                    pl.BlockSpec((1, 1024), lambda g, *_: (0, 0)),
                    pl.BlockSpec((512, 768), place),
                    pl.BlockSpec((512, 256), place),
                    pl.BlockSpec((1024, 1024), lambda g, *_: (0, 0), pipeline_mode=once),
                ]
                + [own_at(3, 512)] * 2
                + [oth_at(3, 512)] * 2,
                out_specs=pl.BlockSpec((2, 256, 1, 1024), lambda g, meta, *_: (*place(g, meta), 0, 0)),
            ),
            out_shape=jax.ShapeDtypeStruct((8, 256, 1, 1024), jnp.float32),
            compiler_params=params(),
            cost_estimate=NO_COST,
            name="tail",
        )(meta, eps_slab, eps_pair, row_energy, col_energy, part, late, last_row, *own, *oth)

    def dense(state):
        out = dense_shards(
            as_is(amplitudes), as_is(integrals), amp_mask, int_mask, eps_slab, eps_pair, eps_vir
        )
        return as_is(out), jnp.zeros((), jnp.int32)

    out = finish((part, late, last_row, halves, halves_oth))
    return lax.while_loop(lambda state: state[1] > 0, dense, (out, over[0]))[0]


def shards(sizes, *args):
    amplitudes, integrals, amp_mask, int_mask = args[:4]
    fits = (
        sizes == {"frag": 2, "vir": 4, "occ": 2, "rep": 2}
        and amplitudes.shape == (8, 2, 256, 1024)
        and integrals.shape == (2, 2, 256, 1024)
        and amp_mask.shape == (4, 16, 16)
        and int_mask.shape == (4, 4, 16, 16)
    )
    return packed_shards(*args) if fits else dense_shards(*args)


def solution(mesh):
    in_specs = (
        P("frag", "rep", "vir", None),
        P(("frag", "rep"), "occ", "vir", None),
        P("frag", None, None),
        P("frag", None, None, None),
        P("frag"),
        P(("frag", "occ", "rep")),
        P("frag"),
    )
    out_specs = P("frag", "vir", ("occ", "rep"), None)
    return jax.shard_map(
        functools.partial(shards, dict(mesh.shape)),
        mesh=mesh,
        in_specs=in_specs,
        out_specs=out_specs,
        check_vma=False,
    )
```

```python
import functools

import jax
import jax.numpy as jnp
from jax import lax
from jax.experimental import pallas as pl
from jax.experimental.pallas import tpu as pltpu
from jax.sharding import PartitionSpec as P

TILE = 64
LANES = 128
AMP_SLOTS = 46
INT_SLOTS = 160
VMEM_LIMIT = 60 * 1024 * 1024
NO_COST = pl.CostEstimate(flops=1024, bytes_accessed=1024, transcendentals=0)


def tile_mask(mask_tiles, row_start, row_count, tile_size):
    tile_count = mask_tiles.shape[-1]
    row_tiles = (row_start + jnp.arange(row_count, dtype=jnp.int32)) // tile_size
    select = (row_tiles[:, None] == jnp.arange(tile_count, dtype=jnp.int32)[None, :]).astype(
        jnp.float32
    )
    picked = jnp.einsum("ra,...ac->...rc", select, mask_tiles.astype(jnp.float32))
    return jnp.repeat(picked, tile_size, axis=-1)


def cycle_terms(combined, gathered):
    direct_term = jnp.einsum(
        "ikac,kjcb->iajb", combined, gathered, preferred_element_type=jnp.float32
    )
    swapped_term = jnp.einsum(
        "ikac,kjbc->iajb", combined, gathered, preferred_element_type=jnp.float32
    )
    return 2.0 * direct_term - swapped_term


def dense_shards(amplitudes, integrals, amp_mask, int_mask, eps_slab, eps_pair, eps_vir):
    row_count = amplitudes.shape[2]
    half_count = amplitudes.shape[1]
    pair_count = integrals.shape[1]
    row_start = lax.axis_index("vir") * row_count
    k_start = lax.axis_index("rep") * half_count
    j_start = lax.axis_index("occ") * pair_count
    zero_index = jnp.zeros((), jnp.int32)
    k_masks = lax.dynamic_slice_in_dim(amp_mask, k_start, half_count, 0)
    screened = (
        amplitudes.astype(jnp.float32) * tile_mask(k_masks, row_start, row_count, TILE)[None]
    ).astype(jnp.bfloat16)
    received = lax.all_to_all(screened, "vir", split_axis=3, concat_axis=2, tiled=True)
    combined = (
        2.0 * screened.astype(jnp.float32) - jnp.swapaxes(received, 2, 3).astype(jnp.float32)
    ).astype(jnp.bfloat16)
    pair_masks = lax.dynamic_slice(
        int_mask,
        (k_start, j_start, zero_index, zero_index),
        (half_count, pair_count, int_mask.shape[2], int_mask.shape[3]),
    )
    kept_local = (
        integrals.astype(jnp.float32) * tile_mask(pair_masks, row_start, row_count, TILE)
    ).astype(jnp.bfloat16)
    gathered = lax.all_gather(kept_local, "vir", axis=2, tiled=True)
    partial_cycle = cycle_terms(combined, gathered)
    cycle = lax.psum_scatter(partial_cycle, "rep", scatter_dimension=2, tiled=True)
    row_energy = lax.dynamic_slice_in_dim(eps_vir, row_start, row_count, 0)
    denominator = (
        row_energy[None, :, None, None]
        + eps_vir[None, None, None, :]
        - eps_slab[:, None, None, None]
        - eps_pair[None, None, :, None]
    )
    return cycle / denominator


def low_lanes(rows):
    return lax.broadcasted_iota(jnp.int32, (rows, LANES), 1) < TILE


def swap_halves(block):
    return pltpu.roll(block, TILE, 1)


def fill(buf, choices):
    for chosen, ref in choices:

        @pl.when(chosen)
        def _(ref=ref):
            pltpu.sync_copy(ref, buf)


def pack_int_kernel(meta, mask, own_ref, oth_ref, out_ref):
    v, r, j = meta[0], meta[2], meta[3]
    low = low_lanes(32)
    count = jnp.int32(0)
    for half in range(2):

        def body(n, count, half=half):
            kk, ap = n // 2, n % 2
            k = lax.rem(kk + 2 * half + 2 * r, 4)
            for cp in range(8):
                for a2 in range(2):
                    row = pl.multiple_of(ap * 128 + a2 * TILE, TILE)
                    if half == 0:
                        block = own_ref[kk, r, pl.ds(row, TILE), cp * LANES : (cp + 1) * LANES]
                    else:
                        block = oth_ref[kk, r, pl.ds(row, TILE), cp * LANES : (cp + 1) * LANES]
                    top, bottom = block[:32], block[32:]
                    turned_top, turned_bottom = swap_halves(top), swap_halves(bottom)
                    at_row = 4 * v + 2 * ap + a2
                    out_ref[jnp.minimum(count, INT_SLOTS - 1)] = jnp.where(low, top, turned_bottom)
                    count = count + mask[k, j, at_row, 2 * cp]
                    out_ref[jnp.minimum(count, INT_SLOTS - 1)] = jnp.where(low, turned_top, bottom)
                    count = count + mask[k, j, at_row, 2 * cp + 1]
            return count

        count = lax.fori_loop(0, 4, body, count)


def pack_amp_kernel(meta, mask, own_ref, oth_ref, *out_refs):
    v, r = meta[0], meta[2]
    low = low_lanes(TILE)
    for d in range(1, 4):
        dest = v ^ d
        count = jnp.int32(0)
        for half in range(2):
            ref = own_ref if half == 0 else oth_ref

            def body(kk, count, d=d, dest=dest, half=half, ref=ref):
                k = lax.rem(kk + 2 * half + 2 * r, 4)
                for ap in range(2):
                    for cp in range(2):
                        col = pl.multiple_of(dest * 256 + cp * LANES, LANES)
                        tiles = []
                        for a2 in range(2):
                            row = ap * 128 + a2 * TILE
                            x0 = ref[0, 0, 0, kk, row : row + TILE, pl.ds(col, LANES)]
                            x1 = ref[0, 0, 1, kk, row : row + TILE, pl.ds(col, LANES)]
                            tiles.append(
                                (jnp.where(low, x0, swap_halves(x1)), jnp.where(low, swap_halves(x0), x1))
                            )
                        for c2 in range(2):
                            for a2 in range(2):
                                out_refs[d - 1][jnp.minimum(count, AMP_SLOTS - 1)] = tiles[a2][c2]
                                count = count + mask[k, 4 * v + 2 * ap + a2, 4 * dest + 2 * cp + c2]
                return count

            count = lax.fori_loop(0, 2, body, count)


def unpack_group(buf_ref, mask, k, j, s, ap, count, d_ref, t_ref, at):
    low = low_lanes(32)
    zero = jnp.zeros((32, LANES), jnp.bfloat16)
    row = pl.multiple_of(ap * 128, 128)
    for cp in range(8):
        parts = []
        for a2 in range(2):
            at_row = 4 * s + 2 * ap + a2
            m0, m1 = mask[k, j, at_row, 2 * cp], mask[k, j, at_row, 2 * cp + 1]
            y0 = buf_ref[jnp.minimum(count, INT_SLOTS - 1)]
            count = count + m0
            y1 = buf_ref[jnp.minimum(count, INT_SLOTS - 1)]
            count = count + m1
            y0 = jnp.where(m0 > 0, y0, zero)
            y1 = jnp.where(m1 > 0, y1, zero)
            parts.append(jnp.where(low, y0, swap_halves(y1)))
            parts.append(jnp.where(low, swap_halves(y0), y1))
        block = jnp.concatenate(parts, axis=0)
        d_ref[at, pl.ds(row, 128), cp * LANES : (cp + 1) * LANES] = block
        t_ref[at, cp * LANES : (cp + 1) * LANES, pl.ds(row, 128)] = block.T
    return count


def unpack_int_kernel(d, meta, mask, *refs):
    sources, (d_ref, t_ref, buf_ref, count_ref) = refs[:-4], refs[-4:]
    v, r, j = meta[0], meta[2], meta[3]
    kk = pl.program_id(0)
    k = lax.rem(kk + 2 * r, 4)
    s = v ^ d

    @pl.when(kk == 0)
    def _():
        count_ref[0] = 0
        if d < 3:
            fill(buf_ref, [(s > v, sources[0]), (s < v, sources[1])])
        else:
            fill(buf_ref, [(v == n, source) for n, source in enumerate(sources)])

    count_ref[0] = lax.fori_loop(
        0,
        2,
        lambda ap, count: unpack_group(buf_ref, mask, k, j, s, ap, count, d_ref, t_ref, 0),
        count_ref[0],
    )


def own_int_kernel(meta, mask, own_ref, oth_ref, d_ref, t_ref):
    v, r, j = meta[0], meta[2], meta[3]
    kk = pl.program_id(0)
    k = lax.rem(kk + 2 * r, 4)
    low = low_lanes(TILE)
    zero = jnp.zeros((TILE, LANES), jnp.bfloat16)

    def body(ap, carry):
        for cp in range(8):
            parts = []
            for a2 in range(2):
                at_row = 4 * v + 2 * ap + a2
                row = pl.multiple_of(ap * 128 + a2 * TILE, TILE)
                m0, m1 = mask[k, j, at_row, 2 * cp], mask[k, j, at_row, 2 * cp + 1]
                block = jnp.where(
                    kk < 2,
                    own_ref[0, 0, pl.ds(row, TILE), cp * LANES : (cp + 1) * LANES],
                    oth_ref[0, 0, pl.ds(row, TILE), cp * LANES : (cp + 1) * LANES],
                )
                parts.append(
                    jnp.where(low, jnp.where(m0 > 0, block, zero), jnp.where(m1 > 0, block, zero))
                )
            block = jnp.concatenate(parts, axis=0)
            row = pl.multiple_of(ap * 128, 128)
            d_ref[0, pl.ds(row, 128), cp * LANES : (cp + 1) * LANES] = block
            t_ref[0, cp * LANES : (cp + 1) * LANES, pl.ds(row, 128)] = block.T
        return carry

    lax.fori_loop(0, 2, body, 0)


def lane_scale(m0, m1, value):
    lane = lax.broadcasted_iota(jnp.int32, (1, LANES), 1)
    return value * jnp.where(lane < TILE, m0, m1).astype(jnp.float32)


def combine_kernel(d, base, meta, mask, own_ref, oth_ref, near_ref, far_ref, *refs):
    if d == 3:
        out_ref, count_ref = refs[-2:]
    else:
        out_ref, count_ref = refs[1:]
    v, x, r = meta[0], meta[1], meta[2]
    kk = pl.program_id(0) + base
    k = lax.rem(kk + 2 * r, 4)
    s = v ^ d
    zero = jnp.zeros((TILE, LANES), jnp.bfloat16)

    @pl.when(pl.program_id(0) == 0)
    def _():
        count_ref[0] = 0 if base == 0 else refs[0][0]

    def body(ap, count):
        ccol = pl.multiple_of(ap * 128, 128)
        for c in range(4):
            arow = c * TILE
            slots, kept = [], []
            for a2 in range(2):
                m = mask[k, 4 * s + 2 * ap + a2, 4 * v + c]
                slots.append(jnp.minimum(count, AMP_SLOTS - 1))
                kept.append(m)
                count = count + m
            own_scale = lane_scale(
                mask[k, 4 * v + c, 4 * s + 2 * ap], mask[k, 4 * v + c, 4 * s + 2 * ap + 1], 2.0
            )
            for xx, buf in ((x, near_ref), (1 - x, far_ref)):
                stacked = jnp.concatenate(
                    [jnp.where(kept[a2] > 0, buf[slots[a2]], zero) for a2 in range(2)], axis=0
                )
                turned = stacked.T.astype(jnp.float32)
                for ii in range(2):
                    local = jnp.where(
                        kk < 2,
                        own_ref[xx, 0, ii, 0, pl.ds(arow, TILE), pl.ds(ccol, 128)],
                        oth_ref[xx, 0, ii, 0, pl.ds(arow, TILE), pl.ds(ccol, 128)],
                    ).astype(jnp.float32)
                    value = own_scale * local - turned[ii * TILE : (ii + 1) * TILE]
                    out_ref[0, xx, ii, pl.ds(arow, TILE), pl.ds(ccol, 128)] = value.astype(jnp.bfloat16)
        return count

    count_ref[0] = lax.fori_loop(0, 2, body, count_ref[0])


def diagonal_kernel(meta, mask, own_ref, oth_ref, out_ref):
    v, r = meta[0], meta[2]
    kk = pl.program_id(0)
    k = lax.rem(kk + 2 * r, 4)

    def screened(xx, ii, a0, c0):
        rows = []
        for a2 in range(2):
            start = a0 * 128 + a2 * TILE
            block = jnp.where(
                kk < 2,
                own_ref[xx, 0, ii, 0, start : start + TILE, c0 * 128 : (c0 + 1) * 128],
                oth_ref[xx, 0, ii, 0, start : start + TILE, c0 * 128 : (c0 + 1) * 128],
            ).astype(jnp.float32)
            at_row = 4 * v + 2 * a0 + a2
            rows.append(
                block
                * lane_scale(
                    mask[k, at_row, 4 * v + 2 * c0], mask[k, at_row, 4 * v + 2 * c0 + 1], 1.0
                )
            )
        return jnp.concatenate(rows, axis=0)

    for xx in range(2):
        for ii in range(2):
            for a0 in range(2):
                for c0 in range(2):
                    value = 2.0 * screened(xx, ii, a0, c0) - screened(xx, ii, c0, a0).T
                    out_ref[0, xx, ii, a0 * 128 : (a0 + 1) * 128, c0 * 128 : (c0 + 1) * 128] = (
                        value.astype(jnp.bfloat16)
                    )


def folded(direct, swapped):
    return (2.0 * direct.astype(jnp.float32) - swapped.astype(jnp.float32)).astype(jnp.bfloat16)


def fold_kernel(meta, *refs):
    direct, swapped, w_ref = refs[:3], refs[3:6], refs[6]
    v = meta[0]
    for q in range(3):
        for p in range(3):
            col = pl.multiple_of((v ^ p) * 256, 256)
            row = pl.multiple_of((v ^ q) * 256, 256)
            w_ref[q, :, p * 256 : (p + 1) * 256] = folded(
                direct[q][0, :, pl.ds(col, 256)], swapped[p][0, pl.ds(row, 256), :]
            )


def early_kernel(meta, w_ref, *refs):
    blocks, out_ref = refs[:3], refs[-1]
    total = jnp.dot(
        blocks[0][...].reshape(512, 1024), w_ref[0], preferred_element_type=jnp.float32
    )
    for q in range(1, 3):
        total += jnp.dot(
            blocks[q][...].reshape(512, 1024), w_ref[q], preferred_element_type=jnp.float32
        )
    out_ref[...] = total


def late_kernel(meta, *refs):
    direct, swapped, own, oth = refs[:4], refs[4:8], refs[8:11], refs[11:14]
    row_ref, out_ref, col_ref = refs[14:]
    v = meta[0]
    g = pl.program_id(0)
    last_at = pl.multiple_of((v ^ 3) * 256, 256)

    for p in range(4):
        at = pl.multiple_of((v ^ p) * 256, 256)
        row_ref[:, p * 256 : (p + 1) * 256] = folded(
            direct[3][g, :, pl.ds(at, 256)],
            swapped[p][g] if p < 3 else swapped[3][g, pl.ds(last_at, 256), :],
        )

    @pl.when(g == 0)
    def _():
        for p in range(3):
            at = pl.multiple_of((v ^ p) * 256, 256)
            for k in range(4):
                col_ref[p, k * 256 : (k + 1) * 256, :] = folded(
                    direct[p][k], swapped[3][k, pl.ds(at, 256), :]
                )

    def work(blocks):
        total = jnp.dot(
            blocks[0][...].reshape(512, 1024), col_ref[0], preferred_element_type=jnp.float32
        )
        for q in range(1, 3):
            total += jnp.dot(
                blocks[q][...].reshape(512, 1024), col_ref[q], preferred_element_type=jnp.float32
            )
        out_ref[...] = total

    @pl.when(g < 2)
    def _():
        work(own)

    @pl.when(g >= 2)
    def _():
        work(oth)


def tail_kernel(meta, eps_slab, eps_pair, eps_rows, eps_cols, part_ref, late_ref, row_ref, *refs):
    own, oth, out_ref = refs[:2], refs[2:4], refs[4]
    flat_ref = out_ref.reshape(4096, 128)
    v, r = meta[0], meta[2]
    g = pl.program_id(0)

    def work(blocks, i, k0):
        total = jnp.float32(0)
        for half in range(2):
            at = pl.multiple_of(256 * lax.rem(k0 + 2 * half, 4), 512)
            total += jnp.dot(
                blocks[half][...].reshape(512, 512),
                row_ref[pl.ds(at, 512), :],
                preferred_element_type=jnp.float32,
            )
        for p in range(4):
            s = v ^ p
            before = late_ref[...] if p == 3 else part_ref[:, p * 256 : (p + 1) * 256]
            value = total[:, p * 256 : (p + 1) * 256] + before
            cols = eps_cols[:, pl.ds(pl.multiple_of(s * 256, 256), 256)]
            for ii in range(2):
                energy = (eps_rows[...] + cols) - eps_slab[i + ii] - eps_pair[0]
                done = value[ii * 256 : (ii + 1) * 256] / energy
                for n in range(2):
                    flat_ref[pl.ds(ii * 2048 + 2 * s + n, 256, stride=8), :] = done[
                        :, n * 128 : (n + 1) * 128
                    ]

    @pl.when(g < 2)
    def _():
        work(own, 4 * g + 2 * r, 2 * r)

    @pl.when(g >= 2)
    def _():
        work(oth, 4 * (g - 2) + 2 * (1 - r), 2 * (1 - r))


def smem():
    return pl.BlockSpec(memory_space=pltpu.SMEM)


def whole():
    return pl.BlockSpec(memory_space=pltpu.VMEM)


def anywhere():
    return pl.BlockSpec(memory_space=pl.ANY)


def params():
    return pltpu.CompilerParams(vmem_limit_bytes=VMEM_LIMIT)


def as_is(array):
    def kernel(from_ref, to_ref):
        pltpu.sync_copy(from_ref, to_ref)

    return pl.pallas_call(
        kernel,
        out_shape=jax.ShapeDtypeStruct(array.shape, array.dtype),
        in_specs=[anywhere()],
        out_specs=anywhere(),
        name="as_is",
    )(array)


def k_place(kk, r):
    return lax.rem(kk + 2 * r, 4)


def packed_shards(amplitudes, integrals, amp_mask, int_mask, eps_slab, eps_pair, eps_vir):
    v, x, r = lax.axis_index("vir"), lax.axis_index("occ"), lax.axis_index("rep")
    meta = jnp.stack([v, x, r, 2 * x + r]).astype(jnp.int32)
    swap = [(0, 1), (1, 0)]
    bf16 = jnp.bfloat16

    pairs = amp_mask.reshape(4, 4, 4, 4, 4).sum((0, 2, 4))
    pairs = jnp.where(jnp.eye(4, dtype=bool), 0, pairs)
    pieces = int_mask.reshape(4, 4, 4, 4, 16).sum((0, 3, 4))
    over = jnp.logical_or(jnp.max(pairs) > AMP_SLOTS - 1, jnp.max(pieces) > INT_SLOTS - 1)
    over = over.astype(jnp.int32).reshape(1)

    int_oth = lax.ppermute(integrals, "rep", swap)
    amps = amplitudes.reshape(2, 2, 2, 2, 256, 1024)
    int_oth, later = lax.optimization_barrier((int_oth, amps))
    amp_oth = lax.ppermute(later, "rep", swap)

    packed_int = pl.pallas_call(
        pack_int_kernel,
        out_shape=jax.ShapeDtypeStruct((INT_SLOTS, 32, LANES), bf16),
        in_specs=[smem(), smem(), whole(), whole()],
        out_specs=whole(),
        compiler_params=params(),
        cost_estimate=NO_COST,
        name="pack_int",
    )(meta, int_mask, integrals, int_oth)

    up1 = lax.ppermute(packed_int, "vir", [(0, 1), (1, 2), (2, 3)])
    down1 = lax.ppermute(packed_int, "vir", [(1, 0), (2, 1), (3, 2)])

    packed_amp = pl.pallas_call(
        pack_amp_kernel,
        grid_spec=pltpu.PrefetchScalarGridSpec(
            num_scalar_prefetch=2,
            grid=(1,),
            in_specs=[
                pl.BlockSpec((1, 1, 2, 2, 256, 1024), lambda g, meta, mask: (meta[1], meta[2], 0, 0, 0, 0)),
                pl.BlockSpec((1, 1, 2, 2, 256, 1024), lambda g, meta, mask: (meta[1], meta[2], 0, 0, 0, 0)),
            ],
            out_specs=[pl.BlockSpec((AMP_SLOTS, TILE, LANES), lambda g, meta, mask: (0, 0, 0))] * 3,
        ),
        out_shape=[jax.ShapeDtypeStruct((AMP_SLOTS, TILE, LANES), bf16)] * 3,
        compiler_params=params(),
        cost_estimate=NO_COST,
        name="pack_amp",
    )(meta, amp_mask, amps, amp_oth)

    def across(d, packed):
        return lax.ppermute(packed, "vir", [(s, s ^ d) for s in range(4)])

    packed3, over = lax.optimization_barrier((packed_amp[2], over))
    over = over + lax.ppermute(over, "frag", swap)
    up1, down1, over = lax.optimization_barrier((up1, down1, over))
    up2 = lax.ppermute(up1, "vir", [(1, 2), (2, 3)])
    down2 = lax.ppermute(down1, "vir", [(1, 0), (2, 1)])

    int_shapes = [
        jax.ShapeDtypeStruct((4, 256, 1024), bf16),
        jax.ShapeDtypeStruct((4, 1024, 256), bf16),
    ]
    int_outs = [
        pl.BlockSpec((1, 256, 1024), lambda kk, meta, mask: (k_place(kk, meta[2]), 0, 0)),
        pl.BlockSpec((1, 1024, 256), lambda kk, meta, mask: (k_place(kk, meta[2]), 0, 0)),
    ]
    def unpack(d, *operands):
        if d == 0:
            kernel, scratch = own_int_kernel, []
            specs = [
                pl.BlockSpec((1, 1, 256, 1024), lambda kk, meta, mask: (jnp.minimum(kk, 1), meta[2], 0, 0)),
                pl.BlockSpec((1, 1, 256, 1024), lambda kk, meta, mask: (jnp.maximum(kk - 2, 0), meta[2], 0, 0)),
            ]
        else:
            kernel = functools.partial(unpack_int_kernel, d)
            scratch = [pltpu.VMEM((INT_SLOTS, 32, LANES), bf16), pltpu.SMEM((1,), jnp.int32)]
            specs = [anywhere() for _ in operands]
        return pl.pallas_call(
            kernel,
            grid_spec=pltpu.PrefetchScalarGridSpec(
                num_scalar_prefetch=2, grid=(4,), in_specs=specs, out_specs=int_outs, scratch_shapes=scratch
            ),
            out_shape=int_shapes,
            compiler_params=params(),
            cost_estimate=NO_COST,
            name=f"ints_{d}",
        )(meta, int_mask, *operands)

    def local_specs(d, base):
        def at(side):
            def place(kk, meta, mask):
                k = jnp.minimum(kk + base, 1) if side == 0 else jnp.maximum(kk + base - 2, 0)
                return (0, meta[2], 0, k, 0, meta[0] ^ d)

            return place

        return [pl.BlockSpec((2, 1, 2, 1, 256, 256), at(side)) for side in range(2)]

    def combine(d, base, near, far, steps, extra_specs, extra, out_specs, out_shape, aliases, scratch):
        kernel = diagonal_kernel if d == 0 else functools.partial(combine_kernel, d, base)
        specs, operands = [], ()
        if d > 0:
            specs = [pl.BlockSpec((AMP_SLOTS, TILE, LANES), lambda kk, meta, mask: (0, 0, 0))] * 2
            operands = (near, far)
        return pl.pallas_call(
            kernel,
            grid_spec=pltpu.PrefetchScalarGridSpec(
                num_scalar_prefetch=2,
                grid=(steps,),
                in_specs=local_specs(d, base) + specs + extra_specs,
                out_specs=out_specs,
                scratch_shapes=scratch,
            ),
            out_shape=out_shape,
            input_output_aliases=aliases,
            compiler_params=params(),
            cost_estimate=NO_COST,
            name=f"combine_{d}_{base}",
        )(meta, amp_mask, amps, amp_oth, *operands, *extra)

    def combine_first(d, near, far, sofar):
        return combine(
            d,
            0,
            near,
            far,
            4,
            [] if d == 0 else [anywhere()],
            () if d == 0 else (sofar,),
            pl.BlockSpec(
                (1, 2, 2, 256, 256), lambda kk, meta, mask: (d, 0, 0, 0, k_place(kk, meta[2]))
            ),
            jax.ShapeDtypeStruct((3, 2, 2, 256, 1024), bf16),
            {} if d == 0 else {6: 0},
            [] if d == 0 else [pltpu.SMEM((1,), jnp.int32)],
        )

    def combine_half(base, near, far, *count):
        return combine(
            3,
            base,
            near,
            far,
            2,
            [smem() for _ in count],
            count,
            [pl.BlockSpec((1, 2, 2, 256, 256), lambda kk, meta, mask: (0, 0, 0, 0, kk)), smem()],
            [jax.ShapeDtypeStruct((1, 2, 2, 256, 512), bf16), jax.ShapeDtypeStruct((1,), jnp.int32)],
            {},
            [],
        )

    ready = lax.optimization_barrier
    ints = [unpack(0, integrals, int_oth)]
    first = combine_first(0, None, None, None)
    near1, near2 = across(1, packed_amp[0]), across(2, packed_amp[1])
    near1, ints[0], first = ready((near1, ints[0], first))
    far1, far2 = lax.ppermute(near1, "occ", swap), lax.ppermute(near2, "occ", swap)
    ints.append(unpack(1, down1, up1))
    ints[1], far1 = ready((ints[1], far1))
    first = combine_first(1, near1, far1, first)
    first = combine_first(2, near2, far2, first)
    near3 = across(3, packed3)
    up2, down2, first = ready((up2, down2, first))
    ints.append(unpack(2, down2, up2))
    folded_w = pl.pallas_call(
        fold_kernel,
        grid_spec=pltpu.PrefetchScalarGridSpec(
            num_scalar_prefetch=1,
            grid=(4,),
            in_specs=[pl.BlockSpec((1, 256, 1024), lambda k, meta: (k, 0, 0))] * 3
            + [pl.BlockSpec((1, 1024, 256), lambda k, meta: (k, 0, 0))] * 3,
            out_specs=pl.BlockSpec((3, 256, 768), lambda k, meta: (0, k, 0)),
        ),
        out_shape=jax.ShapeDtypeStruct((3, 1024, 768), bf16),
        compiler_params=params(),
        cost_estimate=NO_COST,
        name="fold",
    )(meta, *[d for d, _ in ints], *[t for _, t in ints])
    up2, down2, near3, first, folded_w = ready((up2, down2, near3, first, folded_w))
    end_down = lax.ppermute(down2, "vir", [(1, 0)])
    end_up = lax.ppermute(up2, "vir", [(2, 3)])
    first_oth = lax.ppermute(first, "rep", swap)

    def own_at(d, width=1024):
        return pl.BlockSpec((1, 1, 2, 256, width), lambda g, *_: (d % 3, jnp.minimum(g, 1), 0, 0, 0))

    def oth_at(d, width=1024):
        return pl.BlockSpec((1, 1, 2, 256, width), lambda g, *_: (d % 3, jnp.maximum(g - 2, 0), 0, 0, 0))

    def place(g, meta, *_):
        return (2 * (g % 2) + jnp.where(g < 2, meta[2], 1 - meta[2]), 0)

    once = pl.Buffered(1)
    def early(c, other, *sofar):
        def at(d):
            return pl.BlockSpec((1, 1, 2, 256, 1024), lambda g, *_: (d, g, 0, 0, 0))

        return pl.pallas_call(
            early_kernel,
            grid_spec=pltpu.PrefetchScalarGridSpec(
                num_scalar_prefetch=1,
                grid=(2,),
                in_specs=[pl.BlockSpec((3, 1024, 768), lambda g, *_: (0, 0, 0), pipeline_mode=once)]
                + [at(d) for d in range(3)]
                + [anywhere() for _ in sofar],
                out_specs=pl.BlockSpec((512, 768), lambda g, meta: place(g + 2 * other, meta)),
            ),
            out_shape=jax.ShapeDtypeStruct((2048, 768), jnp.float32),
            input_output_aliases={5: 0} if sofar else {},
            compiler_params=params(),
            cost_estimate=NO_COST,
            name=f"early_{other}",
        )(meta, folded_w, c, c, c, *sofar)

    part = early(first_oth, 1, early(first, 0))

    far3 = lax.ppermute(near3, "occ", swap)
    far3, part = ready((far3, part))
    half0, count = combine_half(0, near3, far3)
    half1, _ = combine_half(2, near3, far3, count)
    halves = (half0, half1)
    halves_oth = tuple(lax.ppermute(h, "rep", swap) for h in halves)
    end_down, end_up, half1 = ready((end_down, end_up, half1))
    ints.append(unpack(3, end_down, down1, up1, end_up))
    rows, cols = [d for d, _ in ints], [t for _, t in ints]
    last_row, late = pl.pallas_call(
        late_kernel,
        grid_spec=pltpu.PrefetchScalarGridSpec(
            num_scalar_prefetch=1,
            grid=(4,),
            in_specs=[pl.BlockSpec((4, 256, 256), lambda g, meta: (0, 0, meta[0] ^ 3), pipeline_mode=once)] * 3
            + [pl.BlockSpec((4, 256, 1024), lambda g, meta: (0, 0, 0), pipeline_mode=once)]
            + [pl.BlockSpec((4, 256, 256), lambda g, meta: (0, meta[0] ^ 3, 0), pipeline_mode=once)] * 3
            + [pl.BlockSpec((4, 1024, 256), lambda g, meta: (0, 0, 0), pipeline_mode=once)]
            + [own_at(d) for d in range(3)]
            + [oth_at(d) for d in range(3)],
            out_specs=[
                pl.BlockSpec((256, 1024), lambda g, meta: (g, 0)),
                pl.BlockSpec((512, 256), place),
            ],
            scratch_shapes=[pltpu.VMEM((3, 1024, 256), bf16)],
        ),
        out_shape=[
            jax.ShapeDtypeStruct((1024, 1024), bf16),
            jax.ShapeDtypeStruct((2048, 256), jnp.float32),
        ],
        compiler_params=params(),
        cost_estimate=NO_COST,
        name="late",
    )(meta, *rows, *cols, *[first] * 3, *[first_oth] * 3)
    row_energy = lax.dynamic_slice_in_dim(eps_vir, v * 256, 256, 0).reshape(256, 1)
    col_energy = eps_vir.reshape(1, 1024)

    def finish(ops):
        part, late, last_row, own, oth = ops
        return pl.pallas_call(
            tail_kernel,
            grid_spec=pltpu.PrefetchScalarGridSpec(
                num_scalar_prefetch=3,
                grid=(4,),
                in_specs=[
                    pl.BlockSpec((256, 1), lambda g, *_: (0, 0)),
                    pl.BlockSpec((1, 1024), lambda g, *_: (0, 0)),
                    pl.BlockSpec((512, 768), place),
                    pl.BlockSpec((512, 256), place),
                    pl.BlockSpec((1024, 1024), lambda g, *_: (0, 0), pipeline_mode=once),
                ]
                + [own_at(3, 512)] * 2
                + [oth_at(3, 512)] * 2,
                out_specs=pl.BlockSpec((2, 256, 1, 1024), lambda g, meta, *_: (*place(g, meta), 0, 0)),
            ),
            out_shape=jax.ShapeDtypeStruct((8, 256, 1, 1024), jnp.float32),
            compiler_params=params(),
            cost_estimate=NO_COST,
            name="tail",
        )(meta, eps_slab, eps_pair, row_energy, col_energy, part, late, last_row, *own, *oth)

    def dense(state):
        out = dense_shards(
            as_is(amplitudes), as_is(integrals), amp_mask, int_mask, eps_slab, eps_pair, eps_vir
        )
        return as_is(out), jnp.zeros((), jnp.int32)

    out = finish((part, late, last_row, halves, halves_oth))
    return lax.while_loop(lambda state: state[1] > 0, dense, (out, over[0]))[0]


def shards(sizes, *args):
    amplitudes, integrals, amp_mask, int_mask = args[:4]
    fits = (
        sizes == {"frag": 2, "vir": 4, "occ": 2, "rep": 2}
        and amplitudes.shape == (8, 2, 256, 1024)
        and integrals.shape == (2, 2, 256, 1024)
        and amp_mask.shape == (4, 16, 16)
        and int_mask.shape == (4, 4, 16, 16)
    )
    return packed_shards(*args) if fits else dense_shards(*args)


def solution(mesh):
    in_specs = (
        P("frag", "rep", "vir", None),
        P(("frag", "rep"), "occ", "vir", None),
        P("frag", None, None),
        P("frag", None, None, None),
        P("frag"),
        P(("frag", "occ", "rep")),
        P("frag"),
    )
    out_specs = P("frag", "vir", ("occ", "rep"), None)
    return jax.shard_map(
        functools.partial(shards, dict(mesh.shape)),
        mesh=mesh,
        in_specs=in_specs,
        out_specs=out_specs,
        check_vma=False,
    )
```

```python
import functools

import jax
import jax.numpy as jnp
from jax import lax
from jax.experimental import pallas as pl
from jax.experimental.pallas import tpu as pltpu
from jax.sharding import PartitionSpec as P

TILE = 64
LANES = 128
AMP_SLOTS = 46
INT_SLOTS = 160
VMEM_LIMIT = 60 * 1024 * 1024
NO_COST = pl.CostEstimate(flops=1024, bytes_accessed=1024, transcendentals=0)


def tile_mask(mask_tiles, row_start, row_count, tile_size):
    tile_count = mask_tiles.shape[-1]
    row_tiles = (row_start + jnp.arange(row_count, dtype=jnp.int32)) // tile_size
    select = (row_tiles[:, None] == jnp.arange(tile_count, dtype=jnp.int32)[None, :]).astype(
        jnp.float32
    )
    picked = jnp.einsum("ra,...ac->...rc", select, mask_tiles.astype(jnp.float32))
    return jnp.repeat(picked, tile_size, axis=-1)


def cycle_terms(combined, gathered):
    direct_term = jnp.einsum(
        "ikac,kjcb->iajb", combined, gathered, preferred_element_type=jnp.float32
    )
    swapped_term = jnp.einsum(
        "ikac,kjbc->iajb", combined, gathered, preferred_element_type=jnp.float32
    )
    return 2.0 * direct_term - swapped_term


def dense_shards(amplitudes, integrals, amp_mask, int_mask, eps_slab, eps_pair, eps_vir):
    row_count = amplitudes.shape[2]
    half_count = amplitudes.shape[1]
    pair_count = integrals.shape[1]
    row_start = lax.axis_index("vir") * row_count
    k_start = lax.axis_index("rep") * half_count
    j_start = lax.axis_index("occ") * pair_count
    zero_index = jnp.zeros((), jnp.int32)
    k_masks = lax.dynamic_slice_in_dim(amp_mask, k_start, half_count, 0)
    screened = (
        amplitudes.astype(jnp.float32) * tile_mask(k_masks, row_start, row_count, TILE)[None]
    ).astype(jnp.bfloat16)
    received = lax.all_to_all(screened, "vir", split_axis=3, concat_axis=2, tiled=True)
    combined = (
        2.0 * screened.astype(jnp.float32) - jnp.swapaxes(received, 2, 3).astype(jnp.float32)
    ).astype(jnp.bfloat16)
    pair_masks = lax.dynamic_slice(
        int_mask,
        (k_start, j_start, zero_index, zero_index),
        (half_count, pair_count, int_mask.shape[2], int_mask.shape[3]),
    )
    kept_local = (
        integrals.astype(jnp.float32) * tile_mask(pair_masks, row_start, row_count, TILE)
    ).astype(jnp.bfloat16)
    gathered = lax.all_gather(kept_local, "vir", axis=2, tiled=True)
    partial_cycle = cycle_terms(combined, gathered)
    cycle = lax.psum_scatter(partial_cycle, "rep", scatter_dimension=2, tiled=True)
    row_energy = lax.dynamic_slice_in_dim(eps_vir, row_start, row_count, 0)
    denominator = (
        row_energy[None, :, None, None]
        + eps_vir[None, None, None, :]
        - eps_slab[:, None, None, None]
        - eps_pair[None, None, :, None]
    )
    return cycle / denominator


def low_lanes(rows):
    return lax.broadcasted_iota(jnp.int32, (rows, LANES), 1) < TILE


def swap_halves(block):
    return pltpu.roll(block, TILE, 1)


def fill(buf, choices):
    for chosen, ref in choices:

        @pl.when(chosen)
        def _(ref=ref):
            pltpu.sync_copy(ref, buf)


def pack_int_kernel(meta, mask, own_ref, oth_ref, out_ref):
    v, r, j = meta[0], meta[2], meta[3]
    low = low_lanes(32)
    count = jnp.int32(0)
    for half in range(2):

        def body(n, count, half=half):
            kk, ap = n // 2, n % 2
            k = lax.rem(kk + 2 * half + 2 * r, 4)
            for cp in range(8):
                for a2 in range(2):
                    row = pl.multiple_of(ap * 128 + a2 * TILE, TILE)
                    if half == 0:
                        block = own_ref[kk, r, pl.ds(row, TILE), cp * LANES : (cp + 1) * LANES]
                    else:
                        block = oth_ref[kk, r, pl.ds(row, TILE), cp * LANES : (cp + 1) * LANES]
                    top, bottom = block[:32], block[32:]
                    turned_top, turned_bottom = swap_halves(top), swap_halves(bottom)
                    at_row = 4 * v + 2 * ap + a2
                    out_ref[jnp.minimum(count, INT_SLOTS - 1)] = jnp.where(low, top, turned_bottom)
                    count = count + mask[k, j, at_row, 2 * cp]
                    out_ref[jnp.minimum(count, INT_SLOTS - 1)] = jnp.where(low, turned_top, bottom)
                    count = count + mask[k, j, at_row, 2 * cp + 1]
            return count

        count = lax.fori_loop(0, 4, body, count)


def pack_amp_kernel(meta, mask, own_ref, oth_ref, *out_refs):
    v, r = meta[0], meta[2]
    low = low_lanes(TILE)
    for d in range(1, 4):
        dest = v ^ d
        count = jnp.int32(0)
        for half in range(2):
            ref = own_ref if half == 0 else oth_ref

            def body(kk, count, d=d, dest=dest, half=half, ref=ref):
                k = lax.rem(kk + 2 * half + 2 * r, 4)
                for ap in range(2):
                    for cp in range(2):
                        col = pl.multiple_of(dest * 256 + cp * LANES, LANES)
                        tiles = []
                        for a2 in range(2):
                            row = ap * 128 + a2 * TILE
                            x0 = ref[0, 0, 0, kk, row : row + TILE, pl.ds(col, LANES)]
                            x1 = ref[0, 0, 1, kk, row : row + TILE, pl.ds(col, LANES)]
                            tiles.append(
                                (jnp.where(low, x0, swap_halves(x1)), jnp.where(low, swap_halves(x0), x1))
                            )
                        for c2 in range(2):
                            for a2 in range(2):
                                out_refs[d - 1][jnp.minimum(count, AMP_SLOTS - 1)] = tiles[a2][c2]
                                count = count + mask[k, 4 * v + 2 * ap + a2, 4 * dest + 2 * cp + c2]
                return count

            count = lax.fori_loop(0, 2, body, count)


def unpack_group(buf_ref, mask, k, j, s, ap, count, d_ref, t_ref, at):
    low = low_lanes(32)
    zero = jnp.zeros((32, LANES), jnp.bfloat16)
    row = pl.multiple_of(ap * 128, 128)
    for cp in range(8):
        parts = []
        for a2 in range(2):
            at_row = 4 * s + 2 * ap + a2
            m0, m1 = mask[k, j, at_row, 2 * cp], mask[k, j, at_row, 2 * cp + 1]
            y0 = buf_ref[jnp.minimum(count, INT_SLOTS - 1)]
            count = count + m0
            y1 = buf_ref[jnp.minimum(count, INT_SLOTS - 1)]
            count = count + m1
            y0 = jnp.where(m0 > 0, y0, zero)
            y1 = jnp.where(m1 > 0, y1, zero)
            parts.append(jnp.where(low, y0, swap_halves(y1)))
            parts.append(jnp.where(low, swap_halves(y0), y1))
        block = jnp.concatenate(parts, axis=0)
        d_ref[at, pl.ds(row, 128), cp * LANES : (cp + 1) * LANES] = block
        t_ref[at, cp * LANES : (cp + 1) * LANES, pl.ds(row, 128)] = block.T
    return count


def unpack_int_kernel(d, meta, mask, *refs):
    sources, (d_ref, t_ref, buf_ref, count_ref) = refs[:-4], refs[-4:]
    v, r, j = meta[0], meta[2], meta[3]
    kk = pl.program_id(0)
    k = lax.rem(kk + 2 * r, 4)
    s = v ^ d

    @pl.when(kk == 0)
    def _():
        count_ref[0] = 0
        if d < 3:
            fill(buf_ref, [(s > v, sources[0]), (s < v, sources[1])])
        else:
            fill(buf_ref, [(v == n, source) for n, source in enumerate(sources)])

    count_ref[0] = lax.fori_loop(
        0,
        2,
        lambda ap, count: unpack_group(buf_ref, mask, k, j, s, ap, count, d_ref, t_ref, 0),
        count_ref[0],
    )


def own_int_kernel(meta, mask, own_ref, oth_ref, d_ref, t_ref):
    v, r, j = meta[0], meta[2], meta[3]
    kk = pl.program_id(0)
    k = lax.rem(kk + 2 * r, 4)
    low = low_lanes(TILE)
    zero = jnp.zeros((TILE, LANES), jnp.bfloat16)

    def body(ap, carry):
        for cp in range(8):
            parts = []
            for a2 in range(2):
                at_row = 4 * v + 2 * ap + a2
                row = pl.multiple_of(ap * 128 + a2 * TILE, TILE)
                m0, m1 = mask[k, j, at_row, 2 * cp], mask[k, j, at_row, 2 * cp + 1]
                block = jnp.where(
                    kk < 2,
                    own_ref[0, 0, pl.ds(row, TILE), cp * LANES : (cp + 1) * LANES],
                    oth_ref[0, 0, pl.ds(row, TILE), cp * LANES : (cp + 1) * LANES],
                )
                parts.append(
                    jnp.where(low, jnp.where(m0 > 0, block, zero), jnp.where(m1 > 0, block, zero))
                )
            block = jnp.concatenate(parts, axis=0)
            row = pl.multiple_of(ap * 128, 128)
            d_ref[0, pl.ds(row, 128), cp * LANES : (cp + 1) * LANES] = block
            t_ref[0, cp * LANES : (cp + 1) * LANES, pl.ds(row, 128)] = block.T
        return carry

    lax.fori_loop(0, 2, body, 0)


def lane_scale(m0, m1, value):
    lane = lax.broadcasted_iota(jnp.int32, (1, LANES), 1)
    return value * jnp.where(lane < TILE, m0, m1).astype(jnp.float32)


def combine_kernel(d, base, meta, mask, own_ref, oth_ref, near_ref, far_ref, *refs):
    if d == 3:
        out_ref, count_ref = refs[-2:]
    else:
        out_ref, count_ref = refs[1:]
    v, x, r = meta[0], meta[1], meta[2]
    kk = pl.program_id(0) + base
    k = lax.rem(kk + 2 * r, 4)
    s = v ^ d
    zero = jnp.zeros((TILE, LANES), jnp.bfloat16)

    @pl.when(pl.program_id(0) == 0)
    def _():
        count_ref[0] = 0 if base == 0 else refs[0][0]

    def body(ap, count):
        ccol = pl.multiple_of(ap * 128, 128)
        for c in range(4):
            arow = c * TILE
            slots, kept = [], []
            for a2 in range(2):
                m = mask[k, 4 * s + 2 * ap + a2, 4 * v + c]
                slots.append(jnp.minimum(count, AMP_SLOTS - 1))
                kept.append(m)
                count = count + m
            own_scale = lane_scale(
                mask[k, 4 * v + c, 4 * s + 2 * ap], mask[k, 4 * v + c, 4 * s + 2 * ap + 1], 2.0
            )
            for xx, buf in ((x, near_ref), (1 - x, far_ref)):
                stacked = jnp.concatenate(
                    [jnp.where(kept[a2] > 0, buf[slots[a2]], zero) for a2 in range(2)], axis=0
                )
                turned = stacked.T.astype(jnp.float32)
                for ii in range(2):
                    local = jnp.where(
                        kk < 2,
                        own_ref[xx, 0, ii, 0, pl.ds(arow, TILE), pl.ds(ccol, 128)],
                        oth_ref[xx, 0, ii, 0, pl.ds(arow, TILE), pl.ds(ccol, 128)],
                    ).astype(jnp.float32)
                    value = own_scale * local - turned[ii * TILE : (ii + 1) * TILE]
                    out_ref[0, xx, ii, pl.ds(arow, TILE), pl.ds(ccol, 128)] = value.astype(jnp.bfloat16)
        return count

    count_ref[0] = lax.fori_loop(0, 2, body, count_ref[0])


def diagonal_kernel(meta, mask, own_ref, oth_ref, out_ref):
    v, r = meta[0], meta[2]
    kk = pl.program_id(0)
    k = lax.rem(kk + 2 * r, 4)

    def screened(xx, ii, a0, c0):
        rows = []
        for a2 in range(2):
            start = a0 * 128 + a2 * TILE
            block = jnp.where(
                kk < 2,
                own_ref[xx, 0, ii, 0, start : start + TILE, c0 * 128 : (c0 + 1) * 128],
                oth_ref[xx, 0, ii, 0, start : start + TILE, c0 * 128 : (c0 + 1) * 128],
            ).astype(jnp.float32)
            at_row = 4 * v + 2 * a0 + a2
            rows.append(
                block
                * lane_scale(
                    mask[k, at_row, 4 * v + 2 * c0], mask[k, at_row, 4 * v + 2 * c0 + 1], 1.0
                )
            )
        return jnp.concatenate(rows, axis=0)

    for xx in range(2):
        for ii in range(2):
            for a0 in range(2):
                for c0 in range(2):
                    value = 2.0 * screened(xx, ii, a0, c0) - screened(xx, ii, c0, a0).T
                    out_ref[0, xx, ii, a0 * 128 : (a0 + 1) * 128, c0 * 128 : (c0 + 1) * 128] = (
                        value.astype(jnp.bfloat16)
                    )


def folded(direct, swapped):
    return (2.0 * direct.astype(jnp.float32) - swapped.astype(jnp.float32)).astype(jnp.bfloat16)


def fold_kernel(meta, *refs):
    direct, swapped, w_ref = refs[:3], refs[3:6], refs[6]
    v = meta[0]
    for q in range(3):
        for p in range(3):
            col = pl.multiple_of((v ^ p) * 256, 256)
            row = pl.multiple_of((v ^ q) * 256, 256)
            w_ref[q, :, p * 256 : (p + 1) * 256] = folded(
                direct[q][0, :, pl.ds(col, 256)], swapped[p][0, pl.ds(row, 256), :]
            )


def early_kernel(meta, w_ref, *refs):
    blocks, out_ref = refs[:3], refs[-1]
    total = jnp.dot(
        blocks[0][...].reshape(512, 1024), w_ref[0], preferred_element_type=jnp.float32
    )
    for q in range(1, 3):
        total += jnp.dot(
            blocks[q][...].reshape(512, 1024), w_ref[q], preferred_element_type=jnp.float32
        )
    out_ref[...] = total


def late_kernel(meta, *refs):
    direct, swapped, own, oth = refs[:4], refs[4:8], refs[8:11], refs[11:14]
    row_ref, out_ref, col_ref = refs[14:]
    v = meta[0]
    g = pl.program_id(0)
    last_at = pl.multiple_of((v ^ 3) * 256, 256)

    for p in range(4):
        at = pl.multiple_of((v ^ p) * 256, 256)
        row_ref[:, p * 256 : (p + 1) * 256] = folded(
            direct[3][g, :, pl.ds(at, 256)],
            swapped[p][g] if p < 3 else swapped[3][g, pl.ds(last_at, 256), :],
        )

    @pl.when(g == 0)
    def _():
        for p in range(3):
            at = pl.multiple_of((v ^ p) * 256, 256)
            for k in range(4):
                col_ref[p, k * 256 : (k + 1) * 256, :] = folded(
                    direct[p][k], swapped[3][k, pl.ds(at, 256), :]
                )

    def work(blocks):
        total = jnp.dot(
            blocks[0][...].reshape(512, 1024), col_ref[0], preferred_element_type=jnp.float32
        )
        for q in range(1, 3):
            total += jnp.dot(
                blocks[q][...].reshape(512, 1024), col_ref[q], preferred_element_type=jnp.float32
            )
        out_ref[...] = total

    @pl.when(g < 2)
    def _():
        work(own)

    @pl.when(g >= 2)
    def _():
        work(oth)


def tail_kernel(meta, eps_slab, eps_pair, eps_rows, eps_cols, part_ref, late_ref, row_ref, *refs):
    own, oth, out_ref = refs[:2], refs[2:4], refs[4]
    flat_ref = out_ref.reshape(4096, 128)
    v, r = meta[0], meta[2]
    g = pl.program_id(0)

    def work(blocks, i, k0):
        total = jnp.float32(0)
        for half in range(2):
            at = pl.multiple_of(256 * lax.rem(k0 + 2 * half, 4), 512)
            total += jnp.dot(
                blocks[half][...].reshape(512, 512),
                row_ref[pl.ds(at, 512), :],
                preferred_element_type=jnp.float32,
            )
        for p in range(4):
            s = v ^ p
            before = late_ref[...] if p == 3 else part_ref[:, p * 256 : (p + 1) * 256]
            value = total[:, p * 256 : (p + 1) * 256] + before
            cols = eps_cols[:, pl.ds(pl.multiple_of(s * 256, 256), 256)]
            for ii in range(2):
                energy = (eps_rows[...] + cols) - eps_slab[i + ii] - eps_pair[0]
                done = value[ii * 256 : (ii + 1) * 256] / energy
                for n in range(2):
                    flat_ref[pl.ds(ii * 2048 + 2 * s + n, 256, stride=8), :] = done[
                        :, n * 128 : (n + 1) * 128
                    ]

    @pl.when(g < 2)
    def _():
        work(own, 4 * g + 2 * r, 2 * r)

    @pl.when(g >= 2)
    def _():
        work(oth, 4 * (g - 2) + 2 * (1 - r), 2 * (1 - r))


def smem():
    return pl.BlockSpec(memory_space=pltpu.SMEM)


def whole():
    return pl.BlockSpec(memory_space=pltpu.VMEM)


def anywhere():
    return pl.BlockSpec(memory_space=pl.ANY)


def params():
    return pltpu.CompilerParams(vmem_limit_bytes=VMEM_LIMIT)


def as_is(array):
    def kernel(from_ref, to_ref):
        pltpu.sync_copy(from_ref, to_ref)

    return pl.pallas_call(
        kernel,
        out_shape=jax.ShapeDtypeStruct(array.shape, array.dtype),
        in_specs=[anywhere()],
        out_specs=anywhere(),
        name="as_is",
    )(array)


def k_place(kk, r):
    return lax.rem(kk + 2 * r, 4)


def packed_shards(amplitudes, integrals, amp_mask, int_mask, eps_slab, eps_pair, eps_vir):
    v, x, r = lax.axis_index("vir"), lax.axis_index("occ"), lax.axis_index("rep")
    meta = jnp.stack([v, x, r, 2 * x + r]).astype(jnp.int32)
    swap = [(0, 1), (1, 0)]
    bf16 = jnp.bfloat16

    pairs = amp_mask.reshape(4, 4, 4, 4, 4).sum((0, 2, 4))
    pairs = jnp.where(jnp.eye(4, dtype=bool), 0, pairs)
    pieces = int_mask.reshape(4, 4, 4, 4, 16).sum((0, 3, 4))
    over = jnp.logical_or(jnp.max(pairs) > AMP_SLOTS - 1, jnp.max(pieces) > INT_SLOTS - 1)
    over = over.astype(jnp.int32).reshape(1)

    int_oth = lax.ppermute(integrals, "rep", swap)
    amps = amplitudes.reshape(2, 2, 2, 2, 256, 1024)
    int_oth, later = lax.optimization_barrier((int_oth, amps))
    amp_oth = lax.ppermute(later, "rep", swap)

    packed_int = pl.pallas_call(
        pack_int_kernel,
        out_shape=jax.ShapeDtypeStruct((INT_SLOTS, 32, LANES), bf16),
        in_specs=[smem(), smem(), whole(), whole()],
        out_specs=whole(),
        compiler_params=params(),
        cost_estimate=NO_COST,
        name="pack_int",
    )(meta, int_mask, integrals, int_oth)

    up1 = lax.ppermute(packed_int, "vir", [(0, 1), (1, 2), (2, 3)])
    down1 = lax.ppermute(packed_int, "vir", [(1, 0), (2, 1), (3, 2)])

    packed_amp = pl.pallas_call(
        pack_amp_kernel,
        grid_spec=pltpu.PrefetchScalarGridSpec(
            num_scalar_prefetch=2,
            grid=(1,),
            in_specs=[
                pl.BlockSpec((1, 1, 2, 2, 256, 1024), lambda g, meta, mask: (meta[1], meta[2], 0, 0, 0, 0)),
                pl.BlockSpec((1, 1, 2, 2, 256, 1024), lambda g, meta, mask: (meta[1], meta[2], 0, 0, 0, 0)),
            ],
            out_specs=[pl.BlockSpec((AMP_SLOTS, TILE, LANES), lambda g, meta, mask: (0, 0, 0))] * 3,
        ),
        out_shape=[jax.ShapeDtypeStruct((AMP_SLOTS, TILE, LANES), bf16)] * 3,
        compiler_params=params(),
        cost_estimate=NO_COST,
        name="pack_amp",
    )(meta, amp_mask, amps, amp_oth)

    def across(d, packed):
        return lax.ppermute(packed, "vir", [(s, s ^ d) for s in range(4)])

    packed3, over = lax.optimization_barrier((packed_amp[2], over))
    over = over + lax.ppermute(over, "frag", swap)

    int_shapes = [
        jax.ShapeDtypeStruct((4, 256, 1024), bf16),
        jax.ShapeDtypeStruct((4, 1024, 256), bf16),
    ]
    int_outs = [
        pl.BlockSpec((1, 256, 1024), lambda kk, meta, mask: (k_place(kk, meta[2]), 0, 0)),
        pl.BlockSpec((1, 1024, 256), lambda kk, meta, mask: (k_place(kk, meta[2]), 0, 0)),
    ]
    def unpack(d, *operands):
        if d == 0:
            kernel, scratch = own_int_kernel, []
            specs = [
                pl.BlockSpec((1, 1, 256, 1024), lambda kk, meta, mask: (jnp.minimum(kk, 1), meta[2], 0, 0)),
                pl.BlockSpec((1, 1, 256, 1024), lambda kk, meta, mask: (jnp.maximum(kk - 2, 0), meta[2], 0, 0)),
            ]
        else:
            kernel = functools.partial(unpack_int_kernel, d)
            scratch = [pltpu.VMEM((INT_SLOTS, 32, LANES), bf16), pltpu.SMEM((1,), jnp.int32)]
            specs = [anywhere() for _ in operands]
        return pl.pallas_call(
            kernel,
            grid_spec=pltpu.PrefetchScalarGridSpec(
                num_scalar_prefetch=2, grid=(4,), in_specs=specs, out_specs=int_outs, scratch_shapes=scratch
            ),
            out_shape=int_shapes,
            compiler_params=params(),
            cost_estimate=NO_COST,
            name=f"ints_{d}",
        )(meta, int_mask, *operands)

    def local_specs(d, base):
        def at(side):
            def place(kk, meta, mask):
                k = jnp.minimum(kk + base, 1) if side == 0 else jnp.maximum(kk + base - 2, 0)
                return (0, meta[2], 0, k, 0, meta[0] ^ d)

            return place

        return [pl.BlockSpec((2, 1, 2, 1, 256, 256), at(side)) for side in range(2)]

    def combine(d, base, near, far, steps, extra_specs, extra, out_specs, out_shape, aliases, scratch):
        kernel = diagonal_kernel if d == 0 else functools.partial(combine_kernel, d, base)
        specs, operands = [], ()
        if d > 0:
            specs = [pl.BlockSpec((AMP_SLOTS, TILE, LANES), lambda kk, meta, mask: (0, 0, 0))] * 2
            operands = (near, far)
        return pl.pallas_call(
            kernel,
            grid_spec=pltpu.PrefetchScalarGridSpec(
                num_scalar_prefetch=2,
                grid=(steps,),
                in_specs=local_specs(d, base) + specs + extra_specs,
                out_specs=out_specs,
                scratch_shapes=scratch,
            ),
            out_shape=out_shape,
            input_output_aliases=aliases,
            compiler_params=params(),
            cost_estimate=NO_COST,
            name=f"combine_{d}_{base}",
        )(meta, amp_mask, amps, amp_oth, *operands, *extra)

    def combine_first(d, near, far, sofar):
        return combine(
            d,
            0,
            near,
            far,
            4,
            [] if d == 0 else [anywhere()],
            () if d == 0 else (sofar,),
            pl.BlockSpec(
                (1, 2, 2, 256, 256), lambda kk, meta, mask: (d, 0, 0, 0, k_place(kk, meta[2]))
            ),
            jax.ShapeDtypeStruct((3, 2, 2, 256, 1024), bf16),
            {} if d == 0 else {6: 0},
            [] if d == 0 else [pltpu.SMEM((1,), jnp.int32)],
        )

    def combine_half(base, near, far, *count):
        return combine(
            3,
            base,
            near,
            far,
            2,
            [smem() for _ in count],
            count,
            [pl.BlockSpec((1, 2, 2, 256, 256), lambda kk, meta, mask: (0, 0, 0, 0, kk)), smem()],
            [jax.ShapeDtypeStruct((1, 2, 2, 256, 512), bf16), jax.ShapeDtypeStruct((1,), jnp.int32)],
            {},
            [],
        )

    ready = lax.optimization_barrier
    ints = [unpack(0, integrals, int_oth)]
    first = combine_first(0, None, None, None)
    near1, near2 = across(1, packed_amp[0]), across(2, packed_amp[1])
    up1, down1, over, ints[0], first = ready((up1, down1, over, ints[0], first))
    up2 = lax.ppermute(up1, "vir", [(1, 2), (2, 3)])
    down2 = lax.ppermute(down1, "vir", [(1, 0), (2, 1)])
    far1, far2 = lax.ppermute(near1, "occ", swap), lax.ppermute(near2, "occ", swap)
    ints.append(unpack(1, down1, up1))
    ints[1], far1 = ready((ints[1], far1))
    first = combine_first(1, near1, far1, first)
    first = combine_first(2, near2, far2, first)
    near3 = across(3, packed3)
    up2, down2, first = ready((up2, down2, first))
    ints.append(unpack(2, down2, up2))
    folded_w = pl.pallas_call(
        fold_kernel,
        grid_spec=pltpu.PrefetchScalarGridSpec(
            num_scalar_prefetch=1,
            grid=(4,),
            in_specs=[pl.BlockSpec((1, 256, 1024), lambda k, meta: (k, 0, 0))] * 3
            + [pl.BlockSpec((1, 1024, 256), lambda k, meta: (k, 0, 0))] * 3,
            out_specs=pl.BlockSpec((3, 256, 768), lambda k, meta: (0, k, 0)),
        ),
        out_shape=jax.ShapeDtypeStruct((3, 1024, 768), bf16),
        compiler_params=params(),
        cost_estimate=NO_COST,
        name="fold",
    )(meta, *[d for d, _ in ints], *[t for _, t in ints])
    up2, down2, near3, first, folded_w = ready((up2, down2, near3, first, folded_w))
    end_down = lax.ppermute(down2, "vir", [(1, 0)])
    end_up = lax.ppermute(up2, "vir", [(2, 3)])
    first_oth = lax.ppermute(first, "rep", swap)

    def own_at(d, width=1024):
        return pl.BlockSpec((1, 1, 2, 256, width), lambda g, *_: (d % 3, jnp.minimum(g, 1), 0, 0, 0))

    def oth_at(d, width=1024):
        return pl.BlockSpec((1, 1, 2, 256, width), lambda g, *_: (d % 3, jnp.maximum(g - 2, 0), 0, 0, 0))

    def place(g, meta, *_):
        return (2 * (g % 2) + jnp.where(g < 2, meta[2], 1 - meta[2]), 0)

    once = pl.Buffered(1)
    def early(c, other, *sofar):
        def at(d):
            return pl.BlockSpec((1, 1, 2, 256, 1024), lambda g, *_: (d, g, 0, 0, 0))

        return pl.pallas_call(
            early_kernel,
            grid_spec=pltpu.PrefetchScalarGridSpec(
                num_scalar_prefetch=1,
                grid=(2,),
                in_specs=[pl.BlockSpec((3, 1024, 768), lambda g, *_: (0, 0, 0), pipeline_mode=once)]
                + [at(d) for d in range(3)]
                + [anywhere() for _ in sofar],
                out_specs=pl.BlockSpec((512, 768), lambda g, meta: place(g + 2 * other, meta)),
            ),
            out_shape=jax.ShapeDtypeStruct((2048, 768), jnp.float32),
            input_output_aliases={5: 0} if sofar else {},
            compiler_params=params(),
            cost_estimate=NO_COST,
            name=f"early_{other}",
        )(meta, folded_w, c, c, c, *sofar)

    part = early(first_oth, 1, early(first, 0))

    far3 = lax.ppermute(near3, "occ", swap)
    far3, part = ready((far3, part))
    half0, count = combine_half(0, near3, far3)
    half1, _ = combine_half(2, near3, far3, count)
    halves = (half0, half1)
    halves_oth = tuple(lax.ppermute(h, "rep", swap) for h in halves)
    end_down, end_up, half1 = ready((end_down, end_up, half1))
    ints.append(unpack(3, end_down, down1, up1, end_up))
    rows, cols = [d for d, _ in ints], [t for _, t in ints]
    last_row, late = pl.pallas_call(
        late_kernel,
        grid_spec=pltpu.PrefetchScalarGridSpec(
            num_scalar_prefetch=1,
            grid=(4,),
            in_specs=[pl.BlockSpec((4, 256, 256), lambda g, meta: (0, 0, meta[0] ^ 3), pipeline_mode=once)] * 3
            + [pl.BlockSpec((4, 256, 1024), lambda g, meta: (0, 0, 0), pipeline_mode=once)]
            + [pl.BlockSpec((4, 256, 256), lambda g, meta: (0, meta[0] ^ 3, 0), pipeline_mode=once)] * 3
            + [pl.BlockSpec((4, 1024, 256), lambda g, meta: (0, 0, 0), pipeline_mode=once)]
            + [own_at(d) for d in range(3)]
            + [oth_at(d) for d in range(3)],
            out_specs=[
                pl.BlockSpec((256, 1024), lambda g, meta: (g, 0)),
                pl.BlockSpec((512, 256), place),
            ],
            scratch_shapes=[pltpu.VMEM((3, 1024, 256), bf16)],
        ),
        out_shape=[
            jax.ShapeDtypeStruct((1024, 1024), bf16),
            jax.ShapeDtypeStruct((2048, 256), jnp.float32),
        ],
        compiler_params=params(),
        cost_estimate=NO_COST,
        name="late",
    )(meta, *rows, *cols, *[first] * 3, *[first_oth] * 3)
    row_energy = lax.dynamic_slice_in_dim(eps_vir, v * 256, 256, 0).reshape(256, 1)
    col_energy = eps_vir.reshape(1, 1024)

    def finish(ops):
        part, late, last_row, own, oth = ops
        return pl.pallas_call(
            tail_kernel,
            grid_spec=pltpu.PrefetchScalarGridSpec(
                num_scalar_prefetch=3,
                grid=(4,),
                in_specs=[
                    pl.BlockSpec((256, 1), lambda g, *_: (0, 0)),
                    pl.BlockSpec((1, 1024), lambda g, *_: (0, 0)),
                    pl.BlockSpec((512, 768), place),
                    pl.BlockSpec((512, 256), place),
                    pl.BlockSpec((1024, 1024), lambda g, *_: (0, 0), pipeline_mode=once),
                ]
                + [own_at(3, 512)] * 2
                + [oth_at(3, 512)] * 2,
                out_specs=pl.BlockSpec((2, 256, 1, 1024), lambda g, meta, *_: (*place(g, meta), 0, 0)),
            ),
            out_shape=jax.ShapeDtypeStruct((8, 256, 1, 1024), jnp.float32),
            compiler_params=params(),
            cost_estimate=NO_COST,
            name="tail",
        )(meta, eps_slab, eps_pair, row_energy, col_energy, part, late, last_row, *own, *oth)

    def dense(state):
        out = dense_shards(
            as_is(amplitudes), as_is(integrals), amp_mask, int_mask, eps_slab, eps_pair, eps_vir
        )
        return as_is(out), jnp.zeros((), jnp.int32)

    out = finish((part, late, last_row, halves, halves_oth))
    return lax.while_loop(lambda state: state[1] > 0, dense, (out, over[0]))[0]


def shards(sizes, *args):
    amplitudes, integrals, amp_mask, int_mask = args[:4]
    fits = (
        sizes == {"frag": 2, "vir": 4, "occ": 2, "rep": 2}
        and amplitudes.shape == (8, 2, 256, 1024)
        and integrals.shape == (2, 2, 256, 1024)
        and amp_mask.shape == (4, 16, 16)
        and int_mask.shape == (4, 4, 16, 16)
    )
    return packed_shards(*args) if fits else dense_shards(*args)


def solution(mesh):
    in_specs = (
        P("frag", "rep", "vir", None),
        P(("frag", "rep"), "occ", "vir", None),
        P("frag", None, None),
        P("frag", None, None, None),
        P("frag"),
        P(("frag", "occ", "rep")),
        P("frag"),
    )
    out_specs = P("frag", "vir", ("occ", "rep"), None)
    return jax.shard_map(
        functools.partial(shards, dict(mesh.shape)),
        mesh=mesh,
        in_specs=in_specs,
        out_specs=out_specs,
        check_vma=False,
    )
```

```python
import functools

import jax
import jax.numpy as jnp
from jax import lax
from jax.experimental import pallas as pl
from jax.experimental.pallas import tpu as pltpu
from jax.sharding import PartitionSpec as P

TILE = 64
LANES = 128
AMP_SLOTS = 48
INT_SLOTS = 160
VMEM_LIMIT = 60 * 1024 * 1024
NO_COST = pl.CostEstimate(flops=1024, bytes_accessed=1024, transcendentals=0)


def tile_mask(mask_tiles, row_start, row_count, tile_size):
    tile_count = mask_tiles.shape[-1]
    row_tiles = (row_start + jnp.arange(row_count, dtype=jnp.int32)) // tile_size
    select = (row_tiles[:, None] == jnp.arange(tile_count, dtype=jnp.int32)[None, :]).astype(
        jnp.float32
    )
    picked = jnp.einsum("ra,...ac->...rc", select, mask_tiles.astype(jnp.float32))
    return jnp.repeat(picked, tile_size, axis=-1)


def cycle_terms(combined, gathered):
    direct_term = jnp.einsum(
        "ikac,kjcb->iajb", combined, gathered, preferred_element_type=jnp.float32
    )
    swapped_term = jnp.einsum(
        "ikac,kjbc->iajb", combined, gathered, preferred_element_type=jnp.float32
    )
    return 2.0 * direct_term - swapped_term


def dense_shards(amplitudes, integrals, amp_mask, int_mask, eps_slab, eps_pair, eps_vir):
    row_count = amplitudes.shape[2]
    half_count = amplitudes.shape[1]
    pair_count = integrals.shape[1]
    row_start = lax.axis_index("vir") * row_count
    k_start = lax.axis_index("rep") * half_count
    j_start = lax.axis_index("occ") * pair_count
    zero_index = jnp.zeros((), jnp.int32)
    k_masks = lax.dynamic_slice_in_dim(amp_mask, k_start, half_count, 0)
    screened = (
        amplitudes.astype(jnp.float32) * tile_mask(k_masks, row_start, row_count, TILE)[None]
    ).astype(jnp.bfloat16)
    received = lax.all_to_all(screened, "vir", split_axis=3, concat_axis=2, tiled=True)
    combined = (
        2.0 * screened.astype(jnp.float32) - jnp.swapaxes(received, 2, 3).astype(jnp.float32)
    ).astype(jnp.bfloat16)
    pair_masks = lax.dynamic_slice(
        int_mask,
        (k_start, j_start, zero_index, zero_index),
        (half_count, pair_count, int_mask.shape[2], int_mask.shape[3]),
    )
    kept_local = (
        integrals.astype(jnp.float32) * tile_mask(pair_masks, row_start, row_count, TILE)
    ).astype(jnp.bfloat16)
    gathered = lax.all_gather(kept_local, "vir", axis=2, tiled=True)
    partial_cycle = cycle_terms(combined, gathered)
    cycle = lax.psum_scatter(partial_cycle, "rep", scatter_dimension=2, tiled=True)
    row_energy = lax.dynamic_slice_in_dim(eps_vir, row_start, row_count, 0)
    denominator = (
        row_energy[None, :, None, None]
        + eps_vir[None, None, None, :]
        - eps_slab[:, None, None, None]
        - eps_pair[None, None, :, None]
    )
    return cycle / denominator


def low_lanes(rows):
    return lax.broadcasted_iota(jnp.int32, (rows, LANES), 1) < TILE


def swap_halves(block):
    return pltpu.roll(block, TILE, 1)


def fill(buf, choices):
    for chosen, ref in choices:

        @pl.when(chosen)
        def _(ref=ref):
            pltpu.sync_copy(ref, buf)


def pack_int_kernel(meta, mask, own_ref, oth_ref, out_ref):
    v, r, j = meta[0], meta[2], meta[3]
    low = low_lanes(32)
    count = jnp.int32(0)
    for half in range(2):

        def body(n, count, half=half):
            kk, ap = n // 2, n % 2
            k = lax.rem(kk + 2 * half + 2 * r, 4)
            for cp in range(8):
                for a2 in range(2):
                    row = pl.multiple_of(ap * 128 + a2 * TILE, TILE)
                    if half == 0:
                        block = own_ref[kk, r, pl.ds(row, TILE), cp * LANES : (cp + 1) * LANES]
                    else:
                        block = oth_ref[kk, r, pl.ds(row, TILE), cp * LANES : (cp + 1) * LANES]
                    top, bottom = block[:32], block[32:]
                    turned_top, turned_bottom = swap_halves(top), swap_halves(bottom)
                    at_row = 4 * v + 2 * ap + a2
                    out_ref[jnp.minimum(count, INT_SLOTS - 1)] = jnp.where(low, top, turned_bottom)
                    count = count + mask[k, j, at_row, 2 * cp]
                    out_ref[jnp.minimum(count, INT_SLOTS - 1)] = jnp.where(low, turned_top, bottom)
                    count = count + mask[k, j, at_row, 2 * cp + 1]
            return count

        count = lax.fori_loop(0, 4, body, count)


def pack_amp_kernel(meta, mask, own_ref, oth_ref, *out_refs):
    v, r = meta[0], meta[2]
    low = low_lanes(TILE)
    for d in range(1, 4):
        dest = v ^ d
        count = jnp.int32(0)
        for half in range(2):
            ref = own_ref if half == 0 else oth_ref

            def body(kk, count, d=d, dest=dest, half=half, ref=ref):
                k = lax.rem(kk + 2 * half + 2 * r, 4)
                for ap in range(2):
                    for cp in range(2):
                        col = pl.multiple_of(dest * 256 + cp * LANES, LANES)
                        tiles = []
                        for a2 in range(2):
                            row = ap * 128 + a2 * TILE
                            x0 = ref[0, 0, 0, kk, row : row + TILE, pl.ds(col, LANES)]
                            x1 = ref[0, 0, 1, kk, row : row + TILE, pl.ds(col, LANES)]
                            tiles.append(
                                (jnp.where(low, x0, swap_halves(x1)), jnp.where(low, swap_halves(x0), x1))
                            )
                        for c2 in range(2):
                            for a2 in range(2):
                                out_refs[d - 1][jnp.minimum(count, AMP_SLOTS - 1)] = tiles[a2][c2]
                                count = count + mask[k, 4 * v + 2 * ap + a2, 4 * dest + 2 * cp + c2]
                return count

            count = lax.fori_loop(0, 2, body, count)


def unpack_group(buf_ref, mask, k, j, s, ap, count, d_ref, t_ref, at):
    low = low_lanes(32)
    zero = jnp.zeros((32, LANES), jnp.bfloat16)
    row = pl.multiple_of(ap * 128, 128)
    for cp in range(8):
        parts = []
        for a2 in range(2):
            at_row = 4 * s + 2 * ap + a2
            m0, m1 = mask[k, j, at_row, 2 * cp], mask[k, j, at_row, 2 * cp + 1]
            y0 = buf_ref[jnp.minimum(count, INT_SLOTS - 1)]
            count = count + m0
            y1 = buf_ref[jnp.minimum(count, INT_SLOTS - 1)]
            count = count + m1
            y0 = jnp.where(m0 > 0, y0, zero)
            y1 = jnp.where(m1 > 0, y1, zero)
            parts.append(jnp.where(low, y0, swap_halves(y1)))
            parts.append(jnp.where(low, swap_halves(y0), y1))
        block = jnp.concatenate(parts, axis=0)
        d_ref[at, pl.ds(row, 128), cp * LANES : (cp + 1) * LANES] = block
        t_ref[at, cp * LANES : (cp + 1) * LANES, pl.ds(row, 128)] = block.T
    return count


def unpack_int_kernel(d, meta, mask, *refs):
    sources, (d_ref, t_ref, buf_ref, count_ref) = refs[:-4], refs[-4:]
    v, r, j = meta[0], meta[2], meta[3]
    kk = pl.program_id(0)
    k = lax.rem(kk + 2 * r, 4)
    s = v ^ d

    @pl.when(kk == 0)
    def _():
        count_ref[0] = 0
        if d < 3:
            fill(buf_ref, [(s > v, sources[0]), (s < v, sources[1])])
        else:
            fill(buf_ref, [(v == n, source) for n, source in enumerate(sources)])

    count_ref[0] = lax.fori_loop(
        0,
        2,
        lambda ap, count: unpack_group(buf_ref, mask, k, j, s, ap, count, d_ref, t_ref, 0),
        count_ref[0],
    )


def own_int_kernel(meta, mask, own_ref, oth_ref, d_ref, t_ref):
    v, r, j = meta[0], meta[2], meta[3]
    kk = pl.program_id(0)
    k = lax.rem(kk + 2 * r, 4)
    low = low_lanes(TILE)
    zero = jnp.zeros((TILE, LANES), jnp.bfloat16)

    def body(ap, carry):
        for cp in range(8):
            parts = []
            for a2 in range(2):
                at_row = 4 * v + 2 * ap + a2
                row = pl.multiple_of(ap * 128 + a2 * TILE, TILE)
                m0, m1 = mask[k, j, at_row, 2 * cp], mask[k, j, at_row, 2 * cp + 1]
                block = jnp.where(
                    kk < 2,
                    own_ref[0, 0, pl.ds(row, TILE), cp * LANES : (cp + 1) * LANES],
                    oth_ref[0, 0, pl.ds(row, TILE), cp * LANES : (cp + 1) * LANES],
                )
                parts.append(
                    jnp.where(low, jnp.where(m0 > 0, block, zero), jnp.where(m1 > 0, block, zero))
                )
            block = jnp.concatenate(parts, axis=0)
            row = pl.multiple_of(ap * 128, 128)
            d_ref[0, pl.ds(row, 128), cp * LANES : (cp + 1) * LANES] = block
            t_ref[0, cp * LANES : (cp + 1) * LANES, pl.ds(row, 128)] = block.T
        return carry

    lax.fori_loop(0, 2, body, 0)


def lane_scale(m0, m1, value):
    lane = lax.broadcasted_iota(jnp.int32, (1, LANES), 1)
    return value * jnp.where(lane < TILE, m0, m1).astype(jnp.float32)


def combine_kernel(d, base, meta, mask, own_ref, oth_ref, near_ref, far_ref, *refs):
    if d == 3:
        out_ref, count_ref = refs[-2:]
    else:
        out_ref, count_ref = refs[1:]
    v, x, r = meta[0], meta[1], meta[2]
    kk = pl.program_id(0) + base
    k = lax.rem(kk + 2 * r, 4)
    s = v ^ d
    zero = jnp.zeros((TILE, LANES), jnp.bfloat16)

    @pl.when(pl.program_id(0) == 0)
    def _():
        count_ref[0] = 0 if base == 0 else refs[0][0]

    def body(ap, count):
        ccol = pl.multiple_of(ap * 128, 128)
        for c in range(4):
            arow = c * TILE
            slots, kept = [], []
            for a2 in range(2):
                m = mask[k, 4 * s + 2 * ap + a2, 4 * v + c]
                slots.append(jnp.minimum(count, AMP_SLOTS - 1))
                kept.append(m)
                count = count + m
            own_scale = lane_scale(
                mask[k, 4 * v + c, 4 * s + 2 * ap], mask[k, 4 * v + c, 4 * s + 2 * ap + 1], 2.0
            )
            for xx, buf in ((x, near_ref), (1 - x, far_ref)):
                stacked = jnp.concatenate(
                    [jnp.where(kept[a2] > 0, buf[slots[a2]], zero) for a2 in range(2)], axis=0
                )
                turned = stacked.T.astype(jnp.float32)
                for ii in range(2):
                    local = jnp.where(
                        kk < 2,
                        own_ref[xx, 0, ii, 0, pl.ds(arow, TILE), pl.ds(ccol, 128)],
                        oth_ref[xx, 0, ii, 0, pl.ds(arow, TILE), pl.ds(ccol, 128)],
                    ).astype(jnp.float32)
                    value = own_scale * local - turned[ii * TILE : (ii + 1) * TILE]
                    out_ref[0, xx, ii, pl.ds(arow, TILE), pl.ds(ccol, 128)] = value.astype(jnp.bfloat16)
        return count

    count_ref[0] = lax.fori_loop(0, 2, body, count_ref[0])


def diagonal_kernel(meta, mask, own_ref, oth_ref, out_ref):
    v, r = meta[0], meta[2]
    kk = pl.program_id(0)
    k = lax.rem(kk + 2 * r, 4)

    def screened(xx, ii, a0, c0):
        rows = []
        for a2 in range(2):
            start = a0 * 128 + a2 * TILE
            block = jnp.where(
                kk < 2,
                own_ref[xx, 0, ii, 0, start : start + TILE, c0 * 128 : (c0 + 1) * 128],
                oth_ref[xx, 0, ii, 0, start : start + TILE, c0 * 128 : (c0 + 1) * 128],
            ).astype(jnp.float32)
            at_row = 4 * v + 2 * a0 + a2
            rows.append(
                block
                * lane_scale(
                    mask[k, at_row, 4 * v + 2 * c0], mask[k, at_row, 4 * v + 2 * c0 + 1], 1.0
                )
            )
        return jnp.concatenate(rows, axis=0)

    for xx in range(2):
        for ii in range(2):
            for a0 in range(2):
                for c0 in range(2):
                    value = 2.0 * screened(xx, ii, a0, c0) - screened(xx, ii, c0, a0).T
                    out_ref[0, xx, ii, a0 * 128 : (a0 + 1) * 128, c0 * 128 : (c0 + 1) * 128] = (
                        value.astype(jnp.bfloat16)
                    )


def folded(direct, swapped):
    return (2.0 * direct.astype(jnp.float32) - swapped.astype(jnp.float32)).astype(jnp.bfloat16)


def fold_kernel(meta, *refs):
    direct, swapped, w_ref = refs[:3], refs[3:6], refs[6]
    v = meta[0]
    for q in range(3):
        for p in range(3):
            col = pl.multiple_of((v ^ p) * 256, 256)
            row = pl.multiple_of((v ^ q) * 256, 256)
            w_ref[q, :, p * 256 : (p + 1) * 256] = folded(
                direct[q][0, :, pl.ds(col, 256)], swapped[p][0, pl.ds(row, 256), :]
            )


def early_kernel(meta, w_ref, *refs):
    blocks, out_ref = refs[:3], refs[-1]
    total = jnp.dot(
        blocks[0][...].reshape(512, 1024), w_ref[0], preferred_element_type=jnp.float32
    )
    for q in range(1, 3):
        total += jnp.dot(
            blocks[q][...].reshape(512, 1024), w_ref[q], preferred_element_type=jnp.float32
        )
    out_ref[...] = total


def late_kernel(meta, *refs):
    direct, swapped, own, oth = refs[:4], refs[4:8], refs[8:11], refs[11:14]
    row_ref, out_ref, col_ref = refs[14:]
    v = meta[0]
    g = pl.program_id(0)
    last_at = pl.multiple_of((v ^ 3) * 256, 256)

    for p in range(4):
        at = pl.multiple_of((v ^ p) * 256, 256)
        row_ref[:, p * 256 : (p + 1) * 256] = folded(
            direct[3][g, :, pl.ds(at, 256)],
            swapped[p][g] if p < 3 else swapped[3][g, pl.ds(last_at, 256), :],
        )

    @pl.when(g == 0)
    def _():
        for p in range(3):
            at = pl.multiple_of((v ^ p) * 256, 256)
            for k in range(4):
                col_ref[p, k * 256 : (k + 1) * 256, :] = folded(
                    direct[p][k], swapped[3][k, pl.ds(at, 256), :]
                )

    def work(blocks):
        total = jnp.dot(
            blocks[0][...].reshape(512, 1024), col_ref[0], preferred_element_type=jnp.float32
        )
        for q in range(1, 3):
            total += jnp.dot(
                blocks[q][...].reshape(512, 1024), col_ref[q], preferred_element_type=jnp.float32
            )
        out_ref[...] = total

    @pl.when(g < 2)
    def _():
        work(own)

    @pl.when(g >= 2)
    def _():
        work(oth)


def tail_kernel(meta, eps_slab, eps_pair, eps_rows, eps_cols, part_ref, late_ref, row_ref, *refs):
    own, oth, out_ref = refs[:2], refs[2:4], refs[4]
    flat_ref = out_ref.reshape(4096, 128)
    v, r = meta[0], meta[2]
    g = pl.program_id(0)

    def work(blocks, i, k0):
        total = jnp.float32(0)
        for half in range(2):
            at = pl.multiple_of(256 * lax.rem(k0 + 2 * half, 4), 512)
            total += jnp.dot(
                blocks[half][...].reshape(512, 512),
                row_ref[pl.ds(at, 512), :],
                preferred_element_type=jnp.float32,
            )
        for p in range(4):
            s = v ^ p
            before = late_ref[...] if p == 3 else part_ref[:, p * 256 : (p + 1) * 256]
            value = total[:, p * 256 : (p + 1) * 256] + before
            cols = eps_cols[:, pl.ds(pl.multiple_of(s * 256, 256), 256)]
            for ii in range(2):
                energy = (eps_rows[...] + cols) - eps_slab[i + ii] - eps_pair[0]
                done = value[ii * 256 : (ii + 1) * 256] / energy
                for n in range(2):
                    flat_ref[pl.ds(ii * 2048 + 2 * s + n, 256, stride=8), :] = done[
                        :, n * 128 : (n + 1) * 128
                    ]

    @pl.when(g < 2)
    def _():
        work(own, 4 * g + 2 * r, 2 * r)

    @pl.when(g >= 2)
    def _():
        work(oth, 4 * (g - 2) + 2 * (1 - r), 2 * (1 - r))


def smem():
    return pl.BlockSpec(memory_space=pltpu.SMEM)


def whole():
    return pl.BlockSpec(memory_space=pltpu.VMEM)


def anywhere():
    return pl.BlockSpec(memory_space=pl.ANY)


def params():
    return pltpu.CompilerParams(vmem_limit_bytes=VMEM_LIMIT)


def as_is(array):
    def kernel(from_ref, to_ref):
        pltpu.sync_copy(from_ref, to_ref)

    return pl.pallas_call(
        kernel,
        out_shape=jax.ShapeDtypeStruct(array.shape, array.dtype),
        in_specs=[anywhere()],
        out_specs=anywhere(),
        name="as_is",
    )(array)


def k_place(kk, r):
    return lax.rem(kk + 2 * r, 4)


def packed_shards(amplitudes, integrals, amp_mask, int_mask, eps_slab, eps_pair, eps_vir):
    v, x, r = lax.axis_index("vir"), lax.axis_index("occ"), lax.axis_index("rep")
    meta = jnp.stack([v, x, r, 2 * x + r]).astype(jnp.int32)
    swap = [(0, 1), (1, 0)]
    bf16 = jnp.bfloat16

    pairs = amp_mask.reshape(4, 4, 4, 4, 4).sum((0, 2, 4))
    pairs = jnp.where(jnp.eye(4, dtype=bool), 0, pairs)
    pieces = int_mask.reshape(4, 4, 4, 4, 16).sum((0, 3, 4))
    over = jnp.logical_or(jnp.max(pairs) > AMP_SLOTS - 1, jnp.max(pieces) > INT_SLOTS - 1)
    over = over.astype(jnp.int32).reshape(1)

    int_oth = lax.ppermute(integrals, "rep", swap)
    amps = amplitudes.reshape(2, 2, 2, 2, 256, 1024)
    int_oth, later = lax.optimization_barrier((int_oth, amps))
    amp_oth = lax.ppermute(later, "rep", swap)

    packed_int = pl.pallas_call(
        pack_int_kernel,
        out_shape=jax.ShapeDtypeStruct((INT_SLOTS, 32, LANES), bf16),
        in_specs=[smem(), smem(), whole(), whole()],
        out_specs=whole(),
        compiler_params=params(),
        cost_estimate=NO_COST,
        name="pack_int",
    )(meta, int_mask, integrals, int_oth)

    up1 = lax.ppermute(packed_int, "vir", [(0, 1), (1, 2), (2, 3)])
    down1 = lax.ppermute(packed_int, "vir", [(1, 0), (2, 1), (3, 2)])

    packed_amp = pl.pallas_call(
        pack_amp_kernel,
        grid_spec=pltpu.PrefetchScalarGridSpec(
            num_scalar_prefetch=2,
            grid=(1,),
            in_specs=[
                pl.BlockSpec((1, 1, 2, 2, 256, 1024), lambda g, meta, mask: (meta[1], meta[2], 0, 0, 0, 0)),
                pl.BlockSpec((1, 1, 2, 2, 256, 1024), lambda g, meta, mask: (meta[1], meta[2], 0, 0, 0, 0)),
            ],
            out_specs=[pl.BlockSpec((AMP_SLOTS, TILE, LANES), lambda g, meta, mask: (0, 0, 0))] * 3,
        ),
        out_shape=[jax.ShapeDtypeStruct((AMP_SLOTS, TILE, LANES), bf16)] * 3,
        compiler_params=params(),
        cost_estimate=NO_COST,
        name="pack_amp",
    )(meta, amp_mask, amps, amp_oth)

    def across(d, packed):
        return lax.ppermute(packed, "vir", [(s, s ^ d) for s in range(4)])

    packed3, over = lax.optimization_barrier((packed_amp[2], over))
    over = over + lax.ppermute(over, "frag", swap)

    int_shapes = [
        jax.ShapeDtypeStruct((4, 256, 1024), bf16),
        jax.ShapeDtypeStruct((4, 1024, 256), bf16),
    ]
    int_outs = [
        pl.BlockSpec((1, 256, 1024), lambda kk, meta, mask: (k_place(kk, meta[2]), 0, 0)),
        pl.BlockSpec((1, 1024, 256), lambda kk, meta, mask: (k_place(kk, meta[2]), 0, 0)),
    ]
    def unpack(d, *operands):
        if d == 0:
            kernel, scratch = own_int_kernel, []
            specs = [
                pl.BlockSpec((1, 1, 256, 1024), lambda kk, meta, mask: (jnp.minimum(kk, 1), meta[2], 0, 0)),
                pl.BlockSpec((1, 1, 256, 1024), lambda kk, meta, mask: (jnp.maximum(kk - 2, 0), meta[2], 0, 0)),
            ]
        else:
            kernel = functools.partial(unpack_int_kernel, d)
            scratch = [pltpu.VMEM((INT_SLOTS, 32, LANES), bf16), pltpu.SMEM((1,), jnp.int32)]
            specs = [anywhere() for _ in operands]
        return pl.pallas_call(
            kernel,
            grid_spec=pltpu.PrefetchScalarGridSpec(
                num_scalar_prefetch=2, grid=(4,), in_specs=specs, out_specs=int_outs, scratch_shapes=scratch
            ),
            out_shape=int_shapes,
            compiler_params=params(),
            cost_estimate=NO_COST,
            name=f"ints_{d}",
        )(meta, int_mask, *operands)

    def local_specs(d, base):
        def at(side):
            def place(kk, meta, mask):
                k = jnp.minimum(kk + base, 1) if side == 0 else jnp.maximum(kk + base - 2, 0)
                return (0, meta[2], 0, k, 0, meta[0] ^ d)

            return place

        return [pl.BlockSpec((2, 1, 2, 1, 256, 256), at(side)) for side in range(2)]

    def combine(d, base, near, far, steps, extra_specs, extra, out_specs, out_shape, aliases, scratch):
        kernel = diagonal_kernel if d == 0 else functools.partial(combine_kernel, d, base)
        specs, operands = [], ()
        if d > 0:
            specs = [pl.BlockSpec((AMP_SLOTS, TILE, LANES), lambda kk, meta, mask: (0, 0, 0))] * 2
            operands = (near, far)
        return pl.pallas_call(
            kernel,
            grid_spec=pltpu.PrefetchScalarGridSpec(
                num_scalar_prefetch=2,
                grid=(steps,),
                in_specs=local_specs(d, base) + specs + extra_specs,
                out_specs=out_specs,
                scratch_shapes=scratch,
            ),
            out_shape=out_shape,
            input_output_aliases=aliases,
            compiler_params=params(),
            cost_estimate=NO_COST,
            name=f"combine_{d}_{base}",
        )(meta, amp_mask, amps, amp_oth, *operands, *extra)

    def combine_first(d, near, far, sofar):
        return combine(
            d,
            0,
            near,
            far,
            4,
            [] if d == 0 else [anywhere()],
            () if d == 0 else (sofar,),
            pl.BlockSpec(
                (1, 2, 2, 256, 256), lambda kk, meta, mask: (d, 0, 0, 0, k_place(kk, meta[2]))
            ),
            jax.ShapeDtypeStruct((3, 2, 2, 256, 1024), bf16),
            {} if d == 0 else {6: 0},
            [] if d == 0 else [pltpu.SMEM((1,), jnp.int32)],
        )

    def combine_half(base, near, far, *count):
        return combine(
            3,
            base,
            near,
            far,
            2,
            [smem() for _ in count],
            count,
            [pl.BlockSpec((1, 2, 2, 256, 256), lambda kk, meta, mask: (0, 0, 0, 0, kk)), smem()],
            [jax.ShapeDtypeStruct((1, 2, 2, 256, 512), bf16), jax.ShapeDtypeStruct((1,), jnp.int32)],
            {},
            [],
        )

    ready = lax.optimization_barrier
    ints = [unpack(0, integrals, int_oth)]
    first = combine_first(0, None, None, None)
    near1, near2 = across(1, packed_amp[0]), across(2, packed_amp[1])
    up1, down1, over, ints[0], first = ready((up1, down1, over, ints[0], first))
    up2 = lax.ppermute(up1, "vir", [(1, 2), (2, 3)])
    down2 = lax.ppermute(down1, "vir", [(1, 0), (2, 1)])
    far1, far2 = lax.ppermute(near1, "occ", swap), lax.ppermute(near2, "occ", swap)
    ints.append(unpack(1, down1, up1))
    ints[1], far1 = ready((ints[1], far1))
    first = combine_first(1, near1, far1, first)
    first = combine_first(2, near2, far2, first)
    near3 = across(3, packed3)
    up2, down2, first = ready((up2, down2, first))
    ints.append(unpack(2, down2, up2))
    folded_w = pl.pallas_call(
        fold_kernel,
        grid_spec=pltpu.PrefetchScalarGridSpec(
            num_scalar_prefetch=1,
            grid=(4,),
            in_specs=[pl.BlockSpec((1, 256, 1024), lambda k, meta: (k, 0, 0))] * 3
            + [pl.BlockSpec((1, 1024, 256), lambda k, meta: (k, 0, 0))] * 3,
            out_specs=pl.BlockSpec((3, 256, 768), lambda k, meta: (0, k, 0)),
        ),
        out_shape=jax.ShapeDtypeStruct((3, 1024, 768), bf16),
        compiler_params=params(),
        cost_estimate=NO_COST,
        name="fold",
    )(meta, *[d for d, _ in ints], *[t for _, t in ints])
    up2, down2, near3, first, folded_w = ready((up2, down2, near3, first, folded_w))
    end_down = lax.ppermute(down2, "vir", [(1, 0)])
    end_up = lax.ppermute(up2, "vir", [(2, 3)])
    first_oth = lax.ppermute(first, "rep", swap)

    def own_at(d, width=1024):
        return pl.BlockSpec((1, 1, 2, 256, width), lambda g, *_: (d % 3, jnp.minimum(g, 1), 0, 0, 0))

    def oth_at(d, width=1024):
        return pl.BlockSpec((1, 1, 2, 256, width), lambda g, *_: (d % 3, jnp.maximum(g - 2, 0), 0, 0, 0))

    def place(g, meta, *_):
        return (2 * (g % 2) + jnp.where(g < 2, meta[2], 1 - meta[2]), 0)

    once = pl.Buffered(1)
    def early(c, other, *sofar):
        def at(d):
            return pl.BlockSpec((1, 1, 2, 256, 1024), lambda g, *_: (d, g, 0, 0, 0))

        return pl.pallas_call(
            early_kernel,
            grid_spec=pltpu.PrefetchScalarGridSpec(
                num_scalar_prefetch=1,
                grid=(2,),
                in_specs=[pl.BlockSpec((3, 1024, 768), lambda g, *_: (0, 0, 0), pipeline_mode=once)]
                + [at(d) for d in range(3)]
                + [anywhere() for _ in sofar],
                out_specs=pl.BlockSpec((512, 768), lambda g, meta: place(g + 2 * other, meta)),
            ),
            out_shape=jax.ShapeDtypeStruct((2048, 768), jnp.float32),
            input_output_aliases={5: 0} if sofar else {},
            compiler_params=params(),
            cost_estimate=NO_COST,
            name=f"early_{other}",
        )(meta, folded_w, c, c, c, *sofar)

    part = early(first_oth, 1, early(first, 0))

    far3 = lax.ppermute(near3, "occ", swap)
    far3, part = ready((far3, part))
    half0, count = combine_half(0, near3, far3)
    half1, _ = combine_half(2, near3, far3, count)
    halves = (half0, half1)
    halves_oth = tuple(lax.ppermute(h, "rep", swap) for h in halves)
    end_down, end_up, half1 = ready((end_down, end_up, half1))
    ints.append(unpack(3, end_down, down1, up1, end_up))
    rows, cols = [d for d, _ in ints], [t for _, t in ints]
    last_row, late = pl.pallas_call(
        late_kernel,
        grid_spec=pltpu.PrefetchScalarGridSpec(
            num_scalar_prefetch=1,
            grid=(4,),
            in_specs=[pl.BlockSpec((4, 256, 256), lambda g, meta: (0, 0, meta[0] ^ 3), pipeline_mode=once)] * 3
            + [pl.BlockSpec((4, 256, 1024), lambda g, meta: (0, 0, 0), pipeline_mode=once)]
            + [pl.BlockSpec((4, 256, 256), lambda g, meta: (0, meta[0] ^ 3, 0), pipeline_mode=once)] * 3
            + [pl.BlockSpec((4, 1024, 256), lambda g, meta: (0, 0, 0), pipeline_mode=once)]
            + [own_at(d) for d in range(3)]
            + [oth_at(d) for d in range(3)],
            out_specs=[
                pl.BlockSpec((256, 1024), lambda g, meta: (g, 0)),
                pl.BlockSpec((512, 256), place),
            ],
            scratch_shapes=[pltpu.VMEM((3, 1024, 256), bf16)],
        ),
        out_shape=[
            jax.ShapeDtypeStruct((1024, 1024), bf16),
            jax.ShapeDtypeStruct((2048, 256), jnp.float32),
        ],
        compiler_params=params(),
        cost_estimate=NO_COST,
        name="late",
    )(meta, *rows, *cols, *[first] * 3, *[first_oth] * 3)
    row_energy = lax.dynamic_slice_in_dim(eps_vir, v * 256, 256, 0).reshape(256, 1)
    col_energy = eps_vir.reshape(1, 1024)

    def finish(ops):
        part, late, last_row, own, oth = ops
        return pl.pallas_call(
            tail_kernel,
            grid_spec=pltpu.PrefetchScalarGridSpec(
                num_scalar_prefetch=3,
                grid=(4,),
                in_specs=[
                    pl.BlockSpec((256, 1), lambda g, *_: (0, 0)),
                    pl.BlockSpec((1, 1024), lambda g, *_: (0, 0)),
                    pl.BlockSpec((512, 768), place),
                    pl.BlockSpec((512, 256), place),
                    pl.BlockSpec((1024, 1024), lambda g, *_: (0, 0), pipeline_mode=once),
                ]
                + [own_at(3, 512)] * 2
                + [oth_at(3, 512)] * 2,
                out_specs=pl.BlockSpec((2, 256, 1, 1024), lambda g, meta, *_: (*place(g, meta), 0, 0)),
            ),
            out_shape=jax.ShapeDtypeStruct((8, 256, 1, 1024), jnp.float32),
            compiler_params=params(),
            cost_estimate=NO_COST,
            name="tail",
        )(meta, eps_slab, eps_pair, row_energy, col_energy, part, late, last_row, *own, *oth)

    def dense(state):
        out = dense_shards(
            as_is(amplitudes), as_is(integrals), amp_mask, int_mask, eps_slab, eps_pair, eps_vir
        )
        return as_is(out), jnp.zeros((), jnp.int32)

    out = finish((part, late, last_row, halves, halves_oth))
    return lax.while_loop(lambda state: state[1] > 0, dense, (out, over[0]))[0]


def shards(sizes, *args):
    amplitudes, integrals, amp_mask, int_mask = args[:4]
    fits = (
        sizes == {"frag": 2, "vir": 4, "occ": 2, "rep": 2}
        and amplitudes.shape == (8, 2, 256, 1024)
        and integrals.shape == (2, 2, 256, 1024)
        and amp_mask.shape == (4, 16, 16)
        and int_mask.shape == (4, 4, 16, 16)
    )
    return packed_shards(*args) if fits else dense_shards(*args)


def solution(mesh):
    in_specs = (
        P("frag", "rep", "vir", None),
        P(("frag", "rep"), "occ", "vir", None),
        P("frag", None, None),
        P("frag", None, None, None),
        P("frag"),
        P(("frag", "occ", "rep")),
        P("frag"),
    )
    out_specs = P("frag", "vir", ("occ", "rep"), None)
    return jax.shard_map(
        functools.partial(shards, dict(mesh.shape)),
        mesh=mesh,
        in_specs=in_specs,
        out_specs=out_specs,
        check_vma=False,
    )
```
